32 devices in a mesh: dp: 16 (over z, x, core), tensor: 2 (over y).
Axes of the slice: x: 2, y: 2, z: 4, core: 2. Of those that a mesh axis runs over, the one named last changes fastest.
Arguments:
- patches: bfloat16 [16384, 768], P('dp'), may hold values from -6 to 6
- image_ids: int32 [16, 1024], P('dp'), may hold values from 0 to 7, never falling along the last dimension, each value on 1 to 256 neighbouring positions
- valid: int32 [16, 1024], P('dp'), may hold values 0 or 1
- mask_pos: int32 [16, 1024], P('dp'), may hold values 0 or 1
- mask_token: bfloat16 [768], replicated, may hold values from -5 to 5
- ln1_gain: bfloat16 [768], replicated, may hold values from 0.5 to 1.5
- ln1_bias: bfloat16 [768], replicated, may hold values from -1.5 to 1.5
- w_qkv: bfloat16 [768, 3, 768], P(None, None, 'tensor'), may hold values from -0.21875 to 0.21875
- b_qv: bfloat16 [2, 768], P(None, 'tensor'), may hold values from -2.5 to 2.5
- w_proj: bfloat16 [768, 768], P('tensor'), may hold values from -0.875 to 0.875
- b_proj: bfloat16 [768], replicated, may hold values from -1.5 to 1.5
- ln2_gain: bfloat16 [768], replicated, may hold values from 0.5 to 1.5
- ln2_bias: bfloat16 [768], replicated, may hold values from -1.5 to 1.5
- w_up: bfloat16 [768, 3072], P('dp', 'tensor'), may hold values from -0.21875 to 0.21875
- b_up: bfloat16 [3072], P('tensor'), may hold values from -2.5 to 2.5
- w_down: bfloat16 [3072, 768], P('tensor', 'dp'), may hold values from -0.109375 to 0.109375
- b_down: bfloat16 [768], replicated, may hold values from -1.5 to 1.5
- cotangent: bfloat16 [16384, 768], P('dp'), may hold values from -6 to 6
Outputs:
- mixed: bfloat16 [16384, 768], P('dp')
- grad_input: float32 [16384, 768], P('dp')
- grad_mask_token: float32 [768], replicated
- grad_ln1_gain: float32 [768], replicated
- grad_ln1_bias: float32 [768], replicated
- grad_w_qkv: float32 [768, 3, 768], P(None, None, 'tensor')
- grad_b_qv: float32 [2, 768], P(None, 'tensor')
- grad_w_proj: float32 [768, 768], P('tensor')
- grad_b_proj: float32 [768], replicated
- grad_ln2_gain: float32 [768], replicated
- grad_ln2_bias: float32 [768], replicated
- grad_w_up: float32 [768, 3072], P('dp', 'tensor')
- grad_b_up: float32 [3072], P('tensor')
- grad_w_down: float32 [3072, 768], P('tensor', 'dp')
- grad_b_down: float32 [768], replicated
The draws below stay inside these ranges and needn't reach their ends.
Inputs may be any that keep to these rules, and one draw needn't show every extreme that they name: `image_ids`: within each pack the ids never fall along the patches; an image has 1 to 256 patches and one of each pack has exactly 256.
All inputs are finite; a program needn't handle non-finite values. No bound on the sum of `valid` or of `mask_pos` on one device may be relied on, other than what follows from the above.
Results may differ from the reference program's by a relative error of at most 0.013.
Values may be sent and summed in bfloat16 or wider, within the bound.
A program may use at most 192 MiB of HBM per device.

```python
import math
import jax
import jax.numpy as jnp
import numpy as np
from jax import lax

D = 768
HEAD_DIM = 64
FF = 3072
TOK_DEV = 1024
IMAGES = 8
MOST_PATCH = 256
PACKS = 16
TOKENS = 16384


def set_ends(result, key, least, top_value):
    longest = result.shape.index(max(result.shape))
    spots = []
    for shift in (0, 1):
        where = [jax.random.randint(jax.random.fold_in(key, axis), (), 0, length) for axis, length in enumerate(result.shape)]
        where[longest] = (where[longest] + shift) % result.shape[longest]
        spots.append(tuple(where))
    return result.at[spots[0]].set(least).at[spots[1]].set(top_value)


def with_spikes(entries, own_key, source, target, shards_of, factor):
    def block_of(axis_at):
        return (jnp.arange(entries.shape[axis_at]) // (entries.shape[axis_at] // shards_of)).reshape((-1,) + (1,) * (entries.ndim - 1 - axis_at))

    one_side = jax.random.permutation(own_key, shards_of)[block_of(target)]
    second = (block_of(target) + shards_of // 2) % shards_of
    return jnp.where((block_of(source) == one_side) | (block_of(source) == second), factor * entries, entries)


def shard_levels(stream_key, extent, cuts, least, largest):
    factor_of, own = 1.0, jax.random.fold_in(stream_key, 6)
    for dim, blocks in cuts:
        heights = jnp.exp(jax.random.uniform(jax.random.fold_in(own, dim), (blocks,), jnp.float32, least / len(cuts), largest / len(cuts)))
        factor_of = factor_of * jnp.repeat(heights, extent[dim] // blocks).reshape([-1 if axis == dim else 1 for axis in range(len(extent))])
    return factor_of


def profile(number_of, total, limit, skew):
    loads = [(1 << 20) // math.isqrt(standing ** skew) + 1 for standing in range(2, number_of + 1)]
    surplus, given = total - limit - (number_of - 1), [1] * (number_of - 1)
    while surplus > 0:
        free = [i for i in range(number_of - 1) if given[i] < limit]
        whole, remaining = sum([loads[i] for i in free]), surplus
        for i in free:
            extra = min(limit - given[i], max(1, remaining * loads[i] // whole), surplus)
            given[i] = given[i] + extra
            surplus = surplus - extra
    return np.array([limit] + given)


def ragged_sizes(rng, count, total, bound, lean):
    if count == 2:
        one = jax.random.randint(rng, (), max(1, total - bound), min(bound, total - 1) + 1)
        return jnp.stack([one, total - one])
    sizes = jnp.asarray(profile(count, total, bound, lean), jnp.int32)
    pairs = (count - 1) // 2
    giver, sink = sizes[1:1 + 2 * pairs:2], sizes[2:2 + 2 * pairs:2]
    slack = jnp.minimum(giver - 1, bound - sink)
    moved = jax.random.randint(jax.random.fold_in(rng, 1), (pairs,), 0, 1 << 20) % (slack + 1)
    sizes = sizes.at[1:1 + 2 * pairs:2].set(giver - moved).at[2:2 + 2 * pairs:2].set(sink + moved)
    return sizes[jax.random.permutation(jax.random.fold_in(rng, 2), count)]


def centred(rng, shape, scale, bound, split=(), held_as=jnp.bfloat16):
    loudness = shard_levels(rng, shape, split, -0.22, 0.18) if split else 1.0
    values = jax.random.normal(rng, shape, jnp.float32) * scale * loudness
    return jnp.minimum(jnp.maximum(values, -bound), bound).astype(held_as)


def noise_with(key, extent, scale, bound, split, heavy, kind=jnp.bfloat16):
    result = scale * jax.random.normal(key, extent, jnp.float32)
    if split:
        result = result * shard_levels(key, extent, split, -0.22, 0.18)
    return jnp.clip(with_spikes(result, jax.random.fold_in(key, 3), *heavy), -bound, bound).astype(kind)


def setup_inputs(seed: int = 0) -> dict:
    arg_keys = jax.random.split(jax.random.key(seed), 19)
    patches = noise_with(arg_keys[0], (TOKENS, D), 1.0, 6.0, ((0, 16),), (0, 1, 16, 2.0))
    image_ids = jax.vmap(lambda own: jnp.searchsorted(jnp.cumsum(ragged_sizes(own, IMAGES, TOK_DEV, MOST_PATCH, 1)), jnp.arange(TOK_DEV), side="right"))(jax.random.split(arg_keys[1], PACKS)).reshape((PACKS, TOK_DEV)).astype(jnp.int32)
    valid = set_ends((jax.random.randint(arg_keys[2], (PACKS, TOK_DEV), 0, 10) < 9).astype(jnp.int32), jax.random.fold_in(arg_keys[2], 1), 0, 1)
    mask_pos = set_ends((jax.random.randint(arg_keys[3], (PACKS, TOK_DEV), 0, 5) < 2).astype(jnp.int32), jax.random.fold_in(arg_keys[3], 1), 0, 1)
    mask_token = centred(arg_keys[4], (D,), 1.0, 5.0)
    ln1_gain = jnp.clip(1.0 + 0.1 * jax.random.normal(arg_keys[5], (D,), jnp.float32), 0.5, 1.5).astype(jnp.bfloat16)
    ln1_bias = centred(arg_keys[6], (D,), 0.3, 1.5)
    w_qkv = centred(arg_keys[7], (D, 3, D), D ** -0.5, 0.21875, ((2, 2),))
    b_qv = centred(arg_keys[8], (2, D), 0.5, 2.5, ((1, 2),))
    w_proj = centred(arg_keys[9], (D, D), (D // 16) ** -0.5, 0.875, ((0, 2),))
    b_proj = centred(arg_keys[10], (D,), 0.3, 1.5)
    ln2_gain = jnp.clip(1.0 + 0.1 * jax.random.normal(arg_keys[11], (D,), jnp.float32), 0.5, 1.5).astype(jnp.bfloat16)
    ln2_bias = centred(arg_keys[12], (D,), 0.3, 1.5)
    w_up = centred(arg_keys[13], (D, FF), D ** -0.5, 0.21875, ((0, 16), (1, 2)))
    b_up = centred(arg_keys[14], (FF,), 0.5, 2.5, ((0, 2),))
    w_down = centred(arg_keys[15], (FF, D), FF ** -0.5, 0.109375, ((0, 2), (1, 16)))
    b_down = centred(arg_keys[16], (D,), 0.3, 1.5)
    cotangent = noise_with(arg_keys[17], (TOKENS, D), 1.0, 6.0, ((0, 16),), (0, 1, 16, 2.0))
    return {"patches": patches, "image_ids": image_ids, "valid": valid, "mask_pos": mask_pos, "mask_token": mask_token, "ln1_gain": ln1_gain, "ln1_bias": ln1_bias, "w_qkv": w_qkv, "b_qv": b_qv, "w_proj": w_proj, "b_proj": b_proj, "ln2_gain": ln2_gain, "ln2_bias": ln2_bias, "w_up": w_up, "b_up": b_up, "w_down": w_down, "b_down": b_down, "cotangent": cotangent}


@jax.custom_vjp
def low(v):
    return lax.optimization_barrier(v.astype(jnp.bfloat16)).astype(jnp.float32)

@jax.custom_vjp
def low_back(v):
    return v

def low_keep(v):
    return (low(v), None)

def low_pass(kept, grad):
    return (grad,)

def back_keep(v):
    return (v, None)

def back_low(kept, grad):
    return (low(grad),)
low.defvjp(low_keep, low_pass)
low_back.defvjp(back_keep, back_low)
EPS = 1e-06
HIGH = lax.Precision.HIGHEST

def norm_rows(values, gain, shift):
    mean = lax.optimization_barrier(jnp.mean(values, axis=-1, keepdims=True))
    cent = values - mean
    var = lax.optimization_barrier(jnp.mean(cent * cent, axis=-1, keepdims=True))
    return cent * lax.rsqrt(var + EPS) * gain + shift

def pack_forward(params, x_pack, ids, live, masked):
    mask_token, ln1_gain, ln1_bias, w_qkv, b_qv, w_proj, b_proj, ln2_gain, ln2_bias, w_up, b_up, w_down, b_down = params
    rows = x_pack.shape[0]
    width = x_pack.shape[1]
    heads = width // HEAD_DIM
    start = jnp.where(masked[:, None] == 1, mask_token[None, :], x_pack)
    normed = low(norm_rows(start, ln1_gain, ln1_bias))
    qkv = jnp.einsum('td,dsc->tsc', normed, w_qkv, precision=HIGH)
    bias = jnp.stack([b_qv[0], jnp.zeros_like(b_qv[0]), b_qv[1]])
    qkv = low(low_back(qkv + bias[None]))
    query = qkv[:, 0].reshape(rows, heads, HEAD_DIM)
    keys = qkv[:, 1].reshape(rows, heads, HEAD_DIM)
    values = qkv[:, 2].reshape(rows, heads, HEAD_DIM)
    scale = 1.0 / HEAD_DIM ** 0.5
    scores = low_back(jnp.einsum('qhc,khc->hqk', query, keys, precision=HIGH) * scale)
    places = jnp.arange(rows)
    allowed = (ids[:, None] == ids[None, :]) & ((live[None, :] == 1) | (places[:, None] == places[None, :]))
    scores = jnp.where(allowed[None], scores, -1e+30)
    top = lax.optimization_barrier(jnp.max(scores, axis=-1, keepdims=True))
    expd = jnp.exp(scores - top)
    probs = low(expd / lax.optimization_barrier(jnp.sum(expd, axis=-1, keepdims=True)))
    attended = jnp.einsum('hqk,khc->qhc', probs, values, precision=HIGH).reshape(rows, width)
    attended = low(low_back(attended))
    branch = low_back(jnp.dot(attended, w_proj, precision=HIGH) + b_proj)
    middle = start + branch
    normed2 = low(norm_rows(middle, ln2_gain, ln2_bias))
    hidden = low_back(jnp.dot(normed2, w_up, precision=HIGH) + b_up)
    active = low(jax.nn.gelu(hidden, approximate=False))
    return middle + low_back(jnp.dot(active, w_down, precision=HIGH) + b_down)

def reference(patches, image_ids, valid, mask_pos, mask_token, ln1_gain, ln1_bias, w_qkv, b_qv, w_proj, b_proj, ln2_gain, ln2_bias, w_up, b_up, w_down, b_down, cotangent):
    params = tuple((p.astype(jnp.float32) for p in (mask_token, ln1_gain, ln1_bias, w_qkv, b_qv, w_proj, b_proj, ln2_gain, ln2_bias, w_up, b_up, w_down, b_down)))
    inputs = patches.astype(jnp.float32).reshape(PACKS, TOK_DEV, D)
    seed_cot = cotangent.astype(jnp.float32).reshape(PACKS, TOK_DEV, D)

    def whole(params, inputs):

        def step(carry, item):
            x_pack, ids, live, masked = item
            return (carry, jax.checkpoint(pack_forward)(params, x_pack, ids, live, masked))
        _, outs = lax.scan(step, jnp.zeros((), jnp.float32), (inputs, image_ids, valid, mask_pos))
        return outs
    out, pull = jax.vjp(whole, params, inputs)
    grads, grad_x = pull(seed_cot)
    mixed = out.reshape(TOKENS, D).astype(jnp.bfloat16)
    return (mixed, grad_x.reshape(TOKENS, D), grads[0], grads[1], grads[2], grads[3], grads[4], grads[5], grads[6], grads[7], grads[8], grads[9], grads[10], grads[11], grads[12])
```

```python
from functools import partial

import jax
import jax.numpy as jnp
from jax import lax
from jax.experimental import pallas as pl
from jax.experimental.pallas import tpu as pltpu
from jax.sharding import PartitionSpec as P

BF = jnp.bfloat16
F32 = jnp.float32
MESH = pl.DeviceIdType.MESH
EPS = 1e-06
T = 1024
H = 512
D = 768
HL = 384
BLK = 256
WIN = 768
XCH = 128


def nn(a, b):
    return lax.dot_general(a, b, (((1,), (0,)), ((), ())), preferred_element_type=F32)


def nt(a, b):
    return lax.dot_general(a, b, (((1,), (1,)), ((), ())), preferred_element_type=F32)


def tn(a, b):
    return lax.dot_general(a, b, (((0,), (0,)), ((), ())), preferred_element_type=F32)


def rowsum(v):
    return jnp.sum(v, axis=0, keepdims=True)


def lane_half(shape):
    return lax.broadcasted_iota(jnp.int32, shape, 1) < 64


def stats(v):
    mean = jnp.sum(v, axis=-1, keepdims=True) * (1.0 / D)
    cent = v - mean
    var = jnp.sum(cent * cent, axis=-1, keepdims=True) * (1.0 / D)
    return cent, lax.rsqrt(var + EPS)


def norm_back(xhat, r, d, gain):
    e = d * gain
    m1 = jnp.sum(e, axis=-1, keepdims=True) * (1.0 / D)
    m2 = jnp.sum(e * xhat, axis=-1, keepdims=True) * (1.0 / D)
    return r * (e - m1 - xhat * m2)


def mega(
    patches, codec, coder, vec, wqkv, bqv, wproj, up, dn, bup, cot,
    mixed, gin, fA, gup, gdn, vout,
    n1, nT, qkv, attO, attF, wpf, Wu, Wd, mid, n2, dml, dmlT, outA, dn2A, rO, rN, act, dh, gU, gD,
    rx, rz, sy, ry, sc, rc, dO, rN1, rGP, rAc, rAx, rAz, lseT, bupA, vecA, vR, ssem, rsem, lsem,
):
    d = lax.axis_index("dp")
    t = lax.axis_index("tensor")
    z = lax.div(d, 4)
    x = lax.rem(lax.div(d, 2), 2)
    c = lax.rem(d, 2)
    zk = (z, z + 1 - 2 * lax.rem(z, 2), lax.rem(z + 2, 4), 3 - z)
    xr = (x, 1 - x)
    tr = (t, 1 - t)

    def dev(zz, xx, cc, tt):
        return ((zz * 2 + xx) * 2 + cc, tt)

    core = dev(z, x, 1 - c, t)
    xp = dev(z, 1 - x, c, t)
    yp = dev(z, x, c, 1 - t)
    zp = (None,) + tuple(dev(zk[k], x, c, t) for k in (1, 2, 3))

    counter = [0]
    pending = []

    def xchg(src, dst, to):
        i = counter[0]
        counter[0] += 1
        cp = pltpu.make_async_remote_copy(
            src_ref=src, dst_ref=dst, send_sem=ssem.at[i], recv_sem=rsem.at[i], device_id=to, device_id_type=MESH
        )
        cp.start()
        pending.append(cp)
        return cp

    def al(v, m):
        return pl.multiple_of(v, m)

    bar = pltpu.get_barrier_semaphore()
    peers = (core, xp, yp, zp[1], zp[2], zp[3])
    for p in peers:
        pl.semaphore_signal(bar, inc=1, device_id=p, device_id_type=MESH)
    pl.semaphore_wait(bar, len(peers))

    own = al(t * H, H)
    oth = al((1 - t) * H, H)
    cslot = al(c * H, H)
    sslot = al((1 - c) * H, H)
    W = (Wu, Wd)
    shards = (up, dn)

    def wblk(a, k, xx, yy):
        return W[a].at[tr[yy], pl.ds(al((zk[k] * 2 + xr[xx]) * 96, 32), 96), :]

    ccp = []
    mine = al((z * 2 + x) * 96 + c * 48, 16)
    for a in (0, 1):
        ccp.append(
            xchg(shards[a].at[:, pl.ds(al((1 - c) * D, 128), D)], W[a].at[t, pl.ds(mine, 48), :], core)
        )
    cdml = xchg(cot.at[pl.ds(own, H), :], dml.at[pl.ds(cslot, H), :], core)
    cwp = xchg(wproj, wpf.at[t], yp)
    cbup = xchg(bup, bupA.at[1], yp)
    ldml = pltpu.make_async_copy(cot.at[pl.ds(own, H), :], dml.at[pl.ds(cslot, H), :], lsem.at[0])
    ldml.start()
    lwp = pltpu.make_async_copy(wproj, wpf.at[t], lsem.at[1])
    lwp.start()
    for a in (0, 1):
        W[a][t, pl.ds(mine, 48), :] = shards[a][:, pl.ds(al(c * D, 128), D)]
    bupA[0] = bup[...]

    zc = ([None] * 4, [None] * 4)
    xc = ({}, {})
    yc = ({}, {})

    def xsend(a, k, yy):
        xc[a][(k, yy)] = xchg(wblk(a, k, 0, yy), wblk(a, k, 0, yy), xp)

    def ysend(a, k, xx):
        yc[a][(k, xx)] = xchg(wblk(a, k, xx, 0), wblk(a, k, xx, 0), yp)

    def pump0():
        for a in (0, 1):
            ccp[a].wait_recv()
        for a in (0, 1):
            for k in (1, 2, 3):
                zc[a][k] = xchg(wblk(a, 0, 0, 0), wblk(a, 0, 0, 0), zp[k])
        for a in (0, 1):
            xsend(a, 0, 0)
            ysend(a, 0, 0)

    def pumpk(k):
        for a in (0, 1):
            zc[a][k].wait_recv()
            xsend(a, k, 0)
            ysend(a, k, 0)

    def pumpq(k):
        xc[0][(k, 0)].wait_recv()
        ysend(0, k, 1)
        yc[1][(k, 0)].wait_recv()
        xsend(1, k, 1)

    token = vec[0:1, :]
    ln1g = vec[1:2, :]
    ln1b = vec[2:3, :]

    def start_rows(r0):
        m = lax.shift_right_logical(codec[pl.ds(r0, BLK), :], 5) == 1
        return m, jnp.where(m, token, patches[pl.ds(r0, BLK), :].astype(F32))

    def ln1_block(b, carry):
        r0 = al(b * BLK, BLK)
        _, v = start_rows(r0)
        cent, r = stats(v)
        nb = (cent * r * ln1g + ln1b).astype(BF)
        n1[pl.ds(r0, BLK), :] = nb
        for s in range(3):
            y = nn(nb, wqkv[s])
            if s == 0:
                y = y + bqv[0:1, :]
            if s == 2:
                y = y + bqv[1:2, :]
            qkv[s, pl.ds(r0, BLK), :] = y.astype(BF)
        return carry

    lax.fori_loop(0, 2, ln1_block, 0)
    pump0()
    lax.fori_loop(2, 4, ln1_block, 0)

    def masked_pair(block, scale=None):
        low = lane_half(block.shape)
        zero = jnp.zeros_like(block)
        if scale is not None:
            block = block * jnp.asarray(scale, BF)
        return jnp.where(low, block, zero), jnp.where(low, zero, block)

    def att_block(qb):
        r0 = al(qb * BLK, BLK)
        ws = al(lax.div(qb, 2) * BLK, BLK)
        cr = codec[pl.ds(r0, BLK), :]
        cw = coder[:, pl.ds(ws, WIN)]
        rid = r0 + lax.broadcasted_iota(jnp.int32, (BLK, WIN), 0)
        cid = ws + lax.broadcasted_iota(jnp.int32, (BLK, WIN), 1)
        ok = ((cr & 15) == (cw & 15)) & (((cw & 16) == 16) | (rid == cid))
        dn2A[0:BLK, :] = jnp.where(ok, 0.0, -1e30)
        lane = lax.broadcasted_iota(jnp.int32, (BLK, 128), 1)
        lacc = jnp.zeros((BLK, 128), F32)
        for p in range(3):
            cols = slice(p * 128, p * 128 + 128)
            qs = masked_pair(qkv[0, pl.ds(r0, BLK), cols], 0.125)
            kp = qkv[1, pl.ds(ws, WIN), cols]
            vp = qkv[2, pl.ds(ws, WIN), cols]
            outs = []
            for h in range(2):
                s = nt(qs[h], kp) + dn2A[0:BLK, :]
                top = jnp.max(s, axis=-1, keepdims=True)
                e = jnp.exp(s - top)
                l = jnp.sum(e, axis=-1, keepdims=True)
                o = nn(e.astype(BF), vp) * (1.0 / l)
                outs.append(o)
                lacc = jnp.where(lane == (2 * p + h), top + jnp.log(l), lacc)
            attO[pl.ds(r0, BLK), cols] = jnp.where(lane_half((BLK, 128)), outs[0], outs[1]).astype(BF)
        lseT[:, pl.ds(r0, BLK)] = lacc.T[0:8, :]

    def att_other(i, carry):
        att_block((1 - t) * 2 + i)
        return carry

    def att_own(i, carry):
        att_block(t * 2 + i)
        return carry

    lax.fori_loop(0, 2, att_other, 0)
    catt = xchg(attO.at[pl.ds(oth, H), :], attF.at[t], yp)
    pumpk(1)
    lax.fori_loop(0, 2, att_own, 0)
    attF[t] = attO[pl.ds(own, H), :]
    pumpk(2)
    pumpk(3)

    bproj = vec[3:4, :]
    ln2g = vec[4:5, :]
    ln2b = vec[5:6, :]
    bdown = vec[6:7, :]
    ldml.wait()
    lwp.wait()
    catt.wait_recv()
    cwp.wait_recv()

    def mid_block(b, carry):
        o0 = al(b * BLK, BLK)
        _, v = start_rows(al(own + o0, BLK))
        m = v + (nn(attF[0, pl.ds(o0, BLK), :], wpf[0]) + nn(attF[1, pl.ds(o0, BLK), :], wpf[1])) + bproj
        mid[pl.ds(o0, BLK), :] = m
        cent, r = stats(m)
        n2[pl.ds(al(cslot + o0, BLK), BLK), :] = (cent * r * ln2g + ln2b).astype(BF)
        return carry

    lax.fori_loop(0, 2, mid_block, 0)
    cn2 = xchg(n2.at[pl.ds(cslot, H), :], n2.at[pl.ds(cslot, H), :], core)
    for k in range(4):
        pumpq(k)
    cdml.wait_recv()
    cn2.wait_recv()
    nT[...] = n2[...].T
    dmlT[...] = dml[...].T

    cbup.wait_recv()
    for k in range(4):
        if k:
            pass
        xc[1][(k, 0)].wait_recv()
    G = (gU, gD)
    cRx = [[None, None], [None, None]]
    cRz = [[None, None], [None, None]]
    cRy = [None, None]
    cRc = [None, None]

    def rs_x(j):
        for a in (0, 1):
            cRx[a][j] = xchg(G[a].at[j, 1], rx.at[a, j], xp)

    def rs_z(j):
        for a in (0, 1):
            cRx[a][j].wait_recv()
            for zz in range(4):
                G[a][j, 0, zz] = (G[a][j, 0, zz].astype(F32) + rx[a, j, zz].astype(F32)).astype(BF)
            cRz[a][j] = [xchg(G[a].at[j, 0, zk[k]], rz.at[a, j, k], zp[k]) for k in (1, 2, 3)]

    def rs_zsum(a, j):
        for cp in cRz[a][j]:
            cp.wait_recv()
        total = G[a][j, 0, z].astype(F32)
        for k in (1, 2, 3):
            total = total + rz[a, j, k].astype(F32)
        return total

    def rs_y():
        for a in (0, 1):
            sy[a] = rs_zsum(a, 1).astype(BF)
            cRy[a] = xchg(sy.at[a], ry.at[a], yp)

    def rs_c():
        for a in (0, 1):
            total = rs_zsum(a, 0)
            cRy[a].wait_recv()
            sc[a] = total + ry[a].astype(F32)
            cRc[a] = xchg(sc.at[a, pl.ds(al((1 - c) * 48, 16), 48), :], rc.at[a], core)

    def rs_end():
        for a, out in ((0, gup), (1, gdn)):
            out[:, pl.ds(al(c * D, 128), D)] = sc[a, pl.ds(al(c * 48, 16), 48), :]
            cRc[a].wait_recv()
            out[:, pl.ds(al((1 - c) * D, 128), D)] = rc[a]

    for j in range(2):
        if j == 1:
            for k in range(4):
                yc[0][(k, 0)].wait_recv()
                yc[0][(k, 1)].wait_recv()
                xc[1][(k, 1)].wait_recv()
        yy = tr[j]
        bu = bupA[j, pl.ds(c, 1), :]

        def ff_block(b, carry, j=j, yy=yy, bu=bu):
            rows = pl.ds(al(b * BLK, BLK), BLK)
            hid = nn(n2[rows, :], Wu[yy]) + bu
            phi = 0.5 * (1.0 + lax.erf(hid * 0.7071067811865476))
            a = (hid * phi).astype(BF)
            act[rows, :] = a
            dact = nn(dml[rows, :], Wd[yy])
            dhid = (dact * (phi + hid * (jnp.exp(hid * hid * -0.5) * 0.3989422804014327))).astype(BF)
            dh[rows, :] = dhid
            o = nt(a, Wd[yy])
            g = nt(dhid, Wu[yy])
            if j == 0:
                outA[rows, :] = o
                dn2A[rows, :] = g
            else:
                outA[rows, :] += o
                dn2A[rows, :] += g
            return carry + rowsum(dhid.astype(F32))

        bsum = lax.fori_loop(0, 4, ff_block, jnp.zeros((1, D), F32))
        if j == 0:
            bsum0 = bsum
        else:
            bsum1 = bsum

        def gw_block(b, carry, j=j):
            rows = pl.ds(al(b * 192, 64), 192)
            ru = nn(nT[rows, :], dh[...]).astype(BF)
            rd = nn(dmlT[rows, :], act[...]).astype(BF)
            for xa in range(2):
                rel = lax.rem(xa + x, 2)
                gU[j, rel, b] = ru[xa * 96 : xa * 96 + 96]
                gD[j, rel, b] = rd[xa * 96 : xa * 96 + 96]
            return carry

        lax.fori_loop(0, 4, gw_block, 0)
        rs_x(j)
        if j == 1:
            rs_z(0)

    cn2.wait_send()
    act[0:H, :] = dn2A[pl.ds(sslot, H), :].astype(BF)
    cN = xchg(act.at[0:H, :], rN, core)
    dh[0:H, :] = outA[pl.ds(sslot, H), :].astype(BF)
    cO = xchg(dh.at[0:H, :], rO, core)
    catt.wait_send()
    cN.wait_recv()

    def ln2_back(b, carry):
        s2g, s2b, sp, sd = carry
        o0 = al(b * BLK, BLK)
        rows = pl.ds(o0, BLK)
        crow = pl.ds(al(cslot + o0, BLK), BLK)
        dn = dn2A[crow, :] + rN[rows, :].astype(F32)
        cent, r = stats(mid[rows, :])
        xhat = cent * r
        ct = dml[crow, :].astype(F32)
        dm = ct + norm_back(xhat, r, dn, ln2g)
        db = dm.astype(BF)
        n2[rows, :] = db
        attO[rows, :] = nt(db, wpf[1 - t]).astype(BF)
        dO[pl.ds(al(own + o0, BLK), BLK), :] = nt(db, wpf[t]).astype(BF)
        dn2A[crow, :] = dm
        return (
            s2g + rowsum(dn * xhat),
            s2b + rowsum(dn),
            sp + rowsum(db.astype(F32)),
            sd + rowsum(ct),
        )

    zrow = jnp.zeros((1, D), F32)
    s2g, s2b, sp, sd = lax.fori_loop(0, 2, ln2_back, (zrow, zrow, zrow, zrow))
    cda = xchg(attO.at[0:H, :], dO.at[pl.ds(own, H), :], yp)

    cO.wait_recv()

    def mixed_block(b, carry):
        o0 = al(b * BLK, BLK)
        rows = pl.ds(o0, BLK)
        crow = pl.ds(al(cslot + o0, BLK), BLK)
        out = mid[rows, :] + (outA[crow, :] + rO[rows, :].astype(F32)) + bdown
        mixed[pl.ds(al(own + o0, BLK), BLK), :] = out.astype(BF)
        mid[rows, :] = dn2A[crow, :]
        return carry

    lax.fori_loop(0, 2, mixed_block, 0)
    rs_z(1)

    for a in (0, 1):
        ccp[a].wait_send()
        for cp in zc[a][1:]:
            cp.wait_send()
        for q in (xc[a], yc[a]):
            for key in q:
                q[key].wait_send()

    def gA(s, r0, n):
        return Wu.at[s // 2, pl.ds(r0, n), (s % 2) * HL : (s % 2) * HL + HL]

    Wd[0, 0:HL, :] = tn(attF[1 - t], n2[0:H, :]).astype(BF)
    cGP = xchg(Wd.at[0, 0:HL, :], rGP, yp)
    nT[...] = n1[...].T
    gp = tn(attF[t], n2[0:H, :])
    outA[...] = jnp.zeros((T, D), F32)
    cN.wait_send()
    cO.wait_send()

    def att_back(qb):
        r0 = al(qb * BLK, BLK)
        ws = al(lax.div(qb, 2) * BLK, BLK)
        cw = codec[pl.ds(ws, WIN), :]
        cr = coder[:, pl.ds(r0, BLK)]
        rid = r0 + lax.broadcasted_iota(jnp.int32, (WIN, BLK), 1)
        cid = ws + lax.broadcasted_iota(jnp.int32, (WIN, BLK), 0)
        ok = ((cr & 15) == (cw & 15)) & (((cw & 16) == 16) | (rid == cid))
        dn2A[0:WIN, 0:BLK] = jnp.where(ok, 0.0, -1e30)
        rows = pl.ds(r0, BLK)
        win = pl.ds(ws, WIN)
        for p in range(3):
            cols = slice(p * 128, p * 128 + 128)
            vcols = slice(HL + p * 128, HL + p * 128 + 128)
            qp = qkv[0, rows, cols]
            op = dO[rows, cols]
            qs = masked_pair(qp, 0.125)
            os = masked_pair(op)
            kp = qkv[1, win, cols]
            vp = qkv[2, win, cols]
            dqs, dks, dvs = [], [], []
            for h in range(2):
                lse = lseT[2 * p + h : 2 * p + h + 1, rows]
                pr = jnp.exp(nt(kp, qs[h]) + dn2A[0:WIN, 0:BLK] - lse)
                dp = nt(vp, os[h])
                inner = rowsum(pr * dp)
                ds = (pr * (dp - inner)).astype(BF)
                dvs.append(nn(pr.astype(BF), op))
                dks.append(nn(ds, qp))
                dqs.append(tn(ds, kp))
            low = lane_half((BLK, 128))
            lowk = lane_half((WIN, 128))
            act[rows, cols] = (jnp.where(low, dqs[0], dqs[1]) * 0.125).astype(BF)
            outA[win, cols] += jnp.where(lowk, dks[0], dks[1])
            outA[win, vcols] += jnp.where(lowk, dvs[0], dvs[1])

    def back_step(i, carry):
        att_back(i + (1 - t) * (3 - 2 * i))
        return carry

    def finish_rows(r0):
        rows = pl.ds(r0, BLK)
        act[rows, HL:D] = (outA[rows, 0:HL] * 0.125).astype(BF)
        dh[rows, 0:HL] = outA[rows, HL:D].astype(BF)

    def dn1_rows(r0):
        rows = pl.ds(r0, BLK)
        return nt(act[rows, 0:HL], wqkv[0]) + nt(act[rows, HL:D], wqkv[1]) + nt(dh[rows, 0:HL], wqkv[2])

    cda.wait_recv()
    lax.fori_loop(0, 3, back_step, 0)

    cGP.wait_recv()
    gp = gp + rGP[...].astype(F32)
    gA(3, 0, HL)[...] = gp[:, 0:HL].astype(BF)
    gA(3, HL, HL)[...] = gp[:, HL:D].astype(BF)
    cmix = xchg(mixed.at[pl.ds(own, H), :], mixed.at[pl.ds(own, H), :], yp)

    cAc, cAx, cAz, cGz, cGx, cGc = {}, {}, {}, {}, {}, {}
    cbase = al(c * HL, 128)
    xbase = al(c * HL + x * 192, 64)

    def ar_core(s):
        cAc[s] = xchg(gA(s, al((1 - c) * HL, 128), HL), rAc.at[s], core)

    def ar_x(s):
        cAc[s].wait_recv()
        ref = gA(s, cbase, HL)
        ref[...] = (ref[...].astype(F32) + rAc[s].astype(F32)).astype(BF)
        cAx[s] = xchg(gA(s, al(c * HL + (1 - x) * 192, 64), 192), rAx.at[s], xp)

    def ar_z(s):
        cAx[s].wait_recv()
        ref = gA(s, xbase, 192)
        ref[...] = (ref[...].astype(F32) + rAx[s].astype(F32)).astype(BF)
        cAz[s] = [xchg(gA(s, al(xbase + zk[k] * 48, 16), 48), rAz.at[s, k], zp[k]) for k in (1, 2, 3)]

    def ar_fin(s):
        for cp in cAz[s]:
            cp.wait_recv()
        zb = al(xbase + z * 48, 16)
        total = gA(s, zb, 48)[...].astype(F32)
        for k in (1, 2, 3):
            total = total + rAz[s, k].astype(F32)
        spot = fA.at[s, pl.ds(zb, 48), :]
        spot[...] = total.astype(BF)
        cGz[s] = [xchg(spot, spot, zp[k]) for k in (1, 2, 3)]

    def ar_gx(s):
        for cp in cGz[s]:
            cp.wait_recv()
        spot = fA.at[s, pl.ds(xbase, 192), :]
        cGx[s] = xchg(spot, spot, xp)

    def ar_gc(s):
        cGx[s].wait_recv()
        spot = fA.at[s, pl.ds(cbase, HL), :]
        cGc[s] = xchg(spot, spot, core)

    ar_core(3)
    rs_y()

    def dn1_other(b, carry):
        r0 = al(oth + b * BLK, BLK)
        finish_rows(r0)
        n2[pl.ds(al(b * BLK, BLK), BLK), :] = dn1_rows(r0).astype(BF)
        return carry

    lax.fori_loop(0, 2, dn1_other, 0)
    cdn = xchg(n2.at[0:H, :], rN1, yp)
    ar_x(3)
    lax.fori_loop(3, 4, back_step, 0)
    for b in range(2):
        finish_rows(al(own + b * BLK, BLK))

    def gw(s, src):
        def body(m, carry):
            rows = pl.ds(al(m * BLK, BLK), BLK)
            gA(s, al(m * BLK, BLK), BLK)[...] = nn(nT[rows, :], src[...]).astype(BF)
            return carry

        lax.fori_loop(0, 3, body, 0)
        ar_core(s)

    ar_z(3)
    gw(0, act.at[:, 0:HL])
    gw(1, act.at[:, HL:D])
    ar_x(0)
    gw(2, dh.at[:, 0:HL])
    ar_x(1)
    ar_fin(3)
    ar_z(0)
    rs_c()
    ar_x(2)

    vecA[0] = jnp.zeros((16, D), F32)
    for i, row in ((3, sp), (4, s2g), (5, s2b), (6, sd)):
        vecA[0, i : i + 1, :] = row
    vecA[0, pl.ds(8 + 2 * tr[0] + c, 1), :] = bsum0
    vecA[0, pl.ds(8 + 2 * tr[1] + c, 1), :] = bsum1
    vecA[0, pl.ds(12 + t, 1), 0:HL] = rowsum(act[:, 0:HL].astype(F32))
    vecA[0, pl.ds(12 + t, 1), HL:D] = rowsum(dh[:, 0:HL].astype(F32))

    cdn.wait_recv()
    stok, s1g, s1b = zrow, zrow, zrow
    cgin = []
    for b in range(2):
        o0 = b * BLK
        r0 = al(own + o0, BLK)
        rows = pl.ds(r0, BLK)
        dn = dn1_rows(r0) + rN1[o0 : o0 + BLK, :].astype(F32)
        m, v = start_rows(r0)
        cent, r = stats(v)
        xhat = cent * r
        dst = mid[o0 : o0 + BLK, :] + norm_back(xhat, r, dn, ln1g)
        gin[rows, :] = jnp.where(m, 0.0, dst).astype(BF)
        cgin.append(xchg(gin.at[rows, :], gin.at[rows, :], yp))
        stok = stok + rowsum(jnp.where(m, dst, 0.0))
        s1g = s1g + rowsum(dn * xhat)
        s1b = s1b + rowsum(dn)
    for i, row in ((0, stok), (1, s1g), (2, s1b)):
        vecA[0, i : i + 1, :] = row
    cv = xchg(vecA.at[0], vR.at[0], core)
    ar_z(1)
    ar_z(2)
    ar_gx(3)
    ar_fin(0)
    cv.wait_recv()
    vecA[1] = vecA[0] + vR[0]
    cv = xchg(vecA.at[1], vR.at[1], xp)
    ar_fin(1)
    ar_fin(2)
    ar_gx(0)
    cv.wait_recv()
    vecA[2] = vecA[1] + vR[1]
    cv = xchg(vecA.at[2], vR.at[2], yp)
    rs_end()
    ar_gc(3)
    ar_gx(1)
    ar_gx(2)
    cv.wait_recv()
    vecA[3] = vecA[2] + vR[2]
    cvs = [xchg(vecA.at[3], vR.at[2 + k], zp[k]) for k in (1, 2, 3)]
    ar_gc(0)
    ar_gc(1)
    for cp in cvs:
        cp.wait_recv()
    vout[...] = (vecA[3] + vR[3]) + (vR[4] + vR[5])
    ar_gc(2)
    for s in range(4):
        cGc[s].wait_recv()
    cmix.wait_recv()
    for cp in cgin:
        cp.wait_recv()
    waited = set()
    for a in (0, 1):
        waited.add(id(ccp[a]))
        waited.update(id(cp) for cp in zc[a][1:])
        for q in (xc[a], yc[a]):
            waited.update(id(q[key]) for key in q)
    waited.update(id(cp) for cp in (cn2, catt, cN, cO))
    for cp in pending:
        if id(cp) not in waited:
            cp.wait_send()


def scratch():
    def v(shape, dt):
        return pltpu.VMEM(shape, dt)

    return [
        v((T, D), BF), v((D, T), BF), v((3, T, HL), BF), v((T, HL), BF), v((2, H, HL), BF), v((2, HL, D), BF),
        v((2, D, D), BF), v((2, D, D), BF), v((H, D), F32), v((T, D), BF), v((T, D), BF), v((D, T), BF),
        v((T, D), F32), v((T, D), F32), v((H, D), BF), v((H, D), BF), v((T, D), BF), v((T, D), BF),
        v((2, 2, 4, 96, D), BF), v((2, 2, 4, 96, D), BF),
        v((2, 2, 4, 96, D), BF), v((2, 2, 4, 96, D), BF), v((2, 96, D), BF), v((2, 96, D), BF),
        v((2, 96, D), F32), v((2, 48, D), F32), v((T, HL), BF), v((H, D), BF), v((HL, D), BF),
        v((4, HL, HL), BF), v((4, 192, HL), BF), v((4, 4, 48, HL), BF),
        v((8, T), F32), v((2, 8, D), F32), v((4, 16, D), F32), v((6, 16, D), F32),
        pltpu.SemaphoreType.DMA((XCH,)), pltpu.SemaphoreType.DMA((XCH,)), pltpu.SemaphoreType.DMA((2,)),
    ]


def on_device(
    patches, image_ids, valid, mask_pos, mask_token, ln1_gain, ln1_bias, w_qkv, b_qv, w_proj, b_proj,
    ln2_gain, ln2_bias, w_up, b_up, w_down, b_down, cotangent,
):
    code = image_ids[0] + 16 * valid[0] + 32 * mask_pos[0]
    codec = code[:, None]
    coder = code[None, :]
    vec = jnp.stack([mask_token, ln1_gain, ln1_bias, b_proj, ln2_gain, ln2_bias, b_down, b_down]).astype(F32)
    bup = jnp.pad(b_up.astype(F32).reshape(2, D), ((0, 6), (0, 0)))
    spec = pl.BlockSpec(memory_space=pltpu.VMEM)
    sds = jax.ShapeDtypeStruct
    mixed, gin, fa, gup, gdn, vs = pl.pallas_call(
        mega,
        out_shape=(
            sds((T, D), BF), sds((T, D), BF), sds((4, D, HL), BF), sds((48, 2 * D), F32), sds((48, 2 * D), F32),
            sds((16, D), F32),
        ),
        in_specs=[spec] * 10 + [pl.BlockSpec(memory_space=pl.ANY)],
        out_specs=(spec,) * 6,
        scratch_shapes=scratch(),
        compiler_params=pltpu.CompilerParams(collective_id=0, has_side_effects=True, vmem_limit_bytes=66584576),
        name="block",
    )(
        patches, codec, coder, vec, jnp.transpose(w_qkv, (1, 0, 2)), b_qv.astype(F32), w_proj, w_up, w_down.T, bup,
        cotangent,
    )
    t = lax.axis_index("tensor")
    grad_qkv = jnp.transpose(fa[0:3], (1, 0, 2)).astype(F32)
    grad_proj = jnp.concatenate([fa[3, 0:HL], fa[3, HL:D]], axis=1).astype(F32)
    grad_b_up = lax.dynamic_slice_in_dim(vs, 8 + 2 * t, 2, 0).reshape(2 * D)
    grad_b_qv = lax.dynamic_slice_in_dim(vs, 12 + t, 1, 0).reshape(2, HL)
    return (
        mixed, gin.astype(F32), vs[0], vs[1], vs[2], grad_qkv, grad_b_qv, grad_proj, vs[3], vs[4], vs[5],
        gup, grad_b_up, gdn.T, vs[6],
    )


HEAD_DIM = 64


def norm_rows(values, gain, shift):
    mean = jnp.mean(values, axis=-1, keepdims=True)
    cent = values - mean
    var = jnp.mean(cent * cent, axis=-1, keepdims=True)
    return cent * lax.rsqrt(var + EPS) * gain + shift


def left_dot(first, second):
    return lax.dot_general(
        first, second, (((0,), (0,)), ((), ())), preferred_element_type=jnp.float32
    )


def right_dot(first, second):
    return lax.dot_general(
        first, second, (((1,), (1,)), ((), ())), preferred_element_type=jnp.float32
    )


def allowed_rows(ids, live, begin, count):
    rows = ids.shape[0]
    own_ids = lax.dynamic_slice_in_dim(ids, begin, count, 0)
    places = begin + jnp.arange(count)
    same_place = places[:, None] == jnp.arange(rows)[None, :]
    return (own_ids[:, None] == ids[None, :]) & ((live[None, :] == 1) | same_place)


def spread(
    patches,
    image_ids,
    valid,
    mask_pos,
    mask_token,
    ln1_gain,
    ln1_bias,
    w_qkv,
    b_qv,
    w_proj,
    b_proj,
    ln2_gain,
    ln2_bias,
    w_up,
    b_up,
    w_down,
    b_down,
    cotangent,
):
    rows = patches.shape[0]
    local_width = w_qkv.shape[2]
    local_heads = local_width // HEAD_DIM
    scale = 1.0 / HEAD_DIM**0.5
    ids = image_ids[0]
    live = valid[0]
    masked = mask_pos[0][:, None] == 1
    block = min(512, rows)
    blocks = rows // block
    start = jnp.where(masked, mask_token.astype(jnp.float32)[None, :], patches.astype(jnp.float32))
    normed, norm1_pull = jax.vjp(
        norm_rows, start, ln1_gain.astype(jnp.float32), ln1_bias.astype(jnp.float32)
    )
    normed_b = normed.astype(jnp.bfloat16)
    qv_bias = b_qv.astype(jnp.float32)
    bias = jnp.stack([qv_bias[0], jnp.zeros_like(qv_bias[0]), qv_bias[1]])
    qkv = jnp.einsum("td,dsc->tsc", normed_b, w_qkv, preferred_element_type=jnp.float32)
    qkv_b = (qkv + bias[None]).astype(jnp.bfloat16)
    query = qkv_b[:, 0].reshape(rows, local_heads, HEAD_DIM)
    keys = qkv_b[:, 1].reshape(rows, local_heads, HEAD_DIM)
    values = qkv_b[:, 2].reshape(rows, local_heads, HEAD_DIM)
    outputs = []
    totals = []
    for index in range(blocks):
        begin = index * block
        query_part = query[begin : begin + block]
        allowed = allowed_rows(ids, live, begin, block)
        scores = (
            jnp.einsum("qhc,khc->hqk", query_part, keys, preferred_element_type=jnp.float32) * scale
        )
        scores = jnp.where(allowed[None], scores, -1e30)
        top = jnp.max(scores, axis=-1, keepdims=True)
        expd = jnp.exp(scores - top)
        summed = jnp.sum(expd, axis=-1, keepdims=True)
        probs_b = (expd / summed).astype(jnp.bfloat16)
        totals.append(top + jnp.log(summed))
        outputs.append(
            jnp.einsum("hqk,khc->qhc", probs_b, values, preferred_element_type=jnp.float32)
        )
    attended_b = jnp.concatenate(outputs, axis=0).reshape(rows, local_width).astype(jnp.bfloat16)
    attn_part = jnp.dot(attended_b, w_proj, preferred_element_type=jnp.float32)
    ln2_gain_f = ln2_gain.astype(jnp.float32)
    ln2_bias_f = ln2_bias.astype(jnp.float32)
    attn_total = lax.psum(attn_part, "tensor")
    middle = start + attn_total + b_proj.astype(jnp.float32)
    normed2, norm2_pull = jax.vjp(norm_rows, middle, ln2_gain_f, ln2_bias_f)
    normed2_b = normed2.astype(jnp.bfloat16)
    up_full, down_full = (
        lax.all_gather(w_up, "dp", axis=0, tiled=True),
        lax.all_gather(w_down, "dp", axis=1, tiled=True),
    )
    hidden = jnp.dot(normed2_b, up_full, preferred_element_type=jnp.float32) + b_up.astype(
        jnp.float32
    )
    active, gelu_pull = jax.vjp(partial(jax.nn.gelu, approximate=False), hidden)
    active_b = active.astype(jnp.bfloat16)
    mlp_part = jnp.dot(active_b, down_full, preferred_element_type=jnp.float32)
    mlp_total = lax.psum(mlp_part.astype(jnp.bfloat16), "tensor").astype(jnp.float32)
    mixed = (middle + mlp_total + b_down.astype(jnp.float32)).astype(jnp.bfloat16)
    seed_grad = cotangent.astype(jnp.float32)
    up_back, down_back = (up_full, down_full)
    grad_b_down = jnp.sum(seed_grad, axis=0)
    grad_down_local = left_dot(active_b, cotangent)
    grad_active = right_dot(cotangent, down_back)
    (grad_hidden,) = gelu_pull(grad_active)
    grad_hidden_b = grad_hidden.astype(jnp.bfloat16)
    grad_b_up = jnp.sum(grad_hidden_b.astype(jnp.float32), axis=0)
    grad_up_local = left_dot(normed2_b, grad_hidden_b)
    grad_normed2_part = right_dot(grad_hidden_b, up_back)
    grad_normed2 = lax.psum(grad_normed2_part, "tensor")
    grad_mid_norm, grad_ln2_gain, grad_ln2_bias = norm2_pull(grad_normed2)
    grad_middle = seed_grad + grad_mid_norm
    grad_w_up, grad_w_down = (
        lax.psum_scatter(grad_up_local, "dp", scatter_dimension=0, tiled=True),
        lax.psum_scatter(grad_down_local, "dp", scatter_dimension=1, tiled=True),
    )
    grad_branch_b = grad_middle.astype(jnp.bfloat16)
    grad_b_proj = jnp.sum(grad_branch_b.astype(jnp.float32), axis=0)
    grad_w_proj = left_dot(attended_b, grad_branch_b)
    grad_attended = (
        right_dot(grad_branch_b, w_proj).astype(jnp.bfloat16).reshape(rows, local_heads, HEAD_DIM)
    )
    grad_query_parts = []
    grad_keys = jnp.zeros((rows, local_heads, HEAD_DIM), jnp.float32)
    grad_values = jnp.zeros((rows, local_heads, HEAD_DIM), jnp.float32)
    for index in range(blocks):
        begin = index * block
        query_part = query[begin : begin + block]
        grad_out_part = grad_attended[begin : begin + block]
        allowed = allowed_rows(ids, live, begin, block)
        scores = (
            jnp.einsum("qhc,khc->hqk", query_part, keys, preferred_element_type=jnp.float32) * scale
        )
        scores = jnp.where(allowed[None], scores, -1e30)
        probs = jnp.exp(scores - totals[index])
        probs_b = probs.astype(jnp.bfloat16)
        grad_values = grad_values + jnp.einsum(
            "hqk,qhc->khc", probs_b, grad_out_part, preferred_element_type=jnp.float32
        )
        grad_probs = jnp.einsum(
            "qhc,khc->hqk", grad_out_part, values, preferred_element_type=jnp.float32
        )
        inner = jnp.sum(probs * grad_probs, axis=-1, keepdims=True)
        grad_scores_b = (probs * (grad_probs - inner)).astype(jnp.bfloat16)
        grad_query_parts.append(
            jnp.einsum("hqk,khc->qhc", grad_scores_b, keys, preferred_element_type=jnp.float32)
            * scale
        )
        grad_keys = (
            grad_keys
            + jnp.einsum(
                "hqk,qhc->khc", grad_scores_b, query_part, preferred_element_type=jnp.float32
            )
            * scale
        )
    grad_query = jnp.concatenate(grad_query_parts, axis=0)
    grad_qkv_b = (
        jnp.stack([grad_query, grad_keys, grad_values], axis=1)
        .reshape(rows, 3, local_width)
        .astype(jnp.bfloat16)
    )
    grad_qkv_f = grad_qkv_b.astype(jnp.float32)
    grad_b_qv = jnp.stack([jnp.sum(grad_qkv_f[:, 0], axis=0), jnp.sum(grad_qkv_f[:, 2], axis=0)])
    grad_w_qkv = jnp.einsum("td,tsc->dsc", normed_b, grad_qkv_b, preferred_element_type=jnp.float32)
    grad_normed_part = jnp.einsum(
        "tsc,dsc->td", grad_qkv_b, w_qkv, preferred_element_type=jnp.float32
    )
    grad_normed = lax.psum(grad_normed_part.astype(jnp.bfloat16), "tensor").astype(jnp.float32)
    grad_start_norm, grad_ln1_gain, grad_ln1_bias = norm1_pull(grad_normed)
    grad_start = grad_middle + grad_start_norm
    grad_input = jnp.where(masked, 0.0, grad_start)
    grad_token = jnp.sum(jnp.where(masked, grad_start, 0.0), axis=0)
    summed = lax.psum(
        (
            grad_token,
            grad_ln1_gain,
            grad_ln1_bias,
            grad_w_qkv,
            grad_b_qv,
            grad_w_proj,
            grad_b_proj,
            grad_ln2_gain,
            grad_ln2_bias,
            grad_b_up,
            grad_b_down,
        ),
        "dp",
    )
    return (
        mixed,
        grad_input,
        summed[0],
        summed[1],
        summed[2],
        summed[3],
        summed[4],
        summed[5],
        summed[6],
        summed[7],
        summed[8],
        grad_w_up,
        summed[9],
        grad_w_down,
        summed[10],
    )


def solution(mesh):
    placed = (
        P("dp", None),
        P("dp", None),
        P("dp", None),
        P("dp", None),
        P(),
        P(),
        P(),
        P(None, None, "tensor"),
        P(None, "tensor"),
        P("tensor", None),
        P(),
        P(),
        P(),
        P("dp", "tensor"),
        P("tensor"),
        P("tensor", "dp"),
        P(),
        P("dp", None),
    )
    fits = mesh.shape["dp"] == 16 and mesh.shape["tensor"] == 2
    return jax.shard_map(
        on_device if fits else spread,
        mesh=mesh,
        in_specs=placed,
        out_specs=(
            P("dp", None),
            P("dp", None),
            P(),
            P(),
            P(),
            P(None, None, "tensor"),
            P(None, "tensor"),
            P("tensor", None),
            P(),
            P(),
            P(),
            P("dp", "tensor"),
            P("tensor"),
            P("tensor", "dp"),
            P(),
        ),
        check_vma=False,
    )
```

```python
from functools import partial

import jax
import jax.numpy as jnp
from jax import lax
from jax.experimental import pallas as pl
from jax.experimental.pallas import tpu as pltpu
from jax.sharding import PartitionSpec as P

BF = jnp.bfloat16
F32 = jnp.float32
MESH = pl.DeviceIdType.MESH
EPS = 1e-06
T = 1024
H = 512
D = 768
HL = 384
BLK = 256
WIN = 768
XCH = 240


def nn(a, b):
    return lax.dot_general(a, b, (((1,), (0,)), ((), ())), preferred_element_type=F32)


def nt(a, b):
    return lax.dot_general(a, b, (((1,), (1,)), ((), ())), preferred_element_type=F32)


def tn(a, b):
    return lax.dot_general(a, b, (((0,), (0,)), ((), ())), preferred_element_type=F32)


def rowsum(v):
    return jnp.sum(v, axis=0, keepdims=True)


def lane_half(shape):
    return lax.broadcasted_iota(jnp.int32, shape, 1) < 64


def stats(v):
    mean = jnp.sum(v, axis=-1, keepdims=True) * (1.0 / D)
    cent = v - mean
    var = jnp.sum(cent * cent, axis=-1, keepdims=True) * (1.0 / D)
    return cent, lax.rsqrt(var + EPS)


def norm_back(xhat, r, d, gain):
    e = d * gain
    m1 = jnp.sum(e, axis=-1, keepdims=True) * (1.0 / D)
    m2 = jnp.sum(e * xhat, axis=-1, keepdims=True) * (1.0 / D)
    return r * (e - m1 - xhat * m2)


def mega(
    patches, ids, live, hidden_pos, token_b, ln1g_b, ln1b_b, bproj_b, ln2g_b, ln2b_b, bdown_b, wqkv_h, bqv_b, wproj,
    up, dn, bup, cot,
    mixed, gin, fA, gup, gdn, vout,
    n1, nT, qkv, attO, attF, wpf, Wu, Wd, mid, n2, dml, dmlT, outA, dn2A, rO, rN, act, dh, gU, gD,
    rG, rX, sy, ry, sc, rc, dO, rgp, rA, lseT, bupA, vecA, vR, pat, wqkv, codec, coder, vec, mixS, ginS, fS,
    gS, ssem, rsem, lsem,
):
    d = lax.axis_index("dp")
    t = lax.axis_index("tensor")
    z = lax.div(d, 4)
    x = lax.rem(lax.div(d, 2), 2)
    c = lax.rem(d, 2)
    zk = (z, z + 1 - 2 * lax.rem(z, 2), lax.rem(z + 2, 4), 3 - z)
    xr = (x, 1 - x)
    tr = (t, 1 - t)

    def dev(zz, xx, cc, tt):
        return ((zz * 2 + xx) * 2 + cc, tt)

    core = dev(z, x, 1 - c, t)
    xp = dev(z, 1 - x, c, t)
    yp = dev(z, x, c, 1 - t)
    z1 = dev(zk[1], x, c, t)
    z2 = dev(zk[2], x, c, t)
    z3 = dev(zk[3], x, c, t)
    mid_z = (z == 1) | (z == 2)
    end_z = (z == 0) | (z == 3)

    pending = []
    flushed = set()
    slots = [0]

    def slot():
        slots[0] += 1
        return slots[0] - 1

    def xchg(src, dst, to, when=None, land=None):
        i = len(pending)
        cp = pltpu.make_async_remote_copy(
            src_ref=src, dst_ref=dst, send_sem=ssem.at[i], recv_sem=rsem.at[slot() if land is None else land],
            device_id=to, device_id_type=MESH,
        )
        pending.append((cp, when))
        if when is None:
            cp.start()
        else:
            pl.when(when)(cp.start)
        return cp

    def landed(dst, land, frm):
        pltpu.make_async_remote_copy(
            src_ref=dst, dst_ref=dst, send_sem=ssem.at[0], recv_sem=rsem.at[land], device_id=frm, device_id_type=MESH
        ).wait_recv()

    def flush(cps):
        cps = set(id(cp) for cp in cps)
        for cp, when in pending:
            if id(cp) in cps and id(cp) not in flushed:
                flushed.add(id(cp))
                if when is None:
                    cp.wait_send()
                else:
                    pl.when(when)(cp.wait_send)

    def al(v, m):
        return pl.multiple_of(v, m)

    bar = pltpu.get_barrier_semaphore()
    peers = (core, xp, yp, z1, z2, z3)
    for p in peers:
        pl.semaphore_signal(bar, inc=1, device_id=p, device_id_type=MESH)
    loads = []

    def load(src, dst):
        cp = pltpu.make_async_copy(src, dst, lsem.at[len(loads)])
        cp.start()
        loads.append(cp)
        return cp

    lpat = load(patches, pat)
    lwq = load(wqkv_h, wqkv)
    code = ids[...] + 16 * live[...] + 32 * hidden_pos[...]
    coder[...] = code
    codec[...] = jnp.broadcast_to(code.astype(F32), (128, T)).T.astype(jnp.int32)
    for i, row in enumerate((token_b, ln1g_b, ln1b_b, bproj_b, ln2g_b, ln2b_b, bdown_b)):
        vec[i : i + 1, :] = row[...].astype(F32).reshape(1, D)
    bqv = bqv_b[...].astype(F32)
    bupA[0] = jnp.zeros((8, D), F32)
    for i in range(2):
        bupA[0, i : i + 1, :] = bup[i * D : i * D + D].astype(F32).reshape(1, D)
    pl.semaphore_wait(bar, len(peers))

    own = al(t * H, H)
    oth = al((1 - t) * H, H)
    cslot = al(c * H, H)
    sslot = al((1 - c) * H, H)
    W = (Wu, Wd)
    shards = (up, dn)

    def wblk(a, k, xx, yy):
        return W[a].at[tr[yy], pl.ds(al((zk[k] * 2 + xr[xx]) * 96, 32), 96), :]

    ccp = []
    mine = al((z * 2 + x) * 96 + c * 48, 16)
    for a in (0, 1):
        ccp.append(
            xchg(shards[a].at[:, pl.ds(al((1 - c) * D, 128), D)], W[a].at[t, pl.ds(mine, 48), :], core)
        )
    whalf = pl.ds(al(c * 192, 64), 192)
    cwp = xchg(wproj.at[whalf, :], wpf.at[t, whalf, :], yp)
    cbup = xchg(bupA.at[0], bupA.at[1], yp)
    cdml = xchg(cot.at[pl.ds(own, H), :], dml.at[pl.ds(cslot, H), :], core)
    ldml = load(cot.at[pl.ds(own, H), :], dml.at[pl.ds(cslot, H), :])
    lwp = load(wproj, wpf.at[t])
    for a in (0, 1):
        W[a][t, pl.ds(mine, 48), :] = shards[a][:, pl.ds(al(c * D, 128), D)]

    zc, xc, yc = {}, {}, {}

    zsent = []
    zland = {(a, k, yy): slot() for a in (0, 1) for k in (1, 2, 3) for yy in (0, 1)}

    def zpass(a, k, yy, to, as_k, when):
        zsent.append(xchg(wblk(a, k, 0, yy), wblk(a, k, 0, yy), to, when, zland[(a, as_k, yy)]))

    def zwait(a, k, yy):
        landed(wblk(a, k, 0, yy), zland[(a, k, yy)], z1)

    def zstart(a, yy):
        zpass(a, 0, yy, z1, 1, None)
        zpass(a, 0, yy, z3, 3, mid_z)

    def zstep1(a, yy):
        zwait(a, 1, yy)
        zpass(a, 1, yy, z3, 2, mid_z)
        pl.when(mid_z)(partial(zwait, a, 3, yy))
        zpass(a, 3, yy, z1, 2, mid_z)

    def zstep2(a, yy):
        zwait(a, 2, yy)
        zpass(a, 2, yy, z1, 3, mid_z)

    def zstep3(a, yy):
        pl.when(end_z)(partial(zwait, a, 3, yy))

    def xsend(a, k, yy):
        xc[(a, k, yy)] = xchg(wblk(a, k, 0, yy), wblk(a, k, 0, yy), xp)

    def ysend(a, k, xx):
        yc[(a, k, xx)] = xchg(wblk(a, k, xx, 0), wblk(a, k, xx, 0), yp)

    token = vec[0:1, :]
    ln1g = vec[1:2, :]
    ln1b = vec[2:3, :]

    def start_rows(r0):
        m = lax.shift_right_logical(codec[pl.ds(r0, BLK), 0:1], 5) == 1
        return m, jnp.where(m, token, pat[pl.ds(r0, BLK), :].astype(F32))

    def ln1_block(b, carry):
        r0 = al(b * BLK, BLK)
        _, v = start_rows(r0)
        cent, r = stats(v)
        nb = (cent * r * ln1g + ln1b).astype(BF)
        n1[pl.ds(r0, BLK), :] = nb
        for s in range(3):
            y = nn(nb, wqkv[s])
            if s == 0:
                y = y + bqv[0:1, :]
            if s == 2:
                y = y + bqv[1:2, :]
            qkv[s, pl.ds(r0, BLK), :] = y.astype(BF)
        return carry

    lpat.wait()
    lwq.wait()
    lax.fori_loop(0, 1, ln1_block, 0)
    for a in (0, 1):
        ccp[a].wait_recv()
    zstart(0, 0)
    zstart(1, 0)
    xsend(0, 0, 0)
    xsend(1, 0, 0)
    ysend(1, 0, 0)
    lax.fori_loop(1, 4, ln1_block, 0)
    for a in (0, 1):
        zstep1(a, 0)
        xsend(a, 1, 0)

    def masked_pair(block, scale=None):
        low = lane_half(block.shape)
        zero = jnp.zeros_like(block)
        if scale is not None:
            block = block * jnp.asarray(scale, BF)
        return jnp.where(low, block, zero), jnp.where(low, zero, block)

    def att_block(half, edge):
        qb = half * 3 if edge else 1 + half
        win = H if edge else WIN
        r0 = al(qb * BLK, BLK)
        ws = al(half * H if edge else half * BLK, BLK)
        cr = codec[pl.ds(r0, BLK), 0:1]
        cw = coder[:, pl.ds(ws, win)]
        rid = r0 + lax.broadcasted_iota(jnp.int32, (BLK, win), 0)
        cid = ws + lax.broadcasted_iota(jnp.int32, (BLK, win), 1)
        ok = ((cr & 15) == (cw & 15)) & (((cw & 16) == 16) | (rid == cid))
        dn2A[0:BLK, 0:win] = jnp.where(ok, 0.0, -1e30)
        lane = lax.broadcasted_iota(jnp.int32, (BLK, 128), 1)
        lacc = jnp.zeros((BLK, 128), F32)
        for p in range(3):
            cols = slice(p * 128, p * 128 + 128)
            qs = masked_pair(qkv[0, pl.ds(r0, BLK), cols], 0.125)
            kp = qkv[1, pl.ds(ws, win), cols]
            vp = qkv[2, pl.ds(ws, win), cols]
            outs = []
            for h in range(2):
                s = nt(qs[h], kp) + dn2A[0:BLK, 0:win]
                top = jnp.max(s, axis=-1, keepdims=True)
                e = jnp.exp(s - top)
                l = jnp.sum(e, axis=-1, keepdims=True)
                o = nn(e.astype(BF), vp) * (1.0 / l)
                outs.append(o)
                lacc = jnp.where(lane == (2 * p + h), top + jnp.log(l), lacc)
            attO[pl.ds(r0, BLK), cols] = jnp.where(lane_half((BLK, 128)), outs[0], outs[1]).astype(BF)
        lseT[:, pl.ds(r0, BLK)] = lacc.T[0:8, :]
        return r0

    catt = []

    def att_send(r0):
        catt.append(xchg(attO.at[pl.ds(r0, BLK), :], attF.at[t, pl.ds(al(r0 - oth, BLK), BLK), :], yp))

    att_send(att_block(1 - t, True))
    att_send(att_block(1 - t, False))
    for a in (0, 1):
        zstep2(a, 0)
        xsend(a, 2, 0)
    ysend(0, 0, 0)
    ysend(0, 1, 0)
    ysend(0, 2, 0)
    cwp.wait_recv()
    cwc = xchg(wpf.at[1 - t, whalf, :], wpf.at[1 - t, whalf, :], core)
    att_block(t, True)
    att_block(t, False)
    attF[t] = attO[pl.ds(own, H), :]
    for a in (0, 1):
        zstep3(a, 0)
        xsend(a, 3, 0)
    ysend(0, 3, 0)
    yc[(1, 0, 0)].wait_recv()
    zstart(1, 1)
    xsend(1, 0, 1)

    bproj = vec[3:4, :]
    ln2g = vec[4:5, :]
    ln2b = vec[5:6, :]
    bdown = vec[6:7, :]
    ldml.wait()
    lwp.wait()
    for cp in catt:
        cp.wait_recv()
    cwc.wait_recv()

    def mid_block(b, carry):
        o0 = al(b * BLK, BLK)
        _, v = start_rows(al(own + o0, BLK))
        m = v + (nn(attF[0, pl.ds(o0, BLK), :], wpf[0]) + nn(attF[1, pl.ds(o0, BLK), :], wpf[1])) + bproj
        mid[pl.ds(o0, BLK), :] = m
        cent, r = stats(m)
        n2[pl.ds(al(cslot + o0, BLK), BLK), :] = (cent * r * ln2g + ln2b).astype(BF)
        return carry

    lax.fori_loop(0, 2, mid_block, 0)
    cn2 = xchg(n2.at[pl.ds(cslot, H), :], n2.at[pl.ds(cslot, H), :], core)
    cdml.wait_recv()
    cn2.wait_recv()
    nT[...] = n2[...].T
    dmlT[...] = dml[...].T
    cbup.wait_recv()
    for k in range(4):
        xc[(0, k, 0)].wait_recv()
        ysend(0, k, 1)
    for k in range(4):
        xc[(1, k, 0)].wait_recv()
    zstep1(1, 1)
    xsend(1, 1, 1)

    G = (gU, gD)
    rs = {}

    def addto(dst, src):
        dst[...] = (dst[...].astype(F32) + src[...].astype(F32)).astype(BF)

    def rs_x(a, j):
        rs[(a, j)] = [xchg(G[a].at[j, 1, h * 2 : h * 2 + 2], rG.at[a, j, h * 2 : h * 2 + 2], xp) for h in (0, 1)]

    rland = {(a, j, q): slot() for a in (0, 1) for j in (0, 1) for q in range(4, 9)}

    def rpass(a, j, k, to, q, when):
        xchg(G[a].at[j, 0, zk[k]], rG.at[a, j, q], to, when, rland[(a, j, q)])

    def radd(a, j, k, q):
        landed(rG.at[a, j, q], rland[(a, j, q)], z1)
        addto(G[a].at[j, 0, zk[k]], rG.at[a, j, q])

    def rs_z1(a, j):
        for cp in rs[(a, j)]:
            cp.wait_recv()
        for zz in range(4):
            addto(G[a].at[j, 0, zz], rG.at[a, j, zz])
        for k, q in ((3, 4), (2, 5), (1, 6)):
            rpass(a, j, k, z1, q, end_z)

    def rs_z2(a, j):
        pl.when(mid_z)(partial(radd, a, j, 2, 4))
        rpass(a, j, 2, z3, 7, mid_z)
        pl.when(mid_z)(partial(radd, a, j, 3, 5))
        rpass(a, j, 3, z3, 8, mid_z)

    def rs_z3(a, j):
        pl.when(mid_z)(partial(radd, a, j, 1, 7))
        rpass(a, j, 1, z1, 8, mid_z)

    def rs_sum(a, j):
        pl.when(mid_z)(partial(radd, a, j, 0, 6))
        landed(rG.at[a, j, 8], rland[(a, j, 8)], z1)
        return G[a][j, 0, z].astype(F32) + rG[a, j, 8].astype(F32)

    def rs_y(a):
        sy[a] = rs_sum(a, 1).astype(BF)
        rs[(a, "y")] = xchg(sy.at[a], ry.at[a], yp)

    def rs_c(a):
        total = rs_sum(a, 0)
        rs[(a, "y")].wait_recv()
        sc[a] = total + ry[a].astype(F32)
        rs[(a, "c")] = xchg(sc.at[a, pl.ds(al((1 - c) * 48, 16), 48), :], rc.at[a], core)

    def rs_end(a):
        gS[a, :, pl.ds(al(c * D, 128), D)] = sc[a, pl.ds(al(c * 48, 16), 48), :]
        rs[(a, "c")].wait_recv()
        gS[a, :, pl.ds(al((1 - c) * D, 128), D)] = rc[a]
        load(gS.at[a], (gup, gdn)[a])

    bsums = []

    def ff_fwd(j, lo, hi):
        yy = tr[j]
        bu = bupA[j, pl.ds(c, 1), :]

        def block(b, carry):
            rows = pl.ds(al(b * BLK, BLK), BLK)
            hid = nn(n2[rows, :], Wu[yy]) + bu
            phi = 0.5 * (1.0 + lax.erf(hid * 0.7071067811865476))
            a = (hid * phi).astype(BF)
            act[rows, :] = a
            dh[rows, :] = (phi + hid * (jnp.exp(hid * hid * -0.5) * 0.3989422804014327)).astype(BF)
            o = nt(a, Wd[yy])
            if j == 0:
                outA[rows, :] = o
            else:
                outA[rows, :] += o
            return carry

        lax.fori_loop(lo, hi, block, 0)

    def ff_bwd(j, lo, hi, start):
        yy = tr[j]

        def block(b, carry):
            rows = pl.ds(al(b * BLK, BLK), BLK)
            dhid = (nn(dml[rows, :], Wd[yy]) * dh[rows, :].astype(F32)).astype(BF)
            dh[rows, :] = dhid
            g = nt(dhid, Wu[yy])
            if j == 0:
                dn2A[rows, :] = g
            else:
                dn2A[rows, :] += g
            return carry + rowsum(dhid.astype(F32))

        return lax.fori_loop(lo, hi, block, start)

    def ff_grads(j):
        def gw_block(b, carry):
            rows = pl.ds(al(b * 192, 64), 192)
            ru = nn(nT[rows, :], dh[...]).astype(BF)
            rd = nn(dmlT[rows, :], act[...]).astype(BF)
            for xa in range(2):
                rel = lax.rem(xa + x, 2)
                gU[j, rel, b] = ru[xa * 96 : xa * 96 + 96]
                gD[j, rel, b] = rd[xa * 96 : xa * 96 + 96]
            return carry

        lax.fori_loop(0, 4, gw_block, 0)

    zrow = jnp.zeros((1, D), F32)
    ff_fwd(0, 0, 4)
    zstep2(1, 1)
    xsend(1, 2, 1)
    bsums.append(ff_bwd(0, 0, 4, zrow))
    zstep3(1, 1)
    xsend(1, 3, 1)
    ff_grads(0)
    rs_x(0, 0)
    rs_x(1, 0)
    for k in range(4):
        yc[(0, k, 0)].wait_recv()
        yc[(0, k, 1)].wait_recv()
        xc[(1, k, 1)].wait_recv()
    ff_fwd(1, 0, 4)

    flush([cn2])
    n2[H:T, :] = outA[pl.ds(sslot, H), :].astype(BF)
    cO = xchg(n2.at[H:T, :], rO, core)
    bsums.append(ff_bwd(1, 0, 4, zrow))
    n2[0:H, :] = dn2A[pl.ds(sslot, H), :].astype(BF)
    cN = xchg(n2.at[0:H, :], rN, core)

    cO.wait_recv()
    cmix = []

    def mixed_block(o):
        o0 = al(o * BLK, BLK)
        rows = pl.ds(o0, BLK)
        crow = pl.ds(al(cslot + o0, BLK), BLK)
        out = mid[rows, :] + (outA[crow, :] + rO[rows, :].astype(F32)) + bdown
        mixS[rows, :] = out.astype(BF)

    def mixed_send(o):
        orow = pl.ds(al(own + o * BLK, BLK), BLK)
        rows = pl.ds(al(o * BLK, BLK), BLK)
        cmix.append(xchg(mixS.at[rows, :], mixed.at[orow, :], yp))
        load(mixS.at[rows, :], mixed.at[orow, :])

    mixed_block(0)
    mixed_send(0)
    mixed_block(1)
    ff_grads(1)
    rs_x(0, 1)
    rs_z1(0, 0)
    flush(catt)
    cN.wait_recv()
    flush([cN])

    sums = [zrow, zrow, zrow, zrow]
    cda = []
    for o in (t, 1 - t):
        o0 = al(o * BLK, BLK)
        rows = pl.ds(o0, BLK)
        crow = pl.ds(al(cslot + o0, BLK), BLK)
        dnb = dn2A[crow, :] + rN[rows, :].astype(F32)
        cent, r = stats(mid[rows, :])
        xhat = cent * r
        ct = dml[crow, :].astype(F32)
        dm = ct + norm_back(xhat, r, dnb, ln2g)
        db = dm.astype(BF)
        n2[rows, :] = db
        attO[rows, :] = nt(db, wpf[1 - t]).astype(BF)
        orow = pl.ds(al(own + o0, BLK), BLK)
        cda.append(xchg(attO.at[rows, :], dO.at[orow, :], yp))
        dO[orow, :] = nt(db, wpf[t]).astype(BF)
        mid[rows, :] = dm
        for i, term in enumerate((dnb * xhat, dnb, db.astype(F32), ct)):
            sums[i] = sums[i] + rowsum(term)
    s2g, s2b, sp, sd = sums

    mixed_send(1)
    rs_z2(0, 0)
    outA[...] = jnp.zeros((T, D), F32)
    nT[...] = n1[...].T

    def att_back(half, edge):
        qb = half * 3 if edge else 1 + half
        wl = H if edge else WIN
        r0 = al(qb * BLK, BLK)
        ws = al(half * H if edge else half * BLK, BLK)
        cw = codec[pl.ds(ws, wl), 0:1]
        cr = coder[:, pl.ds(r0, BLK)]
        rid = r0 + lax.broadcasted_iota(jnp.int32, (wl, BLK), 1)
        cid = ws + lax.broadcasted_iota(jnp.int32, (wl, BLK), 0)
        ok = ((cr & 15) == (cw & 15)) & (((cw & 16) == 16) | (rid == cid))
        dn2A[0:wl, 0:BLK] = jnp.where(ok, 0.0, -1e30)
        rows = pl.ds(r0, BLK)
        win = pl.ds(ws, wl)
        for p in range(3):
            cols = slice(p * 128, p * 128 + 128)
            vcols = slice(HL + p * 128, HL + p * 128 + 128)
            qp = qkv[0, rows, cols]
            op = dO[rows, cols]
            qs = masked_pair(qp, 0.125)
            os = masked_pair(op)
            kp = qkv[1, win, cols]
            vp = qkv[2, win, cols]
            dqs, dks, dvs = [], [], []
            for h in range(2):
                lse = lseT[2 * p + h : 2 * p + h + 1, rows]
                pr = jnp.exp(nt(kp, qs[h]) + dn2A[0:wl, 0:BLK] - lse)
                dp = nt(vp, os[h])
                inner = rowsum(pr * dp)
                ds = (pr * (dp - inner)).astype(BF)
                dvs.append(nn(pr.astype(BF), op))
                dks.append(nn(ds, qp))
                dqs.append(tn(ds, kp))
            low = lane_half((BLK, 128))
            lowk = lane_half((wl, 128))
            act[rows, cols] = (jnp.where(low, dqs[0], dqs[1]) * 0.125).astype(BF)
            outA[win, cols] += jnp.where(lowk, dks[0], dks[1])
            outA[win, vcols] += jnp.where(lowk, dvs[0], dvs[1])

    def finish_rows(r0):
        rows = pl.ds(r0, BLK)
        act[rows, HL:D] = (outA[rows, 0:HL] * 0.125).astype(BF)
        dh[rows, 0:HL] = outA[rows, HL:D].astype(BF)

    def dn1_rows(r0):
        rows = pl.ds(r0, BLK)
        return nt(act[rows, 0:HL], wqkv[0]) + nt(act[rows, HL:D], wqkv[1]) + nt(dh[rows, 0:HL], wqkv[2])

    att_back(t, False)

    flush(ccp)
    flush(zsent)
    for q in (xc, yc):
        flush(q.values())
    ar = {}

    def gA(s, r0, n):
        if s == 4:
            return Wd.at[0, pl.ds(r0, n), 0:HL]
        return Wu.at[s // 2, pl.ds(r0, n), (s % 2) * HL : (s % 2) * HL + HL]

    cbase = al(c * HL, 128)
    xbase = al(c * HL + x * 192, 64)
    XFIRST = (True, False, True, False, False)

    def blk_z(s, k):
        if XFIRST[s]:
            return al(xbase + zk[k] * 48, 16), 48
        return al(cbase + zk[k] * 96, 32), 96

    def spot_of(s):
        if XFIRST[s]:
            return al(xbase + z * 48, 16)
        return al(cbase + z * 96 + x * 48, 16)

    def ar_core(s):
        ar[(s, 0)] = xchg(gA(s, al((1 - c) * HL, 128), HL), rA.at[s, 0:HL, :], core)

    def ar_x(s):
        if XFIRST[s]:
            ar[(s, "x")] = xchg(gA(s, al(c * HL + (1 - x) * 192, 64), 192), rA.at[s, 384:576, :], xp)
        else:
            ar[(s, "x")] = xchg(gA(s, al(cbase + z * 96 + (1 - x) * 48, 16), 48), rA.at[s, 672:720, :], xp)

    def ar_xadd(s):
        ar[(s, "x")].wait_recv()
        if XFIRST[s]:
            addto(gA(s, xbase, 192), rA.at[s, 384:576, :])
        else:
            addto(gA(s, spot_of(s), 48), rA.at[s, 672:720, :])

    def ar_z1(s):
        o = 576 if XFIRST[s] else 384
        for i, k in ((0, 1), (1, 3)):
            r0, n = blk_z(s, k)
            ar[(s, "z1", i)] = xchg(gA(s, r0, n), rA.at[s, o + i * n : o + i * n + n, :], z1)

    def ar_z1add(s):
        o = 576 if XFIRST[s] else 384
        for i, k in ((0, 0), (1, 2)):
            r0, n = blk_z(s, k)
            ar[(s, "z1", i)].wait_recv()
            addto(gA(s, r0, n), rA.at[s, o + i * n : o + i * n + n, :])

    def ar_z2(s):
        o = 672 if XFIRST[s] else 576
        r0, n = blk_z(s, 2)
        ar[(s, "z2")] = xchg(gA(s, r0, n), rA.at[s, o : o + n, :], z2)

    def ar_z2add(s):
        o = 672 if XFIRST[s] else 576
        r0, n = blk_z(s, 0)
        ar[(s, "z2")].wait_recv()
        addto(gA(s, r0, n), rA.at[s, o : o + n, :])

    def ar_begin(s):
        ar[(s, 0)].wait_recv()
        addto(gA(s, cbase, HL), rA.at[s, 0:HL, :])
        (ar_x if XFIRST[s] else ar_z1)(s)

    def ar_step2(s):
        if XFIRST[s]:
            ar_xadd(s)
            ar_z1(s)
        else:
            ar_z1add(s)
            ar_z2(s)

    def ar_step3(s):
        if XFIRST[s]:
            ar_z1add(s)
            ar_z2(s)
        else:
            ar_z2add(s)
            ar_x(s)

    def ar_fin(s):
        (ar_z2add if XFIRST[s] else ar_xadd)(s)

    def fslot(s, r0, n):
        return fS.at[s, pl.ds(r0, n), :]

    def ag_z2(s):
        r0, n = blk_z(s, 0)
        f = fslot(s, r0, n)
        ar[(s, "g2")] = xchg(f, f, z2)
        ar[(s, "g1")] = xchg(f, f, z1)

    def ag_z1(s):
        ar[(s, "g2")].wait_recv()
        r0, n = blk_z(s, 2)
        f = fslot(s, r0, n)
        ar[(s, "g3")] = xchg(f, f, z1)

    def ag_zend(s):
        ar[(s, "g1")].wait_recv()
        ar[(s, "g3")].wait_recv()

    def ag_x(s):
        f = fslot(s, xbase, 192) if XFIRST[s] else fslot(s, spot_of(s), 48)
        ar[(s, "gx")] = xchg(f, f, xp)

    def ag_begin(s):
        r0 = spot_of(s)
        fslot(s, r0, 48)[...] = gA(s, r0, 48)[...]
        (ag_z2 if XFIRST[s] else ag_x)(s)

    def ag_step2(s):
        if XFIRST[s]:
            ag_z1(s)
        else:
            ar[(s, "gx")].wait_recv()
            ag_z2(s)

    def ag_step3(s):
        if XFIRST[s]:
            ag_zend(s)
            ag_x(s)
        else:
            ag_z1(s)

    def ag_core(s):
        if XFIRST[s]:
            ar[(s, "gx")].wait_recv()
        else:
            ag_zend(s)
        f = fslot(s, cbase, HL)
        ar[(s, "gc")] = xchg(f, fA.at[s, pl.ds(cbase, HL), :], core)
        load(f, fA.at[s, pl.ds(cbase, HL), :])

    for s, tt in ((3, t), (4, 1 - t)):
        gp = tn(attF[tt], n2[0:H, :])
        gA(s, 0, HL)[...] = gp[:, 0:HL].astype(BF)
        gA(s, HL, HL)[...] = gp[:, HL:D].astype(BF)
        ar_core(s)
    rs_z1(1, 0)
    rs_z3(0, 0)
    rs_x(1, 1)
    cda[0].wait_recv()
    att_back(1 - t, True)
    rs_z2(1, 0)
    cda[1].wait_recv()
    att_back(1 - t, False)

    flush([cO])
    cdn = []
    for o in (1 - t, t):
        r0 = al(oth + o * BLK, BLK)
        finish_rows(r0)
        rows = pl.ds(al(H + o * BLK, BLK), BLK)
        n2[rows, :] = dn1_rows(r0).astype(BF)
        cdn.append(xchg(n2.at[rows, :], rN.at[pl.ds(al(o * BLK, BLK), BLK), :], yp))
    for s in (3, 4):
        ar_begin(s)
    att_back(t, True)
    for b in range(2):
        finish_rows(al(own + b * BLK, BLK))

    def gw(s, src):
        def body(m, carry):
            rows = pl.ds(al(m * BLK, BLK), BLK)
            gA(s, al(m * BLK, BLK), BLK)[...] = nn(nT[rows, :], src[...]).astype(BF)
            return carry

        lax.fori_loop(0, 3, body, 0)
        ar_core(s)

    rs_z1(0, 1)
    rs_z3(1, 0)
    for s in (3, 4):
        ar_step2(s)
    gw(0, act.at[:, 0:HL])
    gw(1, act.at[:, HL:D])
    ar_begin(0)
    gw(2, dh.at[:, 0:HL])
    ar_begin(1)
    rs_z2(0, 1)
    ar_begin(2)
    for s in (3, 4):
        ar_step3(s)

    vecA[0] = jnp.zeros((16, D), F32)
    for i, row in ((3, sp), (4, s2g), (5, s2b), (6, sd)):
        vecA[0, i : i + 1, :] = row
    vecA[0, pl.ds(8 + 2 * tr[0] + c, 1), :] = bsums[0]
    vecA[0, pl.ds(8 + 2 * tr[1] + c, 1), :] = bsums[1]
    vecA[0, pl.ds(12 + t, 1), 0:HL] = rowsum(act[:, 0:HL].astype(F32))
    vecA[0, pl.ds(12 + t, 1), HL:D] = rowsum(dh[:, 0:HL].astype(F32))
    ar_step2(0)
    ar_step2(1)
    rs_z3(0, 1)
    rs_z1(1, 1)

    stok, s1g, s1b = zrow, zrow, zrow
    cgin = []
    for i, o in enumerate((t, 1 - t)):
        o0 = al(o * BLK, BLK)
        r0 = al(own + o0, BLK)
        rows = pl.ds(r0, BLK)
        orow = pl.ds(o0, BLK)
        cdn[i].wait_recv()
        dnb = dn1_rows(r0) + rN[orow, :].astype(F32)
        m, v = start_rows(r0)
        cent, r = stats(v)
        xhat = cent * r
        dst = mid[orow, :] + norm_back(xhat, r, dnb, ln1g)
        ginS[orow, :] = jnp.where(m, 0.0, dst).astype(BF)
        cgin.append(xchg(ginS.at[orow, :], gin.at[rows, :], yp))
        load(ginS.at[orow, :], gin.at[rows, :])
        stok = stok + rowsum(jnp.where(m, dst, 0.0))
        s1g = s1g + rowsum(dnb * xhat)
        s1b = s1b + rowsum(dnb)
        if i == 0:
            rs_z2(1, 1)
            rs_y(0)
            ar_step2(2)
            ar_step3(0)
            ar_step3(1)
            ar_fin(3)
            ar_fin(4)
            cgp = xchg(gA(4, spot_of(4), 48), rgp, yp)
    for i, row in ((0, stok), (1, s1g), (2, s1b)):
        vecA[0, i : i + 1, :] = row
    cv = xchg(vecA.at[0], vR.at[0], core)
    rs_z3(1, 1)
    ar_step3(2)
    ar_fin(0)
    ag_begin(0)
    ar_fin(1)
    ag_begin(1)
    cv.wait_recv()
    vecA[1] = vecA[0] + vR[0]
    cv = xchg(vecA.at[1], vR.at[1], xp)
    cgp.wait_recv()
    addto(gA(3, spot_of(3), 48), rgp)
    ag_begin(3)
    ar_fin(2)
    ag_begin(2)
    cv.wait_recv()
    vecA[2] = vecA[1] + vR[1]
    cv = xchg(vecA.at[2], vR.at[2], z1)
    rs_y(1)
    for s in (0, 1, 3, 2):
        ag_step2(s)
    cv.wait_recv()
    vecA[3] = vecA[2] + vR[2]
    cv = xchg(vecA.at[3], vR.at[3], z2)
    for s in (0, 1, 3, 2):
        ag_step3(s)
    rs_c(0)
    rs_c(1)
    cv.wait_recv()
    vecA[4] = vecA[3] + vR[3]
    cv = xchg(vecA.at[4], vR.at[4], yp)
    for s in (0, 1, 3, 2):
        ag_core(s)
    rs_end(0)
    rs_end(1)
    for s in (0, 1, 3, 2):
        ar[(s, "gc")].wait_recv()
    cv.wait_recv()
    vout[...] = vecA[4] + vR[4]
    for cp in cmix + cgin:
        cp.wait_recv()
    flush([cp for cp, _ in pending])
    for cp in loads[4:]:
        cp.wait()


def scratch():
    def v(shape, dt):
        return pltpu.VMEM(shape, dt)

    return [
        v((T, D), BF), v((D, T), BF), v((3, T, HL), BF), v((T, HL), BF), v((2, H, HL), BF), v((2, HL, D), BF),
        v((2, D, D), BF), v((2, D, D), BF), v((H, D), F32), v((T, D), BF), v((T, D), BF), v((D, T), BF),
        v((T, D), F32), v((T, D), F32), v((H, D), BF), v((H, D), BF), v((T, D), BF), v((T, D), BF),
        v((2, 2, 4, 96, D), BF), v((2, 2, 4, 96, D), BF),
        v((2, 2, 9, 96, D), BF), v((2, 96, D), BF), v((2, 96, D), BF), v((2, 96, D), BF),
        v((2, 96, D), F32), v((2, 48, D), F32), v((T, HL), BF), v((48, HL), BF), v((5, 720, HL), BF),
        v((8, T), F32), v((2, 8, D), F32), v((5, 16, D), F32), v((5, 16, D), F32),
        v((T, D), BF), v((3, D, HL), BF), v((T, 128), jnp.int32), v((1, T), jnp.int32), v((8, D), F32),
        v((H, D), BF), v((H, D), BF), v((4, D, HL), BF), v((2, 48, 2 * D), F32),
        pltpu.SemaphoreType.DMA((XCH,)), pltpu.SemaphoreType.DMA((XCH,)), pltpu.SemaphoreType.DMA((20,)),
    ]


def finish(mixed, gin, fa, gup, gdn, vs, o_mixed, o_gin, o_tok, o_g1, o_b1, o_qkv, o_bqv, o_proj, o_bp, o_g2, o_b2, o_up,
           o_bup, o_dn, o_bd, gb, gf, fb, ff, pf, sem):
    t = lax.axis_index("tensor")
    count = [0]

    def copy(src, dst):
        cp = pltpu.make_async_copy(src, dst, sem.at[count[0]])
        count[0] += 1
        cp.start()
        return cp

    gc = [copy(gin.at[b * BLK : b * BLK + BLK, :], gb.at[b * BLK : b * BLK + BLK, :]) for b in range(4)]
    fc = [copy(fa.at[s], fb.at[s]) for s in range(4)]
    out = [copy(mixed, o_mixed), copy(gup, o_up), copy(gdn, o_dn)]
    for i, o in enumerate((o_tok, o_g1, o_b1, o_bp, o_g2, o_b2, o_bd)):
        o[...] = vs[i : i + 1, :].reshape(D)
    for i in range(2):
        o_bup[i * D : i * D + D] = vs[pl.ds(8 + 2 * t + i, 1), :].reshape(D)
        o_bqv[i : i + 1, :] = vs[pl.ds(12 + t, 1), i * HL : i * HL + HL]
    for b in range(4):
        gc[b].wait()
        rows = slice(b * BLK, b * BLK + BLK)
        gf[rows, :] = gb[rows, :].astype(F32)
        out.append(copy(gf.at[rows, :], o_gin.at[rows, :]))
    for s in range(4):
        fc[s].wait()
        if s < 3:
            ff[s] = fb[s].astype(F32)
            out.append(copy(ff.at[s], o_qkv.at[s]))
        else:
            pf[:, 0:HL] = fb[3, 0:HL, :].astype(F32)
            pf[:, HL:D] = fb[3, HL:D, :].astype(F32)
            out.append(copy(pf, o_proj))
    for cp in out:
        cp.wait()


def on_device(
    patches, image_ids, valid, mask_pos, mask_token, ln1_gain, ln1_bias, w_qkv, b_qv, w_proj, b_proj,
    ln2_gain, ln2_bias, w_up, b_up, w_down, b_down, cotangent,
):
    vm = pl.BlockSpec(memory_space=pltpu.VMEM)
    hbm = pl.BlockSpec(memory_space=pl.ANY)
    sds = jax.ShapeDtypeStruct
    parts = pl.pallas_call(
        mega,
        out_shape=(
            sds((T, D), BF), sds((T, D), BF), sds((4, D, HL), BF), sds((48, 2 * D), F32), sds((48, 2 * D), F32),
            sds((16, D), F32),
        ),
        in_specs=[hbm if i in (0, 11, 13, 17) else vm for i in range(18)],
        out_specs=(hbm,) * 5 + (vm,),
        scratch_shapes=scratch(),
        compiler_params=pltpu.CompilerParams(collective_id=0, has_side_effects=True, vmem_limit_bytes=66584576),
        name="block",
    )(
        patches, image_ids, valid, mask_pos, mask_token, ln1_gain, ln1_bias, b_proj, ln2_gain, ln2_bias, b_down,
        jnp.transpose(w_qkv, (1, 0, 2)), b_qv, w_proj, w_up, w_down.T, b_up, cotangent,
    )
    row = sds((D,), F32)
    big = {0, 1, 5, 7, 11, 13}
    outs = pl.pallas_call(
        finish,
        out_shape=(
            sds((T, D), BF), sds((T, D), F32), row, row, row, sds((3, D, HL), F32), sds((2, HL), F32), sds((HL, D), F32),
            row, row, row, sds((48, 2 * D), F32), sds((2 * D,), F32), sds((48, 2 * D), F32), row,
        ),
        in_specs=[hbm] * 5 + [vm],
        out_specs=tuple(hbm if i in big else vm for i in range(15)),
        scratch_shapes=[
            pltpu.VMEM((T, D), BF), pltpu.VMEM((T, D), F32), pltpu.VMEM((4, D, HL), BF), pltpu.VMEM((3, D, HL), F32),
            pltpu.VMEM((HL, D), F32), pltpu.SemaphoreType.DMA((20,)),
        ],
        compiler_params=pltpu.CompilerParams(vmem_limit_bytes=40 * 2**20),
        name="finish",
    )(*parts)
    outs = list(outs)
    outs[5] = jnp.transpose(outs[5], (1, 0, 2))
    outs[13] = outs[13].T
    return tuple(outs)


HEAD_DIM = 64


def norm_rows(values, gain, shift):
    mean = jnp.mean(values, axis=-1, keepdims=True)
    cent = values - mean
    var = jnp.mean(cent * cent, axis=-1, keepdims=True)
    return cent * lax.rsqrt(var + EPS) * gain + shift


def left_dot(first, second):
    return lax.dot_general(
        first, second, (((0,), (0,)), ((), ())), preferred_element_type=jnp.float32
    )


def right_dot(first, second):
    return lax.dot_general(
        first, second, (((1,), (1,)), ((), ())), preferred_element_type=jnp.float32
    )


def allowed_rows(ids, live, begin, count):
    rows = ids.shape[0]
    own_ids = lax.dynamic_slice_in_dim(ids, begin, count, 0)
    places = begin + jnp.arange(count)
    same_place = places[:, None] == jnp.arange(rows)[None, :]
    return (own_ids[:, None] == ids[None, :]) & ((live[None, :] == 1) | same_place)


def spread(
    patches,
    image_ids,
    valid,
    mask_pos,
    mask_token,
    ln1_gain,
    ln1_bias,
    w_qkv,
    b_qv,
    w_proj,
    b_proj,
    ln2_gain,
    ln2_bias,
    w_up,
    b_up,
    w_down,
    b_down,
    cotangent,
):
    rows = patches.shape[0]
    local_width = w_qkv.shape[2]
    local_heads = local_width // HEAD_DIM
    scale = 1.0 / HEAD_DIM**0.5
    ids = image_ids[0]
    live = valid[0]
    masked = mask_pos[0][:, None] == 1
    block = min(512, rows)
    blocks = rows // block
    start = jnp.where(masked, mask_token.astype(jnp.float32)[None, :], patches.astype(jnp.float32))
    normed, norm1_pull = jax.vjp(
        norm_rows, start, ln1_gain.astype(jnp.float32), ln1_bias.astype(jnp.float32)
    )
    normed_b = normed.astype(jnp.bfloat16)
    qv_bias = b_qv.astype(jnp.float32)
    bias = jnp.stack([qv_bias[0], jnp.zeros_like(qv_bias[0]), qv_bias[1]])
    qkv = jnp.einsum("td,dsc->tsc", normed_b, w_qkv, preferred_element_type=jnp.float32)
    qkv_b = (qkv + bias[None]).astype(jnp.bfloat16)
    query = qkv_b[:, 0].reshape(rows, local_heads, HEAD_DIM)
    keys = qkv_b[:, 1].reshape(rows, local_heads, HEAD_DIM)
    values = qkv_b[:, 2].reshape(rows, local_heads, HEAD_DIM)
    outputs = []
    totals = []
    for index in range(blocks):
        begin = index * block
        query_part = query[begin : begin + block]
        allowed = allowed_rows(ids, live, begin, block)
        scores = (
            jnp.einsum("qhc,khc->hqk", query_part, keys, preferred_element_type=jnp.float32) * scale
        )
        scores = jnp.where(allowed[None], scores, -1e30)
        top = jnp.max(scores, axis=-1, keepdims=True)
        expd = jnp.exp(scores - top)
        summed = jnp.sum(expd, axis=-1, keepdims=True)
        probs_b = (expd / summed).astype(jnp.bfloat16)
        totals.append(top + jnp.log(summed))
        outputs.append(
            jnp.einsum("hqk,khc->qhc", probs_b, values, preferred_element_type=jnp.float32)
        )
    attended_b = jnp.concatenate(outputs, axis=0).reshape(rows, local_width).astype(jnp.bfloat16)
    attn_part = jnp.dot(attended_b, w_proj, preferred_element_type=jnp.float32)
    ln2_gain_f = ln2_gain.astype(jnp.float32)
    ln2_bias_f = ln2_bias.astype(jnp.float32)
    attn_total = lax.psum(attn_part, "tensor")
    middle = start + attn_total + b_proj.astype(jnp.float32)
    normed2, norm2_pull = jax.vjp(norm_rows, middle, ln2_gain_f, ln2_bias_f)
    normed2_b = normed2.astype(jnp.bfloat16)
    up_full, down_full = (
        lax.all_gather(w_up, "dp", axis=0, tiled=True),
        lax.all_gather(w_down, "dp", axis=1, tiled=True),
    )
    hidden = jnp.dot(normed2_b, up_full, preferred_element_type=jnp.float32) + b_up.astype(
        jnp.float32
    )
    active, gelu_pull = jax.vjp(partial(jax.nn.gelu, approximate=False), hidden)
    active_b = active.astype(jnp.bfloat16)
    mlp_part = jnp.dot(active_b, down_full, preferred_element_type=jnp.float32)
    mlp_total = lax.psum(mlp_part.astype(jnp.bfloat16), "tensor").astype(jnp.float32)
    mixed = (middle + mlp_total + b_down.astype(jnp.float32)).astype(jnp.bfloat16)
    seed_grad = cotangent.astype(jnp.float32)
    up_back, down_back = (up_full, down_full)
    grad_b_down = jnp.sum(seed_grad, axis=0)
    grad_down_local = left_dot(active_b, cotangent)
    grad_active = right_dot(cotangent, down_back)
    (grad_hidden,) = gelu_pull(grad_active)
    grad_hidden_b = grad_hidden.astype(jnp.bfloat16)
    grad_b_up = jnp.sum(grad_hidden_b.astype(jnp.float32), axis=0)
    grad_up_local = left_dot(normed2_b, grad_hidden_b)
    grad_normed2_part = right_dot(grad_hidden_b, up_back)
    grad_normed2 = lax.psum(grad_normed2_part, "tensor")
    grad_mid_norm, grad_ln2_gain, grad_ln2_bias = norm2_pull(grad_normed2)
    grad_middle = seed_grad + grad_mid_norm
    grad_w_up, grad_w_down = (
        lax.psum_scatter(grad_up_local, "dp", scatter_dimension=0, tiled=True),
        lax.psum_scatter(grad_down_local, "dp", scatter_dimension=1, tiled=True),
    )
    grad_branch_b = grad_middle.astype(jnp.bfloat16)
    grad_b_proj = jnp.sum(grad_branch_b.astype(jnp.float32), axis=0)
    grad_w_proj = left_dot(attended_b, grad_branch_b)
    grad_attended = (
        right_dot(grad_branch_b, w_proj).astype(jnp.bfloat16).reshape(rows, local_heads, HEAD_DIM)
    )
    grad_query_parts = []
    grad_keys = jnp.zeros((rows, local_heads, HEAD_DIM), jnp.float32)
    grad_values = jnp.zeros((rows, local_heads, HEAD_DIM), jnp.float32)
    for index in range(blocks):
        begin = index * block
        query_part = query[begin : begin + block]
        grad_out_part = grad_attended[begin : begin + block]
        allowed = allowed_rows(ids, live, begin, block)
        scores = (
            jnp.einsum("qhc,khc->hqk", query_part, keys, preferred_element_type=jnp.float32) * scale
        )
        scores = jnp.where(allowed[None], scores, -1e30)
        probs = jnp.exp(scores - totals[index])
        probs_b = probs.astype(jnp.bfloat16)
        grad_values = grad_values + jnp.einsum(
            "hqk,qhc->khc", probs_b, grad_out_part, preferred_element_type=jnp.float32
        )
        grad_probs = jnp.einsum(
            "qhc,khc->hqk", grad_out_part, values, preferred_element_type=jnp.float32
        )
        inner = jnp.sum(probs * grad_probs, axis=-1, keepdims=True)
        grad_scores_b = (probs * (grad_probs - inner)).astype(jnp.bfloat16)
        grad_query_parts.append(
            jnp.einsum("hqk,khc->qhc", grad_scores_b, keys, preferred_element_type=jnp.float32)
            * scale
        )
        grad_keys = (
            grad_keys
            + jnp.einsum(
                "hqk,qhc->khc", grad_scores_b, query_part, preferred_element_type=jnp.float32
            )
            * scale
        )
    grad_query = jnp.concatenate(grad_query_parts, axis=0)
    grad_qkv_b = (
        jnp.stack([grad_query, grad_keys, grad_values], axis=1)
        .reshape(rows, 3, local_width)
        .astype(jnp.bfloat16)
    )
    grad_qkv_f = grad_qkv_b.astype(jnp.float32)
    grad_b_qv = jnp.stack([jnp.sum(grad_qkv_f[:, 0], axis=0), jnp.sum(grad_qkv_f[:, 2], axis=0)])
    grad_w_qkv = jnp.einsum("td,tsc->dsc", normed_b, grad_qkv_b, preferred_element_type=jnp.float32)
    grad_normed_part = jnp.einsum(
        "tsc,dsc->td", grad_qkv_b, w_qkv, preferred_element_type=jnp.float32
    )
    grad_normed = lax.psum(grad_normed_part.astype(jnp.bfloat16), "tensor").astype(jnp.float32)
    grad_start_norm, grad_ln1_gain, grad_ln1_bias = norm1_pull(grad_normed)
    grad_start = grad_middle + grad_start_norm
    grad_input = jnp.where(masked, 0.0, grad_start)
    grad_token = jnp.sum(jnp.where(masked, grad_start, 0.0), axis=0)
    summed = lax.psum(
        (
            grad_token,
            grad_ln1_gain,
            grad_ln1_bias,
            grad_w_qkv,
            grad_b_qv,
            grad_w_proj,
            grad_b_proj,
            grad_ln2_gain,
            grad_ln2_bias,
            grad_b_up,
            grad_b_down,
        ),
        "dp",
    )
    return (
        mixed,
        grad_input,
        summed[0],
        summed[1],
        summed[2],
        summed[3],
        summed[4],
        summed[5],
        summed[6],
        summed[7],
        summed[8],
        grad_w_up,
        summed[9],
        grad_w_down,
        summed[10],
    )


def solution(mesh):
    placed = (
        P("dp", None),
        P("dp", None),
        P("dp", None),
        P("dp", None),
        P(),
        P(),
        P(),
        P(None, None, "tensor"),
        P(None, "tensor"),
        P("tensor", None),
        P(),
        P(),
        P(),
        P("dp", "tensor"),
        P("tensor"),
        P("tensor", "dp"),
        P(),
        P("dp", None),
    )
    fits = mesh.shape["dp"] == 16 and mesh.shape["tensor"] == 2
    return jax.shard_map(
        on_device if fits else spread,
        mesh=mesh,
        in_specs=placed,
        out_specs=(
            P("dp", None),
            P("dp", None),
            P(),
            P(),
            P(),
            P(None, None, "tensor"),
            P(None, "tensor"),
            P("tensor", None),
            P(),
            P(),
            P(),
            P("dp", "tensor"),
            P("tensor"),
            P("tensor", "dp"),
            P(),
        ),
        check_vma=False,
    )
```

```python
from functools import partial

import jax
import jax.numpy as jnp
from jax import lax
from jax.experimental import pallas as pl
from jax.experimental.pallas import tpu as pltpu
from jax.sharding import PartitionSpec as P

BF = jnp.bfloat16
F32 = jnp.float32
MESH = pl.DeviceIdType.MESH
EPS = 1e-06
T = 1024
H = 512
D = 768
HL = 384
BLK = 256
WIN = 768
XCH = 240


def nn(a, b):
    return lax.dot_general(a, b, (((1,), (0,)), ((), ())), preferred_element_type=F32)


def nt(a, b):
    return lax.dot_general(a, b, (((1,), (1,)), ((), ())), preferred_element_type=F32)


def tn(a, b):
    return lax.dot_general(a, b, (((0,), (0,)), ((), ())), preferred_element_type=F32)


def rowsum(v):
    return jnp.sum(v, axis=0, keepdims=True)


def lane_half(shape):
    return lax.broadcasted_iota(jnp.int32, shape, 1) < 64


def stats(v):
    mean = jnp.sum(v, axis=-1, keepdims=True) * (1.0 / D)
    cent = v - mean
    var = jnp.sum(cent * cent, axis=-1, keepdims=True) * (1.0 / D)
    return cent, lax.rsqrt(var + EPS)


def norm_back(xhat, r, d, gain):
    e = d * gain
    m1 = jnp.sum(e, axis=-1, keepdims=True) * (1.0 / D)
    m2 = jnp.sum(e * xhat, axis=-1, keepdims=True) * (1.0 / D)
    return r * (e - m1 - xhat * m2)


def mega(
    patches, ids, live, hidden_pos, token_b, ln1g_b, ln1b_b, bproj_b, ln2g_b, ln2b_b, bdown_b, wqkv_h, bqv_b, wproj,
    up, dn, bup, cot,
    mixed, gin, fA, gup, gdn, vout,
    n1, nT, qkv, attO, attF, wpf, Wu, Wd, mid, n2, dml, dmlT, outA, dn2A, rO, rN, act, dh, gU, gD,
    rG, rX, sy, ry, sc, rc, dO, rgp, rA, lseT, bupA, vecA, vR, pat, wqkv, codec, coder, vec, mixS, ginS, fS,
    gS, ssem, rsem, lsem,
):
    d = lax.axis_index("dp")
    t = lax.axis_index("tensor")
    z = lax.div(d, 4)
    x = lax.rem(lax.div(d, 2), 2)
    c = lax.rem(d, 2)
    zk = (z, z + 1 - 2 * lax.rem(z, 2), lax.rem(z + 2, 4), 3 - z)
    xr = (x, 1 - x)
    tr = (t, 1 - t)

    def dev(zz, xx, cc, tt):
        return ((zz * 2 + xx) * 2 + cc, tt)

    core = dev(z, x, 1 - c, t)
    xp = dev(z, 1 - x, c, t)
    yp = dev(z, x, c, 1 - t)
    z1 = dev(zk[1], x, c, t)
    z2 = dev(zk[2], x, c, t)
    z3 = dev(zk[3], x, c, t)
    mid_z = (z == 1) | (z == 2)
    end_z = (z == 0) | (z == 3)

    pending = []
    flushed = set()
    slots = [0]

    def slot():
        slots[0] += 1
        return slots[0] - 1

    def xchg(src, dst, to, when=None, land=None):
        i = len(pending)
        cp = pltpu.make_async_remote_copy(
            src_ref=src, dst_ref=dst, send_sem=ssem.at[i], recv_sem=rsem.at[slot() if land is None else land],
            device_id=to, device_id_type=MESH,
        )
        pending.append((cp, when))
        if when is None:
            cp.start()
        else:
            pl.when(when)(cp.start)
        return cp

    def landed(dst, land, frm):
        pltpu.make_async_remote_copy(
            src_ref=dst, dst_ref=dst, send_sem=ssem.at[0], recv_sem=rsem.at[land], device_id=frm, device_id_type=MESH
        ).wait_recv()

    def flush(cps):
        cps = set(id(cp) for cp in cps)
        for cp, when in pending:
            if id(cp) in cps and id(cp) not in flushed:
                flushed.add(id(cp))
                if when is None:
                    cp.wait_send()
                else:
                    pl.when(when)(cp.wait_send)

    def al(v, m):
        return pl.multiple_of(v, m)

    bar = pltpu.get_barrier_semaphore()
    peers = (core, xp, yp, z1, z2, z3)
    for p in peers:
        pl.semaphore_signal(bar, inc=1, device_id=p, device_id_type=MESH)
    loads = []

    def load(src, dst):
        cp = pltpu.make_async_copy(src, dst, lsem.at[len(loads)])
        cp.start()
        loads.append(cp)
        return cp

    lpat = load(patches, pat)
    lwq = load(wqkv_h, wqkv)
    code = ids[...] + 16 * live[...] + 32 * hidden_pos[...]
    coder[...] = code
    codec[...] = jnp.broadcast_to(code.astype(F32), (128, T)).T.astype(jnp.int32)
    for i, row in enumerate((token_b, ln1g_b, ln1b_b, bproj_b, ln2g_b, ln2b_b, bdown_b)):
        vec[i : i + 1, :] = row[...].astype(F32).reshape(1, D)
    bqv = bqv_b[...].astype(F32)
    bupA[0] = jnp.zeros((8, D), F32)
    for i in range(2):
        bupA[0, i : i + 1, :] = bup[i * D : i * D + D].astype(F32).reshape(1, D)
    pl.semaphore_wait(bar, len(peers))

    own = al(t * H, H)
    oth = al((1 - t) * H, H)
    cslot = al(c * H, H)
    sslot = al((1 - c) * H, H)
    W = (Wu, Wd)
    shards = (up, dn)

    def wblk(a, k, xx, yy):
        return W[a].at[tr[yy], pl.ds(al((zk[k] * 2 + xr[xx]) * 96, 32), 96), :]

    ccp = []
    mine = al((z * 2 + x) * 96 + c * 48, 16)
    for a in (0, 1):
        ccp.append(
            xchg(shards[a].at[:, pl.ds(al((1 - c) * D, 128), D)], W[a].at[t, pl.ds(mine, 48), :], core)
        )
    whalf = pl.ds(al(c * 192, 64), 192)
    cwp = xchg(wproj.at[whalf, :], wpf.at[t, whalf, :], yp)
    cbup = xchg(bupA.at[0], bupA.at[1], yp)
    cdml = xchg(cot.at[pl.ds(own, H), :], dml.at[pl.ds(cslot, H), :], core)
    ldml = load(cot.at[pl.ds(own, H), :], dml.at[pl.ds(cslot, H), :])
    lwp = load(wproj, wpf.at[t])
    for a in (0, 1):
        W[a][t, pl.ds(mine, 48), :] = shards[a][:, pl.ds(al(c * D, 128), D)]

    zc, xc, yc = {}, {}, {}

    zsent = []
    zland = {(a, k, yy): slot() for a in (0, 1) for k in (1, 2, 3) for yy in (0, 1)}

    def zpass(a, k, yy, to, as_k, when):
        zsent.append(xchg(wblk(a, k, 0, yy), wblk(a, k, 0, yy), to, when, zland[(a, as_k, yy)]))

    def zwait(a, k, yy):
        landed(wblk(a, k, 0, yy), zland[(a, k, yy)], z1)

    def zstart(a, yy):
        zpass(a, 0, yy, z1, 1, None)
        zpass(a, 0, yy, z3, 3, mid_z)

    def zstep1(a, yy):
        zwait(a, 1, yy)
        zpass(a, 1, yy, z3, 2, mid_z)
        pl.when(mid_z)(partial(zwait, a, 3, yy))
        zpass(a, 3, yy, z1, 2, mid_z)

    def zstep2(a, yy):
        zwait(a, 2, yy)
        zpass(a, 2, yy, z1, 3, mid_z)

    def zstep3(a, yy):
        pl.when(end_z)(partial(zwait, a, 3, yy))

    def xsend(a, k, yy):
        xc[(a, k, yy)] = xchg(wblk(a, k, 0, yy), wblk(a, k, 0, yy), xp)

    def ysend(a, k, xx):
        yc[(a, k, xx)] = xchg(wblk(a, k, xx, 0), wblk(a, k, xx, 0), yp)

    token = vec[0:1, :]
    ln1g = vec[1:2, :]
    ln1b = vec[2:3, :]

    def start_rows(r0):
        m = lax.shift_right_logical(codec[pl.ds(r0, BLK), 0:1], 5) == 1
        return m, jnp.where(m, token, pat[pl.ds(r0, BLK), :].astype(F32))

    def ln1_block(b, carry):
        r0 = al(b * BLK, BLK)
        _, v = start_rows(r0)
        cent, r = stats(v)
        nb = (cent * r * ln1g + ln1b).astype(BF)
        n1[pl.ds(r0, BLK), :] = nb
        for s in range(3):
            y = nn(nb, wqkv[s])
            if s == 0:
                y = y + bqv[0:1, :]
            if s == 2:
                y = y + bqv[1:2, :]
            qkv[s, pl.ds(r0, BLK), :] = y.astype(BF)
        return carry

    lpat.wait()
    lwq.wait()
    lax.fori_loop(0, 1, ln1_block, 0)
    for a in (0, 1):
        ccp[a].wait_recv()
    zstart(0, 0)
    zstart(1, 0)
    xsend(0, 0, 0)
    xsend(1, 0, 0)
    ysend(1, 0, 0)
    lax.fori_loop(1, 4, ln1_block, 0)
    for a in (0, 1):
        zstep1(a, 0)
        xsend(a, 1, 0)

    def masked_pair(block, scale=None):
        low = lane_half(block.shape)
        zero = jnp.zeros_like(block)
        if scale is not None:
            block = block * jnp.asarray(scale, BF)
        return jnp.where(low, block, zero), jnp.where(low, zero, block)

    def att_block(half, edge):
        qb = half * 3 if edge else 1 + half
        win = H if edge else WIN
        r0 = al(qb * BLK, BLK)
        ws = al(half * H if edge else half * BLK, BLK)
        cr = codec[pl.ds(r0, BLK), 0:1]
        cw = coder[:, pl.ds(ws, win)]
        rid = r0 + lax.broadcasted_iota(jnp.int32, (BLK, win), 0)
        cid = ws + lax.broadcasted_iota(jnp.int32, (BLK, win), 1)
        ok = ((cr & 15) == (cw & 15)) & (((cw & 16) == 16) | (rid == cid))
        dn2A[0:BLK, 0:win] = jnp.where(ok, 0.0, -1e30)
        lane = lax.broadcasted_iota(jnp.int32, (BLK, 128), 1)

        def pair(p, lacc):
            cols = pl.ds(al(p * 128, 128), 128)
            qs = masked_pair(qkv[0, pl.ds(r0, BLK), cols], 0.125)
            kp = qkv[1, pl.ds(ws, win), cols]
            vp = qkv[2, pl.ds(ws, win), cols]
            outs = []
            for h in range(2):
                s = nt(qs[h], kp) + dn2A[0:BLK, 0:win]
                top = jnp.max(s, axis=-1, keepdims=True)
                e = jnp.exp(s - top)
                l = jnp.sum(e, axis=-1, keepdims=True)
                o = nn(e.astype(BF), vp) * (1.0 / l)
                outs.append(o)
                lacc = jnp.where(lane == (2 * p + h), top + jnp.log(l), lacc)
            attO[pl.ds(r0, BLK), cols] = jnp.where(lane_half((BLK, 128)), outs[0], outs[1]).astype(BF)
            return lacc

        lacc = lax.fori_loop(0, 3, pair, jnp.zeros((BLK, 128), F32))
        lseT[:, pl.ds(r0, BLK)] = lacc.T[0:8, :]
        return r0

    catt = []

    def att_send(r0):
        catt.append(xchg(attO.at[pl.ds(r0, BLK), :], attF.at[t, pl.ds(al(r0 - oth, BLK), BLK), :], yp))

    att_send(att_block(1 - t, True))
    att_send(att_block(1 - t, False))
    for a in (0, 1):
        zstep2(a, 0)
        xsend(a, 2, 0)
    ysend(0, 0, 0)
    ysend(0, 1, 0)
    ysend(0, 2, 0)
    cwp.wait_recv()
    cwc = xchg(wpf.at[1 - t, whalf, :], wpf.at[1 - t, whalf, :], core)
    att_block(t, True)
    att_block(t, False)
    attF[t] = attO[pl.ds(own, H), :]
    for a in (0, 1):
        zstep3(a, 0)
        xsend(a, 3, 0)
    ysend(0, 3, 0)
    yc[(1, 0, 0)].wait_recv()
    zstart(1, 1)
    xsend(1, 0, 1)

    bproj = vec[3:4, :]
    ln2g = vec[4:5, :]
    ln2b = vec[5:6, :]
    bdown = vec[6:7, :]
    ldml.wait()
    lwp.wait()
    for cp in catt:
        cp.wait_recv()
    cwc.wait_recv()

    def mid_block(b, carry):
        o0 = al(b * BLK, BLK)
        _, v = start_rows(al(own + o0, BLK))
        m = v + (nn(attF[0, pl.ds(o0, BLK), :], wpf[0]) + nn(attF[1, pl.ds(o0, BLK), :], wpf[1])) + bproj
        mid[pl.ds(o0, BLK), :] = m
        cent, r = stats(m)
        n2[pl.ds(al(cslot + o0, BLK), BLK), :] = (cent * r * ln2g + ln2b).astype(BF)
        return carry

    lax.fori_loop(0, 2, mid_block, 0)
    cn2 = xchg(n2.at[pl.ds(cslot, H), :], n2.at[pl.ds(cslot, H), :], core)
    cdml.wait_recv()
    cn2.wait_recv()
    nT[...] = n2[...].T
    dmlT[...] = dml[...].T
    cbup.wait_recv()
    for k in range(4):
        xc[(0, k, 0)].wait_recv()
        ysend(0, k, 1)
    for k in range(4):
        xc[(1, k, 0)].wait_recv()
    zstep1(1, 1)
    xsend(1, 1, 1)

    G = (gU, gD)
    rs = {}

    def addto(dst, src):
        dst[...] = (dst[...].astype(F32) + src[...].astype(F32)).astype(BF)

    def rs_x(a, j):
        rs[(a, j)] = [xchg(G[a].at[j, 1, h * 2 : h * 2 + 2], rG.at[a, j, h * 2 : h * 2 + 2], xp) for h in (0, 1)]

    rland = {(a, j, q): slot() for a in (0, 1) for j in (0, 1) for q in range(4, 9)}

    def rpass(a, j, k, to, q, when):
        xchg(G[a].at[j, 0, zk[k]], rG.at[a, j, q], to, when, rland[(a, j, q)])

    def radd(a, j, k, q):
        landed(rG.at[a, j, q], rland[(a, j, q)], z1)
        addto(G[a].at[j, 0, zk[k]], rG.at[a, j, q])

    def rs_z1(a, j):
        for cp in rs[(a, j)]:
            cp.wait_recv()
        for zz in range(4):
            addto(G[a].at[j, 0, zz], rG.at[a, j, zz])
        for k, q in ((3, 4), (2, 5), (1, 6)):
            rpass(a, j, k, z1, q, end_z)

    def rs_z2(a, j):
        pl.when(mid_z)(partial(radd, a, j, 2, 4))
        rpass(a, j, 2, z3, 7, mid_z)
        pl.when(mid_z)(partial(radd, a, j, 3, 5))
        rpass(a, j, 3, z3, 8, mid_z)

    def rs_z3(a, j):
        pl.when(mid_z)(partial(radd, a, j, 1, 7))
        rpass(a, j, 1, z1, 8, mid_z)

    def rs_sum(a, j):
        pl.when(mid_z)(partial(radd, a, j, 0, 6))
        landed(rG.at[a, j, 8], rland[(a, j, 8)], z1)
        return G[a][j, 0, z].astype(F32) + rG[a, j, 8].astype(F32)

    def rs_y(a):
        sy[a] = rs_sum(a, 1).astype(BF)
        rs[(a, "y")] = xchg(sy.at[a], ry.at[a], yp)

    def rs_c(a):
        total = rs_sum(a, 0)
        rs[(a, "y")].wait_recv()
        sc[a] = total + ry[a].astype(F32)
        rs[(a, "c")] = xchg(sc.at[a, pl.ds(al((1 - c) * 48, 16), 48), :], rc.at[a], core)

    def rs_end(a):
        gS[a, :, pl.ds(al(c * D, 128), D)] = sc[a, pl.ds(al(c * 48, 16), 48), :]
        rs[(a, "c")].wait_recv()
        gS[a, :, pl.ds(al((1 - c) * D, 128), D)] = rc[a]
        load(gS.at[a], (gup, gdn)[a])

    bsums = []

    def ff_fwd(j, lo, hi):
        yy = tr[j]
        bu = bupA[j, pl.ds(c, 1), :]

        def block(b, carry):
            rows = pl.ds(al(b * BLK, BLK), BLK)
            hid = nn(n2[rows, :], Wu[yy]) + bu
            phi = 0.5 * (1.0 + lax.erf(hid * 0.7071067811865476))
            a = (hid * phi).astype(BF)
            act[rows, :] = a
            dh[rows, :] = (phi + hid * (jnp.exp(hid * hid * -0.5) * 0.3989422804014327)).astype(BF)
            o = nt(a, Wd[yy])
            if j == 0:
                outA[rows, :] = o
            else:
                outA[rows, :] += o
            return carry

        lax.fori_loop(lo, hi, block, 0)

    def ff_bwd(j, lo, hi, start):
        yy = tr[j]

        def block(b, carry):
            rows = pl.ds(al(b * BLK, BLK), BLK)
            dhid = (nn(dml[rows, :], Wd[yy]) * dh[rows, :].astype(F32)).astype(BF)
            dh[rows, :] = dhid
            g = nt(dhid, Wu[yy])
            if j == 0:
                dn2A[rows, :] = g
            else:
                dn2A[rows, :] += g
            return carry + rowsum(dhid.astype(F32))

        return lax.fori_loop(lo, hi, block, start)

    def ff_grads(j):
        def gw_block(b, carry):
            rows = pl.ds(al(b * 192, 64), 192)
            ru = nn(nT[rows, :], dh[...]).astype(BF)
            rd = nn(dmlT[rows, :], act[...]).astype(BF)
            for xa in range(2):
                rel = lax.rem(xa + x, 2)
                gU[j, rel, b] = ru[xa * 96 : xa * 96 + 96]
                gD[j, rel, b] = rd[xa * 96 : xa * 96 + 96]
            return carry

        lax.fori_loop(0, 4, gw_block, 0)

    zrow = jnp.zeros((1, D), F32)
    ff_fwd(0, 0, 4)
    zstep2(1, 1)
    xsend(1, 2, 1)
    bsums.append(ff_bwd(0, 0, 4, zrow))
    zstep3(1, 1)
    xsend(1, 3, 1)
    ff_grads(0)
    rs_x(0, 0)
    rs_x(1, 0)
    for k in range(4):
        yc[(0, k, 0)].wait_recv()
        yc[(0, k, 1)].wait_recv()
        xc[(1, k, 1)].wait_recv()
    ff_fwd(1, 0, 4)

    flush([cn2])
    n2[H:T, :] = outA[pl.ds(sslot, H), :].astype(BF)
    cO = xchg(n2.at[H:T, :], rO, core)
    bsums.append(ff_bwd(1, 0, 4, zrow))
    n2[0:H, :] = dn2A[pl.ds(sslot, H), :].astype(BF)
    cN = xchg(n2.at[0:H, :], rN, core)

    cO.wait_recv()
    cmix = []

    def mixed_block(o):
        o0 = al(o * BLK, BLK)
        rows = pl.ds(o0, BLK)
        crow = pl.ds(al(cslot + o0, BLK), BLK)
        out = mid[rows, :] + (outA[crow, :] + rO[rows, :].astype(F32)) + bdown
        mixS[rows, :] = out.astype(BF)

    def mixed_send(o):
        orow = pl.ds(al(own + o * BLK, BLK), BLK)
        rows = pl.ds(al(o * BLK, BLK), BLK)
        cmix.append(xchg(mixS.at[rows, :], mixed.at[orow, :], yp))
        load(mixS.at[rows, :], mixed.at[orow, :])

    mixed_block(0)
    mixed_send(0)
    mixed_block(1)
    ff_grads(1)
    rs_x(0, 1)
    rs_z1(0, 0)
    flush(catt)
    cN.wait_recv()
    flush([cN])

    sums = [zrow, zrow, zrow, zrow]
    cda = []
    for o in (t, 1 - t):
        o0 = al(o * BLK, BLK)
        rows = pl.ds(o0, BLK)
        crow = pl.ds(al(cslot + o0, BLK), BLK)
        dnb = dn2A[crow, :] + rN[rows, :].astype(F32)
        cent, r = stats(mid[rows, :])
        xhat = cent * r
        ct = dml[crow, :].astype(F32)
        dm = ct + norm_back(xhat, r, dnb, ln2g)
        db = dm.astype(BF)
        n2[rows, :] = db
        attO[rows, :] = nt(db, wpf[1 - t]).astype(BF)
        orow = pl.ds(al(own + o0, BLK), BLK)
        cda.append(xchg(attO.at[rows, :], dO.at[orow, :], yp))
        dO[orow, :] = nt(db, wpf[t]).astype(BF)
        mid[rows, :] = dm
        for i, term in enumerate((dnb * xhat, dnb, db.astype(F32), ct)):
            sums[i] = sums[i] + rowsum(term)
    s2g, s2b, sp, sd = sums

    mixed_send(1)
    rs_z2(0, 0)
    outA[...] = jnp.zeros((T, D), F32)
    nT[...] = n1[...].T

    def att_back(half, edge):
        qb = half * 3 if edge else 1 + half
        wl = H if edge else WIN
        r0 = al(qb * BLK, BLK)
        ws = al(half * H if edge else half * BLK, BLK)
        cw = codec[pl.ds(ws, wl), 0:1]
        cr = coder[:, pl.ds(r0, BLK)]
        rid = r0 + lax.broadcasted_iota(jnp.int32, (wl, BLK), 1)
        cid = ws + lax.broadcasted_iota(jnp.int32, (wl, BLK), 0)
        ok = ((cr & 15) == (cw & 15)) & (((cw & 16) == 16) | (rid == cid))
        dn2A[0:wl, 0:BLK] = jnp.where(ok, 0.0, -1e30)
        rows = pl.ds(r0, BLK)
        win = pl.ds(ws, wl)

        def pair(p, carry):
            cols = pl.ds(al(p * 128, 128), 128)
            vcols = pl.ds(al(HL + p * 128, 128), 128)
            qp = qkv[0, rows, cols]
            op = dO[rows, cols]
            qs = masked_pair(qp, 0.125)
            os = masked_pair(op)
            kp = qkv[1, win, cols]
            vp = qkv[2, win, cols]
            dqs, dks, dvs = [], [], []
            for h in range(2):
                lse = lseT[pl.ds(2 * p + h, 1), rows]
                pr = jnp.exp(nt(kp, qs[h]) + dn2A[0:wl, 0:BLK] - lse)
                dp = nt(vp, os[h])
                inner = rowsum(pr * dp)
                ds = (pr * (dp - inner)).astype(BF)
                dvs.append(nn(pr.astype(BF), op))
                dks.append(nn(ds, qp))
                dqs.append(tn(ds, kp))
            low = lane_half((BLK, 128))
            lowk = lane_half((wl, 128))
            act[rows, cols] = (jnp.where(low, dqs[0], dqs[1]) * 0.125).astype(BF)
            outA[win, cols] += jnp.where(lowk, dks[0], dks[1])
            outA[win, vcols] += jnp.where(lowk, dvs[0], dvs[1])
            return carry

        lax.fori_loop(0, 3, pair, 0)

    def finish_rows(r0):
        rows = pl.ds(r0, BLK)
        act[rows, HL:D] = (outA[rows, 0:HL] * 0.125).astype(BF)
        dh[rows, 0:HL] = outA[rows, HL:D].astype(BF)

    def dn1_rows(r0):
        rows = pl.ds(r0, BLK)
        return nt(act[rows, 0:HL], wqkv[0]) + nt(act[rows, HL:D], wqkv[1]) + nt(dh[rows, 0:HL], wqkv[2])

    att_back(t, False)

    flush(ccp)
    flush(zsent)
    for q in (xc, yc):
        flush(q.values())
    ar = {}

    def gA(s, r0, n):
        if s == 4:
            return Wd.at[0, pl.ds(r0, n), 0:HL]
        return Wu.at[s // 2, pl.ds(r0, n), (s % 2) * HL : (s % 2) * HL + HL]

    cbase = al(c * HL, 128)
    xbase = al(c * HL + x * 192, 64)
    XFIRST = (True, False, True, False, False)

    def blk_z(s, k):
        if XFIRST[s]:
            return al(xbase + zk[k] * 48, 16), 48
        return al(cbase + zk[k] * 96, 32), 96

    def spot_of(s):
        if XFIRST[s]:
            return al(xbase + z * 48, 16)
        return al(cbase + z * 96 + x * 48, 16)

    def ar_core(s):
        ar[(s, 0)] = xchg(gA(s, al((1 - c) * HL, 128), HL), rA.at[s, 0:HL, :], core)

    def ar_x(s):
        if XFIRST[s]:
            ar[(s, "x")] = xchg(gA(s, al(c * HL + (1 - x) * 192, 64), 192), rA.at[s, 384:576, :], xp)
        else:
            ar[(s, "x")] = xchg(gA(s, al(cbase + z * 96 + (1 - x) * 48, 16), 48), rA.at[s, 672:720, :], xp)

    def ar_xadd(s):
        ar[(s, "x")].wait_recv()
        if XFIRST[s]:
            addto(gA(s, xbase, 192), rA.at[s, 384:576, :])
        else:
            addto(gA(s, spot_of(s), 48), rA.at[s, 672:720, :])

    def ar_z1(s):
        o = 576 if XFIRST[s] else 384
        for i, k in ((0, 1), (1, 3)):
            r0, n = blk_z(s, k)
            ar[(s, "z1", i)] = xchg(gA(s, r0, n), rA.at[s, o + i * n : o + i * n + n, :], z1)

    def ar_z1add(s):
        o = 576 if XFIRST[s] else 384
        for i, k in ((0, 0), (1, 2)):
            r0, n = blk_z(s, k)
            ar[(s, "z1", i)].wait_recv()
            addto(gA(s, r0, n), rA.at[s, o + i * n : o + i * n + n, :])

    def ar_z2(s):
        o = 672 if XFIRST[s] else 576
        r0, n = blk_z(s, 2)
        ar[(s, "z2")] = xchg(gA(s, r0, n), rA.at[s, o : o + n, :], z2)

    def ar_z2add(s):
        o = 672 if XFIRST[s] else 576
        r0, n = blk_z(s, 0)
        ar[(s, "z2")].wait_recv()
        addto(gA(s, r0, n), rA.at[s, o : o + n, :])

    def ar_begin(s):
        ar[(s, 0)].wait_recv()
        addto(gA(s, cbase, HL), rA.at[s, 0:HL, :])
        (ar_x if XFIRST[s] else ar_z1)(s)

    def ar_step2(s):
        if XFIRST[s]:
            ar_xadd(s)
            ar_z1(s)
        else:
            ar_z1add(s)
            ar_z2(s)

    def ar_step3(s):
        if XFIRST[s]:
            ar_z1add(s)
            ar_z2(s)
        else:
            ar_z2add(s)
            ar_x(s)

    def ar_fin(s):
        (ar_z2add if XFIRST[s] else ar_xadd)(s)

    def fslot(s, r0, n):
        return fS.at[s, pl.ds(r0, n), :]

    def ag_z2(s):
        r0, n = blk_z(s, 0)
        f = fslot(s, r0, n)
        ar[(s, "g2")] = xchg(f, f, z2)
        ar[(s, "g1")] = xchg(f, f, z1)

    def ag_z1(s):
        ar[(s, "g2")].wait_recv()
        r0, n = blk_z(s, 2)
        f = fslot(s, r0, n)
        ar[(s, "g3")] = xchg(f, f, z1)

    def ag_zend(s):
        ar[(s, "g1")].wait_recv()
        ar[(s, "g3")].wait_recv()

    def ag_x(s):
        f = fslot(s, xbase, 192) if XFIRST[s] else fslot(s, spot_of(s), 48)
        ar[(s, "gx")] = xchg(f, f, xp)

    def ag_begin(s):
        r0 = spot_of(s)
        fslot(s, r0, 48)[...] = gA(s, r0, 48)[...]
        (ag_z2 if XFIRST[s] else ag_x)(s)

    def ag_step2(s):
        if XFIRST[s]:
            ag_z1(s)
        else:
            ar[(s, "gx")].wait_recv()
            ag_z2(s)

    def ag_step3(s):
        if XFIRST[s]:
            ag_zend(s)
            ag_x(s)
        else:
            ag_z1(s)

    def ag_core(s):
        if XFIRST[s]:
            ar[(s, "gx")].wait_recv()
        else:
            ag_zend(s)
        f = fslot(s, cbase, HL)
        ar[(s, "gc")] = xchg(f, fA.at[s, pl.ds(cbase, HL), :], core)
        load(f, fA.at[s, pl.ds(cbase, HL), :])

    for s, tt in ((3, t), (4, 1 - t)):
        gp = tn(attF[tt], n2[0:H, :])
        gA(s, 0, HL)[...] = gp[:, 0:HL].astype(BF)
        gA(s, HL, HL)[...] = gp[:, HL:D].astype(BF)
        ar_core(s)
    rs_z1(1, 0)
    rs_z3(0, 0)
    rs_x(1, 1)
    cda[0].wait_recv()
    att_back(1 - t, True)
    rs_z2(1, 0)
    cda[1].wait_recv()
    att_back(1 - t, False)

    flush([cO])
    cdn = []
    for o in (1 - t, t):
        r0 = al(oth + o * BLK, BLK)
        finish_rows(r0)
        rows = pl.ds(al(H + o * BLK, BLK), BLK)
        n2[rows, :] = dn1_rows(r0).astype(BF)
        cdn.append(xchg(n2.at[rows, :], rN.at[pl.ds(al(o * BLK, BLK), BLK), :], yp))
    for s in (3, 4):
        ar_begin(s)
    att_back(t, True)
    for b in range(2):
        finish_rows(al(own + b * BLK, BLK))

    def gw(s, src):
        def body(m, carry):
            rows = pl.ds(al(m * BLK, BLK), BLK)
            gA(s, al(m * BLK, BLK), BLK)[...] = nn(nT[rows, :], src[...]).astype(BF)
            return carry

        lax.fori_loop(0, 3, body, 0)
        ar_core(s)

    rs_z1(0, 1)
    rs_z3(1, 0)
    for s in (3, 4):
        ar_step2(s)
    gw(0, act.at[:, 0:HL])
    gw(1, act.at[:, HL:D])
    ar_begin(0)
    gw(2, dh.at[:, 0:HL])
    ar_begin(1)
    rs_z2(0, 1)
    ar_begin(2)
    for s in (3, 4):
        ar_step3(s)

    vecA[0] = jnp.zeros((16, D), F32)
    for i, row in ((3, sp), (4, s2g), (5, s2b), (6, sd)):
        vecA[0, i : i + 1, :] = row
    vecA[0, pl.ds(8 + 2 * tr[0] + c, 1), :] = bsums[0]
    vecA[0, pl.ds(8 + 2 * tr[1] + c, 1), :] = bsums[1]
    vecA[0, pl.ds(12 + t, 1), 0:HL] = rowsum(act[:, 0:HL].astype(F32))
    vecA[0, pl.ds(12 + t, 1), HL:D] = rowsum(dh[:, 0:HL].astype(F32))
    ar_step2(0)
    ar_step2(1)
    rs_z3(0, 1)
    rs_z1(1, 1)

    stok, s1g, s1b = zrow, zrow, zrow
    cgin = []
    for i, o in enumerate((t, 1 - t)):
        o0 = al(o * BLK, BLK)
        r0 = al(own + o0, BLK)
        rows = pl.ds(r0, BLK)
        orow = pl.ds(o0, BLK)
        cdn[i].wait_recv()
        dnb = dn1_rows(r0) + rN[orow, :].astype(F32)
        m, v = start_rows(r0)
        cent, r = stats(v)
        xhat = cent * r
        dst = mid[orow, :] + norm_back(xhat, r, dnb, ln1g)
        ginS[orow, :] = jnp.where(m, 0.0, dst).astype(BF)
        cgin.append(xchg(ginS.at[orow, :], gin.at[rows, :], yp))
        load(ginS.at[orow, :], gin.at[rows, :])
        stok = stok + rowsum(jnp.where(m, dst, 0.0))
        s1g = s1g + rowsum(dnb * xhat)
        s1b = s1b + rowsum(dnb)
        if i == 0:
            rs_z2(1, 1)
            rs_y(0)
            ar_step2(2)
            ar_step3(0)
            ar_step3(1)
            ar_fin(3)
            ar_fin(4)
            cgp = xchg(gA(4, spot_of(4), 48), rgp, yp)
    for i, row in ((0, stok), (1, s1g), (2, s1b)):
        vecA[0, i : i + 1, :] = row
    cv = xchg(vecA.at[0], vR.at[0], core)
    rs_z3(1, 1)
    ar_step3(2)
    ar_fin(0)
    ag_begin(0)
    ar_fin(1)
    ag_begin(1)
    cv.wait_recv()
    vecA[1] = vecA[0] + vR[0]
    cv = xchg(vecA.at[1], vR.at[1], xp)
    cgp.wait_recv()
    addto(gA(3, spot_of(3), 48), rgp)
    ag_begin(3)
    ar_fin(2)
    ag_begin(2)
    cv.wait_recv()
    vecA[2] = vecA[1] + vR[1]
    cv = xchg(vecA.at[2], vR.at[2], z1)
    rs_y(1)
    for s in (0, 1, 3, 2):
        ag_step2(s)
    cv.wait_recv()
    vecA[3] = vecA[2] + vR[2]
    cv = xchg(vecA.at[3], vR.at[3], z2)
    for s in (0, 1, 3, 2):
        ag_step3(s)
    rs_c(0)
    rs_c(1)
    cv.wait_recv()
    vecA[4] = vecA[3] + vR[3]
    cv = xchg(vecA.at[4], vR.at[4], yp)
    for s in (0, 1, 3, 2):
        ag_core(s)
    rs_end(0)
    rs_end(1)
    for s in (0, 1, 3, 2):
        ar[(s, "gc")].wait_recv()
    cv.wait_recv()
    vout[...] = vecA[4] + vR[4]
    for cp in cmix + cgin:
        cp.wait_recv()
    flush([cp for cp, _ in pending])
    for cp in loads[4:]:
        cp.wait()


def scratch():
    def v(shape, dt):
        return pltpu.VMEM(shape, dt)

    return [
        v((T, D), BF), v((D, T), BF), v((3, T, HL), BF), v((T, HL), BF), v((2, H, HL), BF), v((2, HL, D), BF),
        v((2, D, D), BF), v((2, D, D), BF), v((H, D), F32), v((T, D), BF), v((T, D), BF), v((D, T), BF),
        v((T, D), F32), v((T, D), F32), v((H, D), BF), v((H, D), BF), v((T, D), BF), v((T, D), BF),
        v((2, 2, 4, 96, D), BF), v((2, 2, 4, 96, D), BF),
        v((2, 2, 9, 96, D), BF), v((2, 96, D), BF), v((2, 96, D), BF), v((2, 96, D), BF),
        v((2, 96, D), F32), v((2, 48, D), F32), v((T, HL), BF), v((48, HL), BF), v((5, 720, HL), BF),
        v((8, T), F32), v((2, 8, D), F32), v((5, 16, D), F32), v((5, 16, D), F32),
        v((T, D), BF), v((3, D, HL), BF), v((T, 128), jnp.int32), v((1, T), jnp.int32), v((8, D), F32),
        v((H, D), BF), v((H, D), BF), v((4, D, HL), BF), v((2, 48, 2 * D), F32),
        pltpu.SemaphoreType.DMA((XCH,)), pltpu.SemaphoreType.DMA((XCH,)), pltpu.SemaphoreType.DMA((20,)),
    ]


def finish(mixed, gin, fa, gup, gdn, vs, o_mixed, o_gin, o_tok, o_g1, o_b1, o_qkv, o_bqv, o_proj, o_bp, o_g2, o_b2, o_up,
           o_bup, o_dn, o_bd, gb, gf, fb, ff, pf, mb, ub, sem):
    t = lax.axis_index("tensor")
    count = [0]

    def copy(src, dst):
        cp = pltpu.make_async_copy(src, dst, sem.at[count[0]])
        count[0] += 1
        cp.start()
        return cp

    gc = [copy(gin.at[b * BLK : b * BLK + BLK, :], gb.at[b * BLK : b * BLK + BLK, :]) for b in range(4)]
    fc = [copy(fa.at[s], fb.at[s]) for s in range(4)]
    through = [(copy(mixed, mb), mb, o_mixed), (copy(gup, ub.at[0]), ub.at[0], o_up), (copy(gdn, ub.at[1]), ub.at[1], o_dn)]
    out = []
    for i, o in enumerate((o_tok, o_g1, o_b1, o_bp, o_g2, o_b2, o_bd)):
        o[...] = vs[i : i + 1, :].reshape(D)
    for i in range(2):
        o_bup[i * D : i * D + D] = vs[pl.ds(8 + 2 * t + i, 1), :].reshape(D)
        o_bqv[i : i + 1, :] = vs[pl.ds(12 + t, 1), i * HL : i * HL + HL]
    for b in range(4):
        gc[b].wait()
        rows = slice(b * BLK, b * BLK + BLK)
        gf[rows, :] = gb[rows, :].astype(F32)
        out.append(copy(gf.at[rows, :], o_gin.at[rows, :]))
    for cp, here, there in through:
        cp.wait()
        out.append(copy(here, there))
    for s in range(4):
        fc[s].wait()
        if s < 3:
            ff[s] = fb[s].astype(F32)
            out.append(copy(ff.at[s], o_qkv.at[s]))
        else:
            pf[:, 0:HL] = fb[3, 0:HL, :].astype(F32)
            pf[:, HL:D] = fb[3, HL:D, :].astype(F32)
            out.append(copy(pf, o_proj))
    for cp in out:
        cp.wait()


def on_device(
    patches, image_ids, valid, mask_pos, mask_token, ln1_gain, ln1_bias, w_qkv, b_qv, w_proj, b_proj,
    ln2_gain, ln2_bias, w_up, b_up, w_down, b_down, cotangent,
):
    vm = pl.BlockSpec(memory_space=pltpu.VMEM)
    hbm = pl.BlockSpec(memory_space=pl.ANY)
    sds = jax.ShapeDtypeStruct
    parts = pl.pallas_call(
        mega,
        out_shape=(
            sds((T, D), BF), sds((T, D), BF), sds((4, D, HL), BF), sds((48, 2 * D), F32), sds((48, 2 * D), F32),
            sds((16, D), F32),
        ),
        in_specs=[hbm if i in (0, 11, 13, 17) else vm for i in range(18)],
        out_specs=(hbm,) * 5 + (vm,),
        scratch_shapes=scratch(),
        compiler_params=pltpu.CompilerParams(collective_id=0, has_side_effects=True, vmem_limit_bytes=66584576),
        name="block",
    )(
        patches, image_ids, valid, mask_pos, mask_token, ln1_gain, ln1_bias, b_proj, ln2_gain, ln2_bias, b_down,
        jnp.transpose(w_qkv, (1, 0, 2)), b_qv, w_proj, w_up, w_down.T, b_up, cotangent,
    )
    row = sds((D,), F32)
    big = {0, 1, 5, 7, 11, 13}
    outs = pl.pallas_call(
        finish,
        out_shape=(
            sds((T, D), BF), sds((T, D), F32), row, row, row, sds((3, D, HL), F32), sds((2, HL), F32), sds((HL, D), F32),
            row, row, row, sds((48, 2 * D), F32), sds((2 * D,), F32), sds((48, 2 * D), F32), row,
        ),
        in_specs=[hbm] * 5 + [vm],
        out_specs=tuple(hbm if i in big else vm for i in range(15)),
        scratch_shapes=[
            pltpu.VMEM((T, D), BF), pltpu.VMEM((T, D), F32), pltpu.VMEM((4, D, HL), BF), pltpu.VMEM((3, D, HL), F32),
            pltpu.VMEM((HL, D), F32), pltpu.VMEM((T, D), BF), pltpu.VMEM((2, 48, 2 * D), F32),
            pltpu.SemaphoreType.DMA((24,)),
        ],
        compiler_params=pltpu.CompilerParams(vmem_limit_bytes=66584576),
        name="finish",
    )(*parts)
    outs = list(outs)
    outs[5] = jnp.transpose(outs[5], (1, 0, 2))
    outs[13] = outs[13].T
    return tuple(outs)


HEAD_DIM = 64


def norm_rows(values, gain, shift):
    mean = jnp.mean(values, axis=-1, keepdims=True)
    cent = values - mean
    var = jnp.mean(cent * cent, axis=-1, keepdims=True)
    return cent * lax.rsqrt(var + EPS) * gain + shift


def left_dot(first, second):
    return lax.dot_general(
        first, second, (((0,), (0,)), ((), ())), preferred_element_type=jnp.float32
    )


def right_dot(first, second):
    return lax.dot_general(
        first, second, (((1,), (1,)), ((), ())), preferred_element_type=jnp.float32
    )


def allowed_rows(ids, live, begin, count):
    rows = ids.shape[0]
    own_ids = lax.dynamic_slice_in_dim(ids, begin, count, 0)
    places = begin + jnp.arange(count)
    same_place = places[:, None] == jnp.arange(rows)[None, :]
    return (own_ids[:, None] == ids[None, :]) & ((live[None, :] == 1) | same_place)


def spread(
    patches,
    image_ids,
    valid,
    mask_pos,
    mask_token,
    ln1_gain,
    ln1_bias,
    w_qkv,
    b_qv,
    w_proj,
    b_proj,
    ln2_gain,
    ln2_bias,
    w_up,
    b_up,
    w_down,
    b_down,
    cotangent,
):
    rows = patches.shape[0]
    local_width = w_qkv.shape[2]
    local_heads = local_width // HEAD_DIM
    scale = 1.0 / HEAD_DIM**0.5
    ids = image_ids[0]
    live = valid[0]
    masked = mask_pos[0][:, None] == 1
    block = min(512, rows)
    blocks = rows // block
    start = jnp.where(masked, mask_token.astype(jnp.float32)[None, :], patches.astype(jnp.float32))
    normed, norm1_pull = jax.vjp(
        norm_rows, start, ln1_gain.astype(jnp.float32), ln1_bias.astype(jnp.float32)
    )
    normed_b = normed.astype(jnp.bfloat16)
    qv_bias = b_qv.astype(jnp.float32)
    bias = jnp.stack([qv_bias[0], jnp.zeros_like(qv_bias[0]), qv_bias[1]])
    qkv = jnp.einsum("td,dsc->tsc", normed_b, w_qkv, preferred_element_type=jnp.float32)
    qkv_b = (qkv + bias[None]).astype(jnp.bfloat16)
    query = qkv_b[:, 0].reshape(rows, local_heads, HEAD_DIM)
    keys = qkv_b[:, 1].reshape(rows, local_heads, HEAD_DIM)
    values = qkv_b[:, 2].reshape(rows, local_heads, HEAD_DIM)
    outputs = []
    totals = []
    for index in range(blocks):
        begin = index * block
        query_part = query[begin : begin + block]
        allowed = allowed_rows(ids, live, begin, block)
        scores = (
            jnp.einsum("qhc,khc->hqk", query_part, keys, preferred_element_type=jnp.float32) * scale
        )
        scores = jnp.where(allowed[None], scores, -1e30)
        top = jnp.max(scores, axis=-1, keepdims=True)
        expd = jnp.exp(scores - top)
        summed = jnp.sum(expd, axis=-1, keepdims=True)
        probs_b = (expd / summed).astype(jnp.bfloat16)
        totals.append(top + jnp.log(summed))
        outputs.append(
            jnp.einsum("hqk,khc->qhc", probs_b, values, preferred_element_type=jnp.float32)
        )
    attended_b = jnp.concatenate(outputs, axis=0).reshape(rows, local_width).astype(jnp.bfloat16)
    attn_part = jnp.dot(attended_b, w_proj, preferred_element_type=jnp.float32)
    ln2_gain_f = ln2_gain.astype(jnp.float32)
    ln2_bias_f = ln2_bias.astype(jnp.float32)
    attn_total = lax.psum(attn_part, "tensor")
    middle = start + attn_total + b_proj.astype(jnp.float32)
    normed2, norm2_pull = jax.vjp(norm_rows, middle, ln2_gain_f, ln2_bias_f)
    normed2_b = normed2.astype(jnp.bfloat16)
    up_full, down_full = (
        lax.all_gather(w_up, "dp", axis=0, tiled=True),
        lax.all_gather(w_down, "dp", axis=1, tiled=True),
    )
    hidden = jnp.dot(normed2_b, up_full, preferred_element_type=jnp.float32) + b_up.astype(
        jnp.float32
    )
    active, gelu_pull = jax.vjp(partial(jax.nn.gelu, approximate=False), hidden)
    active_b = active.astype(jnp.bfloat16)
    mlp_part = jnp.dot(active_b, down_full, preferred_element_type=jnp.float32)
    mlp_total = lax.psum(mlp_part.astype(jnp.bfloat16), "tensor").astype(jnp.float32)
    mixed = (middle + mlp_total + b_down.astype(jnp.float32)).astype(jnp.bfloat16)
    seed_grad = cotangent.astype(jnp.float32)
    up_back, down_back = (up_full, down_full)
    grad_b_down = jnp.sum(seed_grad, axis=0)
    grad_down_local = left_dot(active_b, cotangent)
    grad_active = right_dot(cotangent, down_back)
    (grad_hidden,) = gelu_pull(grad_active)
    grad_hidden_b = grad_hidden.astype(jnp.bfloat16)
    grad_b_up = jnp.sum(grad_hidden_b.astype(jnp.float32), axis=0)
    grad_up_local = left_dot(normed2_b, grad_hidden_b)
    grad_normed2_part = right_dot(grad_hidden_b, up_back)
    grad_normed2 = lax.psum(grad_normed2_part, "tensor")
    grad_mid_norm, grad_ln2_gain, grad_ln2_bias = norm2_pull(grad_normed2)
    grad_middle = seed_grad + grad_mid_norm
    grad_w_up, grad_w_down = (
        lax.psum_scatter(grad_up_local, "dp", scatter_dimension=0, tiled=True),
        lax.psum_scatter(grad_down_local, "dp", scatter_dimension=1, tiled=True),
    )
    grad_branch_b = grad_middle.astype(jnp.bfloat16)
    grad_b_proj = jnp.sum(grad_branch_b.astype(jnp.float32), axis=0)
    grad_w_proj = left_dot(attended_b, grad_branch_b)
    grad_attended = (
        right_dot(grad_branch_b, w_proj).astype(jnp.bfloat16).reshape(rows, local_heads, HEAD_DIM)
    )
    grad_query_parts = []
    grad_keys = jnp.zeros((rows, local_heads, HEAD_DIM), jnp.float32)
    grad_values = jnp.zeros((rows, local_heads, HEAD_DIM), jnp.float32)
    for index in range(blocks):
        begin = index * block
        query_part = query[begin : begin + block]
        grad_out_part = grad_attended[begin : begin + block]
        allowed = allowed_rows(ids, live, begin, block)
        scores = (
            jnp.einsum("qhc,khc->hqk", query_part, keys, preferred_element_type=jnp.float32) * scale
        )
        scores = jnp.where(allowed[None], scores, -1e30)
        probs = jnp.exp(scores - totals[index])
        probs_b = probs.astype(jnp.bfloat16)
        grad_values = grad_values + jnp.einsum(
            "hqk,qhc->khc", probs_b, grad_out_part, preferred_element_type=jnp.float32
        )
        grad_probs = jnp.einsum(
            "qhc,khc->hqk", grad_out_part, values, preferred_element_type=jnp.float32
        )
        inner = jnp.sum(probs * grad_probs, axis=-1, keepdims=True)
        grad_scores_b = (probs * (grad_probs - inner)).astype(jnp.bfloat16)
        grad_query_parts.append(
            jnp.einsum("hqk,khc->qhc", grad_scores_b, keys, preferred_element_type=jnp.float32)
            * scale
        )
        grad_keys = (
            grad_keys
            + jnp.einsum(
                "hqk,qhc->khc", grad_scores_b, query_part, preferred_element_type=jnp.float32
            )
            * scale
        )
    grad_query = jnp.concatenate(grad_query_parts, axis=0)
    grad_qkv_b = (
        jnp.stack([grad_query, grad_keys, grad_values], axis=1)
        .reshape(rows, 3, local_width)
        .astype(jnp.bfloat16)
    )
    grad_qkv_f = grad_qkv_b.astype(jnp.float32)
    grad_b_qv = jnp.stack([jnp.sum(grad_qkv_f[:, 0], axis=0), jnp.sum(grad_qkv_f[:, 2], axis=0)])
    grad_w_qkv = jnp.einsum("td,tsc->dsc", normed_b, grad_qkv_b, preferred_element_type=jnp.float32)
    grad_normed_part = jnp.einsum(
        "tsc,dsc->td", grad_qkv_b, w_qkv, preferred_element_type=jnp.float32
    )
    grad_normed = lax.psum(grad_normed_part.astype(jnp.bfloat16), "tensor").astype(jnp.float32)
    grad_start_norm, grad_ln1_gain, grad_ln1_bias = norm1_pull(grad_normed)
    grad_start = grad_middle + grad_start_norm
    grad_input = jnp.where(masked, 0.0, grad_start)
    grad_token = jnp.sum(jnp.where(masked, grad_start, 0.0), axis=0)
    summed = lax.psum(
        (
            grad_token,
            grad_ln1_gain,
            grad_ln1_bias,
            grad_w_qkv,
            grad_b_qv,
            grad_w_proj,
            grad_b_proj,
            grad_ln2_gain,
            grad_ln2_bias,
            grad_b_up,
            grad_b_down,
        ),
        "dp",
    )
    return (
        mixed,
        grad_input,
        summed[0],
        summed[1],
        summed[2],
        summed[3],
        summed[4],
        summed[5],
        summed[6],
        summed[7],
        summed[8],
        grad_w_up,
        summed[9],
        grad_w_down,
        summed[10],
    )


def solution(mesh):
    placed = (
        P("dp", None),
        P("dp", None),
        P("dp", None),
        P("dp", None),
        P(),
        P(),
        P(),
        P(None, None, "tensor"),
        P(None, "tensor"),
        P("tensor", None),
        P(),
        P(),
        P(),
        P("dp", "tensor"),
        P("tensor"),
        P("tensor", "dp"),
        P(),
        P("dp", None),
    )
    fits = mesh.shape["dp"] == 16 and mesh.shape["tensor"] == 2
    return jax.shard_map(
        on_device if fits else spread,
        mesh=mesh,
        in_specs=placed,
        out_specs=(
            P("dp", None),
            P("dp", None),
            P(),
            P(),
            P(),
            P(None, None, "tensor"),
            P(None, "tensor"),
            P("tensor", None),
            P(),
            P(),
            P(),
            P("dp", "tensor"),
            P("tensor"),
            P("tensor", "dp"),
            P(),
        ),
        check_vma=False,
    )
```

```python
from functools import partial

import jax
import jax.numpy as jnp
from jax import lax
from jax.experimental import pallas as pl
from jax.experimental.pallas import tpu as pltpu
from jax.sharding import PartitionSpec as P

BF = jnp.bfloat16
F32 = jnp.float32
MESH = pl.DeviceIdType.MESH
EPS = 1e-06
T = 1024
H = 512
D = 768
HL = 384
BLK = 256
WIN = 768
CUT = 640
XCH = 240


def nn(a, b):
    return lax.dot_general(a, b, (((1,), (0,)), ((), ())), preferred_element_type=F32)


def nt(a, b):
    return lax.dot_general(a, b, (((1,), (1,)), ((), ())), preferred_element_type=F32)


def tn(a, b):
    return lax.dot_general(a, b, (((0,), (0,)), ((), ())), preferred_element_type=F32)


def rowsum(v):
    return jnp.sum(v, axis=0, keepdims=True)


def lane_half(shape):
    return lax.broadcasted_iota(jnp.int32, shape, 1) < 64


def stats(v):
    mean = jnp.sum(v, axis=-1, keepdims=True) * (1.0 / D)
    cent = v - mean
    var = jnp.sum(cent * cent, axis=-1, keepdims=True) * (1.0 / D)
    return cent, lax.rsqrt(var + EPS)


def norm_back(xhat, r, d, gain):
    e = d * gain
    m1 = jnp.sum(e, axis=-1, keepdims=True) * (1.0 / D)
    m2 = jnp.sum(e * xhat, axis=-1, keepdims=True) * (1.0 / D)
    return r * (e - m1 - xhat * m2)


def mega(
    patches, ids, live, hidden_pos, token_b, ln1g_b, ln1b_b, bproj_b, ln2g_b, ln2b_b, bdown_b, wqkv_h, bqv_b, wproj,
    up, dn, bup, cot,
    mixed, gin, fA, gup, gdn, vout,
    n1, nT, qkv, attO, attF, wpf, Wu, Wd, mid, n2, dml, dmlT, outA, dn2A, rO, rN, act, dh, gU, gD,
    rG, rX, sy, ry, sc, rc, dO, rgp, rA, lseT, bupA, vecA, vR, pat, wqkv, codec, coder, vec, mixS, ginS, fS,
    gS, ssem, rsem, lsem,
):
    d = lax.axis_index("dp")
    t = lax.axis_index("tensor")
    z = lax.div(d, 4)
    x = lax.rem(lax.div(d, 2), 2)
    c = lax.rem(d, 2)
    zk = (z, z + 1 - 2 * lax.rem(z, 2), lax.rem(z + 2, 4), 3 - z)
    xr = (x, 1 - x)
    tr = (t, 1 - t)

    def dev(zz, xx, cc, tt):
        return ((zz * 2 + xx) * 2 + cc, tt)

    core = dev(z, x, 1 - c, t)
    xp = dev(z, 1 - x, c, t)
    yp = dev(z, x, c, 1 - t)
    z1 = dev(zk[1], x, c, t)
    z2 = dev(zk[2], x, c, t)
    z3 = dev(zk[3], x, c, t)
    mid_z = (z == 1) | (z == 2)
    end_z = (z == 0) | (z == 3)

    pending = []
    flushed = set()
    slots = [0]

    def slot():
        slots[0] += 1
        return slots[0] - 1

    def xchg(src, dst, to, when=None, land=None):
        i = len(pending)
        cp = pltpu.make_async_remote_copy(
            src_ref=src, dst_ref=dst, send_sem=ssem.at[i], recv_sem=rsem.at[slot() if land is None else land],
            device_id=to, device_id_type=MESH,
        )
        pending.append((cp, when))
        if when is None:
            cp.start()
        else:
            pl.when(when)(cp.start)
        return cp

    def landed(dst, land, frm):
        pltpu.make_async_remote_copy(
            src_ref=dst, dst_ref=dst, send_sem=ssem.at[0], recv_sem=rsem.at[land], device_id=frm, device_id_type=MESH
        ).wait_recv()

    def flush(cps):
        cps = set(id(cp) for cp in cps)
        for cp, when in pending:
            if id(cp) in cps and id(cp) not in flushed:
                flushed.add(id(cp))
                if when is None:
                    cp.wait_send()
                else:
                    pl.when(when)(cp.wait_send)

    def al(v, m):
        return pl.multiple_of(v, m)

    bar = pltpu.get_barrier_semaphore()
    peers = (core, xp, yp, z1, z2, z3)
    for p in peers:
        pl.semaphore_signal(bar, inc=1, device_id=p, device_id_type=MESH)
    loads = []

    def load(src, dst):
        cp = pltpu.make_async_copy(src, dst, lsem.at[len(loads)])
        cp.start()
        loads.append(cp)
        return cp

    lpat = load(patches, pat)
    lwq = load(wqkv_h, wqkv)
    code = ids[...] + 16 * live[...] + 32 * hidden_pos[...]
    coder[...] = code
    codec[...] = jnp.broadcast_to(code.astype(F32), (128, T)).T.astype(jnp.int32)
    for i, row in enumerate((token_b, ln1g_b, ln1b_b, bproj_b, ln2g_b, ln2b_b, bdown_b)):
        vec[i : i + 1, :] = row[...].astype(F32).reshape(1, D)
    bqv = bqv_b[...].astype(F32)
    bupA[0] = jnp.zeros((8, D), F32)
    for i in range(2):
        bupA[0, i : i + 1, :] = bup[i * D : i * D + D].astype(F32).reshape(1, D)
    pl.semaphore_wait(bar, len(peers))

    own = al(t * H, H)
    oth = al((1 - t) * H, H)
    cslot = al(c * H, H)
    sslot = al((1 - c) * H, H)
    W = (Wu, Wd)
    shards = (up, dn)

    def wblk(a, k, xx, yy):
        return W[a].at[tr[yy], pl.ds(al((zk[k] * 2 + xr[xx]) * 96, 32), 96), :]

    ccp = []
    mine = al((z * 2 + x) * 96 + c * 48, 16)
    for a in (0, 1):
        ccp.append(
            xchg(shards[a].at[:, pl.ds(al((1 - c) * D, 128), D)], W[a].at[t, pl.ds(mine, 48), :], core)
        )
    whalf = pl.ds(al(c * 192, 64), 192)
    cwp = xchg(wproj.at[whalf, :], wpf.at[t, whalf, :], yp)
    cbup = xchg(bupA.at[0], bupA.at[1], yp)
    cdml = xchg(cot.at[pl.ds(own, H), :], dml.at[pl.ds(cslot, H), :], core)
    ldml = load(cot.at[pl.ds(own, H), :], dml.at[pl.ds(cslot, H), :])
    lwp = load(wproj, wpf.at[t])
    for a in (0, 1):
        W[a][t, pl.ds(mine, 48), :] = shards[a][:, pl.ds(al(c * D, 128), D)]

    zc, xc, yc = {}, {}, {}

    chains = {
        "u": lambda k: wblk(0, k, 0, 0),
        "d": lambda k: wblk(1, k, 0, 0),
        "e": lambda k: wblk(1, k, 0, 1),
        "b": lambda k: Wu.at[tr[1], pl.ds(al(zk[k] * 192, 64), 192), CUT:D],
    }

    def zsend(q, k):
        zc[(q, k)] = xchg(chains[q](0), chains[q](0), z1 if k == 1 else z2)

    def zstart(q):
        zsend(q, 1)
        zsend(q, 2)

    def zstep(q):
        zc[(q, 2)].wait_recv()
        zc[(q, 3)] = xchg(chains[q](2), chains[q](2), z1)

    def zend(q):
        zc[(q, 3)].wait_recv()

    def xsend(a, k, yy):
        xc[(a, k, yy)] = xchg(wblk(a, k, 0, yy), wblk(a, k, 0, yy), xp)

    def ysend(a, k, xx):
        ref = wblk(a, k, xx, 0)
        if a == 0:
            ref = W[0].at[t, pl.ds(al((zk[k] * 2 + xr[xx]) * 96, 32), 96), 0:CUT]
        yc[(a, k, xx)] = xchg(ref, ref, yp)

    def bown(tt):
        return W[0].at[tt, pl.ds(al((z * 2 + x) * 96, 32), 96), CUT:D]

    token = vec[0:1, :]
    ln1g = vec[1:2, :]
    ln1b = vec[2:3, :]

    def start_rows(r0):
        m = lax.shift_right_logical(codec[pl.ds(r0, BLK), 0:1], 5) == 1
        return m, jnp.where(m, token, pat[pl.ds(r0, BLK), :].astype(F32))

    def ln1_block(b, carry):
        r0 = al(b * BLK, BLK)
        _, v = start_rows(r0)
        cent, r = stats(v)
        nb = (cent * r * ln1g + ln1b).astype(BF)
        n1[pl.ds(r0, BLK), :] = nb
        for s in range(3):
            y = nn(nb, wqkv[s])
            if s == 0:
                y = y + bqv[0:1, :]
            if s == 2:
                y = y + bqv[1:2, :]
            qkv[s, pl.ds(r0, BLK), :] = y.astype(BF)
        return carry

    lpat.wait()
    lwq.wait()
    lax.fori_loop(0, 1, ln1_block, 0)
    for a in (0, 1):
        ccp[a].wait_recv()
    zstart("u")
    zsend("d", 1)
    xsend(0, 0, 0)
    xsend(1, 0, 0)
    lax.fori_loop(1, 4, ln1_block, 0)

    def masked_pair(block, scale=None):
        low = lane_half(block.shape)
        zero = jnp.zeros_like(block)
        if scale is not None:
            block = block * jnp.asarray(scale, BF)
        return jnp.where(low, block, zero), jnp.where(low, zero, block)

    def att_block(half, edge):
        qb = half * 3 if edge else 1 + half
        win = H if edge else WIN
        r0 = al(qb * BLK, BLK)
        ws = al(half * H if edge else half * BLK, BLK)
        cr = codec[pl.ds(r0, BLK), 0:1]
        cw = coder[:, pl.ds(ws, win)]
        rid = r0 + lax.broadcasted_iota(jnp.int32, (BLK, win), 0)
        cid = ws + lax.broadcasted_iota(jnp.int32, (BLK, win), 1)
        ok = ((cr & 15) == (cw & 15)) & (((cw & 16) == 16) | (rid == cid))
        dn2A[0:BLK, 0:win] = jnp.where(ok, 0.0, -1e30)
        lane = lax.broadcasted_iota(jnp.int32, (BLK, 128), 1)

        def pair(p, lacc):
            cols = pl.ds(al(p * 128, 128), 128)
            qs = masked_pair(qkv[0, pl.ds(r0, BLK), cols], 0.125)
            kp = qkv[1, pl.ds(ws, win), cols]
            vp = qkv[2, pl.ds(ws, win), cols]
            outs = []
            for h in range(2):
                s = nt(qs[h], kp) + dn2A[0:BLK, 0:win]
                top = jnp.max(s, axis=-1, keepdims=True)
                e = jnp.exp(s - top)
                l = jnp.sum(e, axis=-1, keepdims=True)
                o = nn(e.astype(BF), vp) * (1.0 / l)
                outs.append(o)
                lacc = jnp.where(lane == (2 * p + h), top + jnp.log(l), lacc)
            attO[pl.ds(r0, BLK), cols] = jnp.where(lane_half((BLK, 128)), outs[0], outs[1]).astype(BF)
            return lacc

        lacc = lax.fori_loop(0, 3, pair, jnp.zeros((BLK, 128), F32))
        lseT[:, pl.ds(r0, BLK)] = lacc.T[0:8, :]
        return r0

    catt = []

    def att_send(r0):
        catt.append(xchg(attO.at[pl.ds(r0, BLK), :], attF.at[t, pl.ds(al(r0 - oth, BLK), BLK), :], yp))

    att_send(att_block(1 - t, True))
    att_send(att_block(1 - t, False))
    ysend(1, 0, 0)
    yb = xchg(bown(t), bown(t), yp)
    zc[("u", 1)].wait_recv()
    xsend(0, 1, 0)
    zstep("u")
    zsend("d", 2)
    xsend(0, 2, 0)
    cwp.wait_recv()
    cwc = xchg(wpf.at[1 - t, whalf, :], wpf.at[1 - t, whalf, :], core)
    for k in range(3):
        ysend(0, k, 0)
    att_block(t, True)
    att_block(t, False)
    attF[t] = attO[pl.ds(own, H), :]
    zend("u")
    xsend(0, 3, 0)
    zc[("d", 1)].wait_recv()
    xsend(1, 1, 0)
    ysend(0, 3, 0)

    bproj = vec[3:4, :]
    ln2g = vec[4:5, :]
    ln2b = vec[5:6, :]
    bdown = vec[6:7, :]
    ldml.wait()
    lwp.wait()
    for cp in catt:
        cp.wait_recv()
    cwc.wait_recv()

    def mid_block(b, carry):
        o0 = al(b * BLK, BLK)
        _, v = start_rows(al(own + o0, BLK))
        m = v + (nn(attF[0, pl.ds(o0, BLK), :], wpf[0]) + nn(attF[1, pl.ds(o0, BLK), :], wpf[1])) + bproj
        mid[pl.ds(o0, BLK), :] = m
        cent, r = stats(m)
        n2[pl.ds(al(cslot + o0, BLK), BLK), :] = (cent * r * ln2g + ln2b).astype(BF)
        return carry

    lax.fori_loop(0, 2, mid_block, 0)
    cn2 = xchg(n2.at[pl.ds(cslot, H), :], n2.at[pl.ds(cslot, H), :], core)
    zstep("d")
    xsend(1, 2, 0)
    yc[(1, 0, 0)].wait_recv()
    zstart("e")
    yb.wait_recv()
    xb = xchg(bown(1 - t), bown(1 - t), xp)
    cdml.wait_recv()
    cn2.wait_recv()
    nT[...] = n2[...].T
    dmlT[...] = dml[...].T
    cbup.wait_recv()
    for k in range(4):
        xc[(0, k, 0)].wait_recv()
        ysend(0, k, 1)
    zend("d")
    xsend(1, 3, 0)
    xsend(1, 0, 1)

    G = (gU, gD)
    rs = {}

    def addto(dst, src):
        dst[...] = (dst[...].astype(F32) + src[...].astype(F32)).astype(BF)

    def rs_x(a, j):
        rs[(a, j)] = [xchg(G[a].at[j, 1, h * 2 : h * 2 + 2], rG.at[a, j, h * 2 : h * 2 + 2], xp) for h in (0, 1)]

    rland = {(r, q): slot() for r in ((0, 0, 0), (0, 0, 1), (0, 1, 0), (1, 0, 0), (1, 1, 0)) for q in range(4, 9)}

    def rslot(r, q):
        a, j, xx = r
        if xx == 0:
            return rG.at[a, j, q]
        return rX.at[0] if q == 8 else rG.at[a, j, q - 4]

    def gblk(r, k):
        a, j, xx = r
        return G[a].at[j, xx, zk[k]]

    def rpass(r, k, to, q, when):
        xchg(gblk(r, k), rslot(r, q), to, when, rland[(r, q)])

    def radd(r, k, q):
        landed(rslot(r, q), rland[(r, q)], z1)
        addto(gblk(r, k), rslot(r, q))

    def rs_z0(r):
        for k, q in ((3, 4), (2, 5), (1, 6)):
            rpass(r, k, z1, q, end_z)

    def rs_z1(a, j):
        for cp in rs[(a, j)]:
            cp.wait_recv()
        for zz in range(4):
            addto(G[a].at[j, 0, zz], rG.at[a, j, zz])
        rs_z0((a, j, 0))

    def rs_z2(r):
        pl.when(mid_z)(partial(radd, r, 2, 4))
        rpass(r, 2, z3, 7, mid_z)
        pl.when(mid_z)(partial(radd, r, 3, 5))
        rpass(r, 3, z3, 8, mid_z)

    def rs_z3(r):
        pl.when(mid_z)(partial(radd, r, 1, 7))
        rpass(r, 1, z1, 8, mid_z)

    def rs_zsum(r):
        pl.when(mid_z)(partial(radd, r, 0, 6))
        radd(r, 0, 8)

    def rs_xlast():
        rs_zsum((0, 0, 1))
        rs["xlast"] = xchg(gblk((0, 0, 1), 0), rX.at[1], xp)

    def rs_sum(a, j):
        rs_zsum((a, j, 0))
        total = gblk((a, j, 0), 0)[...].astype(F32)
        if (a, j) == (0, 0):
            rs["xlast"].wait_recv()
            total = total + rX[1].astype(F32)
        return total

    def rs_y(a):
        sy[a] = rs_sum(a, 1).astype(BF)
        rs[(a, "y")] = xchg(sy.at[a], ry.at[a], yp)

    def rs_c(a):
        total = rs_sum(a, 0)
        rs[(a, "y")].wait_recv()
        sc[a] = total + ry[a].astype(F32)
        rs[(a, "c")] = xchg(sc.at[a, pl.ds(al((1 - c) * 48, 16), 48), :], rc.at[a], core)

    def rs_end(a):
        gS[a, :, pl.ds(al(c * D, 128), D)] = sc[a, pl.ds(al(c * 48, 16), 48), :]
        rs[(a, "c")].wait_recv()
        gS[a, :, pl.ds(al((1 - c) * D, 128), D)] = rc[a]
        load(gS.at[a], (gup, gdn)[a])

    bsums = []

    def ff_act(j):
        yy = tr[j]
        bu = bupA[j, pl.ds(c, 1), :]

        def block(b, carry):
            rows = pl.ds(al(b * BLK, BLK), BLK)
            hid = nn(n2[rows, :], Wu[yy]) + bu
            phi = 0.5 * (1.0 + lax.erf(hid * 0.7071067811865476))
            a = (hid * phi).astype(BF)
            act[rows, :] = a
            dh[rows, :] = (phi + hid * (jnp.exp(hid * hid * -0.5) * 0.3989422804014327)).astype(BF)
            return carry

        lax.fori_loop(0, 4, block, 0)

    def ff_out(j):
        yy = tr[j]

        def block(b, carry):
            rows = pl.ds(al(b * BLK, BLK), BLK)
            o = nt(act[rows, :], Wd[yy])
            if j == 0:
                outA[rows, :] = o
            else:
                outA[rows, :] += o
            return carry

        lax.fori_loop(0, 4, block, 0)

    def ff_bwd(j):
        yy = tr[j]

        def block(b, carry):
            rows = pl.ds(al(b * BLK, BLK), BLK)
            dhid = (nn(dml[rows, :], Wd[yy]) * dh[rows, :].astype(F32)).astype(BF)
            dh[rows, :] = dhid
            g = nt(dhid, Wu[yy])
            if j == 0:
                dn2A[rows, :] = g
            else:
                dn2A[rows, :] += g
            return carry + rowsum(dhid.astype(F32))

        bsums.append(lax.fori_loop(0, 4, block, jnp.zeros((1, D), F32)))

    def ff_grads(j, left, right, out):
        def gw_block(b, carry):
            r = nn(left[pl.ds(al(b * 192, 64), 192), :], right[...]).astype(BF)
            for xa in range(2):
                out[j, lax.rem(xa + x, 2), b] = r[xa * 96 : xa * 96 + 96]
            return carry

        lax.fori_loop(0, 4, gw_block, 0)

    def ff_gu(j):
        ff_grads(j, nT, dh, gU)

    def ff_gd(j):
        ff_grads(j, dmlT, act, gD)

    zrow = jnp.zeros((1, D), F32)
    ff_act(0)
    xb.wait_recv()
    zstart("b")
    ff_gd(0)
    zc[("e", 1)].wait_recv()
    xsend(1, 1, 1)
    for k in range(4):
        xc[(1, k, 0)].wait_recv()
    ff_out(0)
    zstep("e")
    xsend(1, 2, 1)
    ff_bwd(0)
    zstep("b")
    ff_gu(0)
    rs_z0((0, 0, 1))
    rs_z0((0, 0, 0))
    zend("e")
    xsend(1, 3, 1)
    rs_x(1, 0)
    zc[("b", 1)].wait_recv()
    zend("b")
    for k in range(4):
        yc[(0, k, 0)].wait_recv()
        yc[(0, k, 1)].wait_recv()
    ff_act(1)
    ff_gd(1)
    rs_x(1, 1)
    for k in range(4):
        xc[(1, k, 1)].wait_recv()
    ff_out(1)

    flush([cn2])
    n2[H:T, :] = outA[pl.ds(sslot, H), :].astype(BF)
    cO = xchg(n2.at[H:T, :], rO, core)
    rs_z2((0, 0, 1))
    ff_bwd(1)
    n2[0:H, :] = dn2A[pl.ds(sslot, H), :].astype(BF)
    cN = xchg(n2.at[0:H, :], rN, core)

    cO.wait_recv()
    cmix = []

    def mixed_block(o):
        o0 = al(o * BLK, BLK)
        rows = pl.ds(o0, BLK)
        crow = pl.ds(al(cslot + o0, BLK), BLK)
        out = mid[rows, :] + (outA[crow, :] + rO[rows, :].astype(F32)) + bdown
        mixS[rows, :] = out.astype(BF)

    def mixed_send(i):
        orow = pl.ds(own + i * 128, 128)
        rows = slice(i * 128, i * 128 + 128)
        cmix.append(xchg(mixS.at[rows, :], mixed.at[orow, :], yp))
        load(mixS.at[rows, :], mixed.at[orow, :])

    mixed_block(0)
    mixed_block(1)
    mixed_send(0)
    ff_gu(1)
    rs_x(0, 1)
    rs_z3((0, 0, 1))
    rs_z2((0, 0, 0))
    flush(catt)
    cN.wait_recv()
    flush([cN])

    sums = [zrow, zrow, zrow, zrow]
    cda = []
    for o in (t, 1 - t):
        o0 = al(o * BLK, BLK)
        rows = pl.ds(o0, BLK)
        crow = pl.ds(al(cslot + o0, BLK), BLK)
        dnb = dn2A[crow, :] + rN[rows, :].astype(F32)
        cent, r = stats(mid[rows, :])
        xhat = cent * r
        ct = dml[crow, :].astype(F32)
        dm = ct + norm_back(xhat, r, dnb, ln2g)
        db = dm.astype(BF)
        n2[rows, :] = db
        attO[rows, :] = nt(db, wpf[1 - t]).astype(BF)
        orow = pl.ds(al(own + o0, BLK), BLK)
        cda.append(xchg(attO.at[rows, :], dO.at[orow, :], yp))
        dO[orow, :] = nt(db, wpf[t]).astype(BF)
        mid[rows, :] = dm
        for i, term in enumerate((dnb * xhat, dnb, db.astype(F32), ct)):
            sums[i] = sums[i] + rowsum(term)
    s2g, s2b, sp, sd = sums

    mixed_send(1)
    mixed_send(2)
    rs_z1(1, 0)
    outA[...] = jnp.zeros((T, D), F32)
    nT[...] = n1[...].T

    def att_back(half, edge):
        qb = half * 3 if edge else 1 + half
        wl = H if edge else WIN
        r0 = al(qb * BLK, BLK)
        ws = al(half * H if edge else half * BLK, BLK)
        cw = codec[pl.ds(ws, wl), 0:1]
        cr = coder[:, pl.ds(r0, BLK)]
        rid = r0 + lax.broadcasted_iota(jnp.int32, (wl, BLK), 1)
        cid = ws + lax.broadcasted_iota(jnp.int32, (wl, BLK), 0)
        ok = ((cr & 15) == (cw & 15)) & (((cw & 16) == 16) | (rid == cid))
        dn2A[0:wl, 0:BLK] = jnp.where(ok, 0.0, -1e30)
        rows = pl.ds(r0, BLK)
        win = pl.ds(ws, wl)

        def pair(p, carry):
            cols = pl.ds(al(p * 128, 128), 128)
            vcols = pl.ds(al(HL + p * 128, 128), 128)
            qp = qkv[0, rows, cols]
            op = dO[rows, cols]
            qs = masked_pair(qp, 0.125)
            os = masked_pair(op)
            kp = qkv[1, win, cols]
            vp = qkv[2, win, cols]
            dqs, dks, dvs = [], [], []
            for h in range(2):
                lse = lseT[pl.ds(2 * p + h, 1), rows]
                pr = jnp.exp(nt(kp, qs[h]) + dn2A[0:wl, 0:BLK] - lse)
                dp = nt(vp, os[h])
                inner = rowsum(pr * dp)
                ds = (pr * (dp - inner)).astype(BF)
                dvs.append(nn(pr.astype(BF), op))
                dks.append(nn(ds, qp))
                dqs.append(tn(ds, kp))
            low = lane_half((BLK, 128))
            lowk = lane_half((wl, 128))
            act[rows, cols] = (jnp.where(low, dqs[0], dqs[1]) * 0.125).astype(BF)
            outA[win, cols] += jnp.where(lowk, dks[0], dks[1])
            outA[win, vcols] += jnp.where(lowk, dvs[0], dvs[1])
            return carry

        lax.fori_loop(0, 3, pair, 0)

    def finish_rows(r0):
        rows = pl.ds(r0, BLK)
        act[rows, HL:D] = (outA[rows, 0:HL] * 0.125).astype(BF)
        dh[rows, 0:HL] = outA[rows, HL:D].astype(BF)

    def dn1_rows(r0):
        rows = pl.ds(r0, BLK)
        return nt(act[rows, 0:HL], wqkv[0]) + nt(act[rows, HL:D], wqkv[1]) + nt(dh[rows, 0:HL], wqkv[2])

    att_back(t, False)

    flush(ccp)
    flush([yb, xb])
    for q in (zc, xc, yc):
        flush(q.values())
    ar = {}

    def gA(s, r0, n):
        if s == 4:
            return Wd.at[0, pl.ds(r0, n), 0:HL]
        return Wu.at[s // 2, pl.ds(r0, n), (s % 2) * HL : (s % 2) * HL + HL]

    cbase = al(c * HL, 128)
    xbase = al(c * HL + x * 192, 64)
    XFIRST = (True, True, True, True, True)

    def blk_z(s, k):
        if XFIRST[s]:
            return al(xbase + zk[k] * 48, 16), 48
        return al(cbase + zk[k] * 96, 32), 96

    def spot_of(s):
        if XFIRST[s]:
            return al(xbase + z * 48, 16)
        return al(cbase + z * 96 + x * 48, 16)

    def ar_core(s):
        ar[(s, 0)] = xchg(gA(s, al((1 - c) * HL, 128), HL), rA.at[s, 0:HL, :], core)

    def ar_x(s):
        if XFIRST[s]:
            ar[(s, "x")] = xchg(gA(s, al(c * HL + (1 - x) * 192, 64), 192), rA.at[s, 384:576, :], xp)
        else:
            ar[(s, "x")] = xchg(gA(s, al(cbase + z * 96 + (1 - x) * 48, 16), 48), rA.at[s, 672:720, :], xp)

    def ar_xadd(s):
        ar[(s, "x")].wait_recv()
        if XFIRST[s]:
            addto(gA(s, xbase, 192), rA.at[s, 384:576, :])
        else:
            addto(gA(s, spot_of(s), 48), rA.at[s, 672:720, :])

    def ar_z1(s):
        o = 576 if XFIRST[s] else 384
        for i, k in ((0, 1), (1, 3)):
            r0, n = blk_z(s, k)
            ar[(s, "z1", i)] = xchg(gA(s, r0, n), rA.at[s, o + i * n : o + i * n + n, :], z1)

    def ar_z1add(s):
        o = 576 if XFIRST[s] else 384
        for i, k in ((0, 0), (1, 2)):
            r0, n = blk_z(s, k)
            ar[(s, "z1", i)].wait_recv()
            addto(gA(s, r0, n), rA.at[s, o + i * n : o + i * n + n, :])

    def ar_z2(s):
        o = 672 if XFIRST[s] else 576
        r0, n = blk_z(s, 2)
        ar[(s, "z2")] = xchg(gA(s, r0, n), rA.at[s, o : o + n, :], z2)

    def ar_z2add(s):
        o = 672 if XFIRST[s] else 576
        r0, n = blk_z(s, 0)
        ar[(s, "z2")].wait_recv()
        addto(gA(s, r0, n), rA.at[s, o : o + n, :])

    def ar_begin(s):
        ar[(s, 0)].wait_recv()
        addto(gA(s, cbase, HL), rA.at[s, 0:HL, :])
        (ar_x if XFIRST[s] else ar_z1)(s)

    def ar_step2(s):
        if XFIRST[s]:
            ar_xadd(s)
            ar_z1(s)
        else:
            ar_z1add(s)
            ar_z2(s)

    def ar_step3(s):
        if XFIRST[s]:
            ar_z1add(s)
            ar_z2(s)
        else:
            ar_z2add(s)
            ar_x(s)

    def ar_fin(s):
        (ar_z2add if XFIRST[s] else ar_xadd)(s)

    def fslot(s, r0, n):
        return fS.at[s, pl.ds(r0, n), :]

    def ag_z2(s):
        r0, n = blk_z(s, 0)
        f = fslot(s, r0, n)
        ar[(s, "g2")] = xchg(f, f, z2)
        ar[(s, "g1")] = xchg(f, f, z1)

    def ag_z1(s):
        ar[(s, "g2")].wait_recv()
        r0, n = blk_z(s, 2)
        f = fslot(s, r0, n)
        ar[(s, "g3")] = xchg(f, f, z1)

    def ag_zend(s):
        ar[(s, "g1")].wait_recv()
        ar[(s, "g3")].wait_recv()

    def ag_x(s):
        f = fslot(s, xbase, 192) if XFIRST[s] else fslot(s, spot_of(s), 48)
        ar[(s, "gx")] = xchg(f, f, xp)

    def ag_begin(s):
        r0 = spot_of(s)
        fslot(s, r0, 48)[...] = gA(s, r0, 48)[...]
        (ag_z2 if XFIRST[s] else ag_x)(s)

    def ag_step2(s):
        if XFIRST[s]:
            ag_z1(s)
        else:
            ar[(s, "gx")].wait_recv()
            ag_z2(s)

    def ag_step3(s):
        if XFIRST[s]:
            ag_zend(s)
            ag_x(s)
        else:
            ag_z1(s)

    def ag_core(s):
        if XFIRST[s]:
            ar[(s, "gx")].wait_recv()
        else:
            ag_zend(s)
        f = fslot(s, cbase, HL)
        ar[(s, "gc")] = xchg(f, fA.at[s, pl.ds(cbase, HL), :], core)
        load(f, fA.at[s, pl.ds(cbase, HL), :])

    for s, tt in ((3, t), (4, 1 - t)):
        gp = tn(attF[tt], n2[0:H, :])
        gA(s, 0, HL)[...] = gp[:, 0:HL].astype(BF)
        gA(s, HL, HL)[...] = gp[:, HL:D].astype(BF)
        ar_core(s)
    rs_z3((0, 0, 0))
    cda[0].wait_recv()
    att_back(1 - t, True)
    rs_z2((1, 0, 0))
    rs_z1(1, 1)
    cda[1].wait_recv()
    att_back(1 - t, False)

    flush([cO])
    cdn = []
    for o in (1 - t, t):
        r0 = al(oth + o * BLK, BLK)
        finish_rows(r0)
        rows = pl.ds(al(H + o * BLK, BLK), BLK)
        n2[rows, :] = dn1_rows(r0).astype(BF)
        cdn.append(xchg(n2.at[rows, :], rN.at[pl.ds(al(o * BLK, BLK), BLK), :], yp))
    for s in (3, 4):
        ar_begin(s)
    rs_z3((1, 0, 0))
    rs_z2((1, 1, 0))
    att_back(t, True)
    rs_z1(0, 1)
    for b in range(2):
        finish_rows(al(own + b * BLK, BLK))

    def gw(s, src):
        def body(m, carry):
            rows = pl.ds(al(m * BLK, BLK), BLK)
            gA(s, al(m * BLK, BLK), BLK)[...] = nn(nT[rows, :], src[...]).astype(BF)
            return carry

        lax.fori_loop(0, 3, body, 0)
        ar_core(s)

    gw(0, act.at[:, 0:HL])
    gw(1, act.at[:, HL:D])
    ar_begin(0)
    gw(2, dh.at[:, 0:HL])
    ar_begin(1)
    ar_begin(2)
    rs_z3((1, 1, 0))
    rs_xlast()

    vecA[0] = jnp.zeros((16, D), F32)
    for i, row in ((3, sp), (4, s2g), (5, s2b), (6, sd)):
        vecA[0, i : i + 1, :] = row
    vecA[0, pl.ds(8 + 2 * tr[0] + c, 1), :] = bsums[0]
    vecA[0, pl.ds(8 + 2 * tr[1] + c, 1), :] = bsums[1]
    vecA[0, pl.ds(12 + t, 1), 0:HL] = rowsum(act[:, 0:HL].astype(F32))
    vecA[0, pl.ds(12 + t, 1), HL:D] = rowsum(dh[:, 0:HL].astype(F32))
    stok, s1g, s1b = zrow, zrow, zrow
    cgin = []
    for i, o in enumerate((t, 1 - t)):
        o0 = al(o * BLK, BLK)
        r0 = al(own + o0, BLK)
        rows = pl.ds(r0, BLK)
        orow = pl.ds(o0, BLK)
        cdn[i].wait_recv()
        dnb = dn1_rows(r0) + rN[orow, :].astype(F32)
        m, v = start_rows(r0)
        cent, r = stats(v)
        xhat = cent * r
        dst = mid[orow, :] + norm_back(xhat, r, dnb, ln1g)
        ginS[orow, :] = jnp.where(m, 0.0, dst).astype(BF)
        stok = stok + rowsum(jnp.where(m, dst, 0.0))
        s1g = s1g + rowsum(dnb * xhat)
        s1b = s1b + rowsum(dnb)
        if i == 1:
            for n, row in ((0, stok), (1, s1g), (2, s1b)):
                vecA[0, n : n + 1, :] = row
            cv = xchg(vecA.at[0], vR.at[0], core)
        cgin.append(xchg(ginS.at[orow, :], gin.at[rows, :], yp))
        load(ginS.at[orow, :], gin.at[rows, :])
        if i == 0:
            ar_step2(0)
            rs_z2((0, 1, 0))
            ar_step2(3)
            ar_step2(4)
            ar_step2(1)
            rs_y(1)
            ar_step2(2)
            ar_step3(0)

    def sum_step(i, to):
        cv.wait_recv()
        vecA[i] = vecA[i - 1] + vR[i - 1]
        return xchg(vecA.at[i], vR.at[i], to)

    ar_step3(3)
    ar_step3(4)
    ar_step3(1)
    rs_z3((0, 1, 0))
    ar_fin(0)
    ag_begin(0)
    ar_step3(2)
    ar_fin(3)
    ar_fin(4)
    cgp = xchg(gA(4, spot_of(4), 48), rgp, yp)
    mixed_send(3)
    cv = sum_step(1, xp)
    ar_fin(1)
    ag_begin(1)
    ag_step2(0)
    ar_fin(2)
    ag_begin(2)
    ag_step2(1)
    ag_step3(0)
    cgp.wait_recv()
    addto(gA(3, spot_of(3), 48), rgp)
    ag_begin(3)
    cv = sum_step(2, z1)
    ag_step2(2)
    ag_step3(1)
    rs_y(0)
    ag_core(0)
    ag_step2(3)
    ag_step3(2)
    cv = sum_step(3, z2)
    ag_core(1)
    ag_step3(3)
    rs_c(0)
    rs_c(1)
    cv = sum_step(4, yp)
    ag_core(2)
    ag_core(3)
    rs_end(0)
    rs_end(1)
    cv.wait_recv()
    vout[...] = vecA[4] + vR[4]
    for s in range(4):
        ar[(s, "gc")].wait_recv()
    for cp in cmix + cgin:
        cp.wait_recv()
    flush([cp for cp, _ in pending])
    for cp in loads[4:]:
        cp.wait()


def scratch():
    def v(shape, dt):
        return pltpu.VMEM(shape, dt)

    return [
        v((T, D), BF), v((D, T), BF), v((3, T, HL), BF), v((T, HL), BF), v((2, H, HL), BF), v((2, HL, D), BF),
        v((2, D, D), BF), v((2, D, D), BF), v((H, D), F32), v((T, D), BF), v((T, D), BF), v((D, T), BF),
        v((T, D), F32), v((T, D), F32), v((H, D), BF), v((H, D), BF), v((T, D), BF), v((T, D), BF),
        v((2, 2, 4, 96, D), BF), v((2, 2, 4, 96, D), BF),
        v((2, 2, 9, 96, D), BF), v((2, 96, D), BF), v((2, 96, D), BF), v((2, 96, D), BF),
        v((2, 96, D), F32), v((2, 48, D), F32), v((T, HL), BF), v((48, HL), BF), v((5, 720, HL), BF),
        v((8, T), F32), v((2, 8, D), F32), v((5, 16, D), F32), v((5, 16, D), F32),
        v((T, D), BF), v((3, D, HL), BF), v((T, 128), jnp.int32), v((1, T), jnp.int32), v((8, D), F32),
        v((H, D), BF), v((H, D), BF), v((4, D, HL), BF), v((2, 48, 2 * D), F32),
        pltpu.SemaphoreType.DMA((XCH,)), pltpu.SemaphoreType.DMA((XCH,)), pltpu.SemaphoreType.DMA((20,)),
    ]


def finish(mixed, gin, fa, gup, gdn, vs, o_mixed, o_gin, o_tok, o_g1, o_b1, o_qkv, o_bqv, o_proj, o_bp, o_g2, o_b2, o_up,
           o_bup, o_dn, o_bd, gb, gf, fb, ff, pf, mb, ub, sem):
    t = lax.axis_index("tensor")
    count = [0]

    def copy(src, dst):
        cp = pltpu.make_async_copy(src, dst, sem.at[count[0]])
        count[0] += 1
        cp.start()
        return cp

    gc = [copy(gin.at[b * BLK : b * BLK + BLK, :], gb.at[b * BLK : b * BLK + BLK, :]) for b in range(4)]
    fc = [copy(fa.at[s], fb.at[s]) for s in range(4)]
    through = [(copy(mixed, mb), mb, o_mixed), (copy(gup, ub.at[0]), ub.at[0], o_up), (copy(gdn, ub.at[1]), ub.at[1], o_dn)]
    out = []
    for i, o in enumerate((o_tok, o_g1, o_b1, o_bp, o_g2, o_b2, o_bd)):
        o[...] = vs[i : i + 1, :].reshape(D)
    for i in range(2):
        o_bup[i * D : i * D + D] = vs[pl.ds(8 + 2 * t + i, 1), :].reshape(D)
        o_bqv[i : i + 1, :] = vs[pl.ds(12 + t, 1), i * HL : i * HL + HL]
    for b in range(4):
        gc[b].wait()
        rows = slice(b * BLK, b * BLK + BLK)
        gf[rows, :] = gb[rows, :].astype(F32)
        out.append(copy(gf.at[rows, :], o_gin.at[rows, :]))
    for cp, here, there in through:
        cp.wait()
        out.append(copy(here, there))
    for s in range(4):
        fc[s].wait()
        if s < 3:
            ff[s] = fb[s].astype(F32)
            out.append(copy(ff.at[s], o_qkv.at[s]))
        else:
            pf[:, 0:HL] = fb[3, 0:HL, :].astype(F32)
            pf[:, HL:D] = fb[3, HL:D, :].astype(F32)
            out.append(copy(pf, o_proj))
    for cp in out:
        cp.wait()


def on_device(
    patches, image_ids, valid, mask_pos, mask_token, ln1_gain, ln1_bias, w_qkv, b_qv, w_proj, b_proj,
    ln2_gain, ln2_bias, w_up, b_up, w_down, b_down, cotangent,
):
    vm = pl.BlockSpec(memory_space=pltpu.VMEM)
    hbm = pl.BlockSpec(memory_space=pl.ANY)
    sds = jax.ShapeDtypeStruct
    parts = pl.pallas_call(
        mega,
        out_shape=(
            sds((T, D), BF), sds((T, D), BF), sds((4, D, HL), BF), sds((48, 2 * D), F32), sds((48, 2 * D), F32),
            sds((16, D), F32),
        ),
        in_specs=[hbm if i in (0, 11, 13, 17) else vm for i in range(18)],
        out_specs=(hbm,) * 5 + (vm,),
        scratch_shapes=scratch(),
        compiler_params=pltpu.CompilerParams(collective_id=0, has_side_effects=True, vmem_limit_bytes=66584576),
        name="block",
    )(
        patches, image_ids, valid, mask_pos, mask_token, ln1_gain, ln1_bias, b_proj, ln2_gain, ln2_bias, b_down,
        jnp.transpose(w_qkv, (1, 0, 2)), b_qv, w_proj, w_up, w_down.T, b_up, cotangent,
    )
    row = sds((D,), F32)
    big = {0, 1, 5, 7, 11, 13}
    outs = pl.pallas_call(
        finish,
        out_shape=(
            sds((T, D), BF), sds((T, D), F32), row, row, row, sds((3, D, HL), F32), sds((2, HL), F32), sds((HL, D), F32),
            row, row, row, sds((48, 2 * D), F32), sds((2 * D,), F32), sds((48, 2 * D), F32), row,
        ),
        in_specs=[hbm] * 5 + [vm],
        out_specs=tuple(hbm if i in big else vm for i in range(15)),
        scratch_shapes=[
            pltpu.VMEM((T, D), BF), pltpu.VMEM((T, D), F32), pltpu.VMEM((4, D, HL), BF), pltpu.VMEM((3, D, HL), F32),
            pltpu.VMEM((HL, D), F32), pltpu.VMEM((T, D), BF), pltpu.VMEM((2, 48, 2 * D), F32),
            pltpu.SemaphoreType.DMA((24,)),
        ],
        compiler_params=pltpu.CompilerParams(vmem_limit_bytes=66584576),
        name="finish",
    )(*parts)
    outs = list(outs)
    outs[5] = jnp.transpose(outs[5], (1, 0, 2))
    outs[13] = outs[13].T
    return tuple(outs)


HEAD_DIM = 64


def norm_rows(values, gain, shift):
    mean = jnp.mean(values, axis=-1, keepdims=True)
    cent = values - mean
    var = jnp.mean(cent * cent, axis=-1, keepdims=True)
    return cent * lax.rsqrt(var + EPS) * gain + shift


def left_dot(first, second):
    return lax.dot_general(
        first, second, (((0,), (0,)), ((), ())), preferred_element_type=jnp.float32
    )


def right_dot(first, second):
    return lax.dot_general(
        first, second, (((1,), (1,)), ((), ())), preferred_element_type=jnp.float32
    )


def allowed_rows(ids, live, begin, count):
    rows = ids.shape[0]
    own_ids = lax.dynamic_slice_in_dim(ids, begin, count, 0)
    places = begin + jnp.arange(count)
    same_place = places[:, None] == jnp.arange(rows)[None, :]
    return (own_ids[:, None] == ids[None, :]) & ((live[None, :] == 1) | same_place)


def spread(
    patches,
    image_ids,
    valid,
    mask_pos,
    mask_token,
    ln1_gain,
    ln1_bias,
    w_qkv,
    b_qv,
    w_proj,
    b_proj,
    ln2_gain,
    ln2_bias,
    w_up,
    b_up,
    w_down,
    b_down,
    cotangent,
):
    rows = patches.shape[0]
    local_width = w_qkv.shape[2]
    local_heads = local_width // HEAD_DIM
    scale = 1.0 / HEAD_DIM**0.5
    ids = image_ids[0]
    live = valid[0]
    masked = mask_pos[0][:, None] == 1
    block = min(512, rows)
    blocks = rows // block
    start = jnp.where(masked, mask_token.astype(jnp.float32)[None, :], patches.astype(jnp.float32))
    normed, norm1_pull = jax.vjp(
        norm_rows, start, ln1_gain.astype(jnp.float32), ln1_bias.astype(jnp.float32)
    )
    normed_b = normed.astype(jnp.bfloat16)
    qv_bias = b_qv.astype(jnp.float32)
    bias = jnp.stack([qv_bias[0], jnp.zeros_like(qv_bias[0]), qv_bias[1]])
    qkv = jnp.einsum("td,dsc->tsc", normed_b, w_qkv, preferred_element_type=jnp.float32)
    qkv_b = (qkv + bias[None]).astype(jnp.bfloat16)
    query = qkv_b[:, 0].reshape(rows, local_heads, HEAD_DIM)
    keys = qkv_b[:, 1].reshape(rows, local_heads, HEAD_DIM)
    values = qkv_b[:, 2].reshape(rows, local_heads, HEAD_DIM)
    outputs = []
    totals = []
    for index in range(blocks):
        begin = index * block
        query_part = query[begin : begin + block]
        allowed = allowed_rows(ids, live, begin, block)
        scores = (
            jnp.einsum("qhc,khc->hqk", query_part, keys, preferred_element_type=jnp.float32) * scale
        )
        scores = jnp.where(allowed[None], scores, -1e30)
        top = jnp.max(scores, axis=-1, keepdims=True)
        expd = jnp.exp(scores - top)
        summed = jnp.sum(expd, axis=-1, keepdims=True)
        probs_b = (expd / summed).astype(jnp.bfloat16)
        totals.append(top + jnp.log(summed))
        outputs.append(
            jnp.einsum("hqk,khc->qhc", probs_b, values, preferred_element_type=jnp.float32)
        )
    attended_b = jnp.concatenate(outputs, axis=0).reshape(rows, local_width).astype(jnp.bfloat16)
    attn_part = jnp.dot(attended_b, w_proj, preferred_element_type=jnp.float32)
    ln2_gain_f = ln2_gain.astype(jnp.float32)
    ln2_bias_f = ln2_bias.astype(jnp.float32)
    attn_total = lax.psum(attn_part, "tensor")
    middle = start + attn_total + b_proj.astype(jnp.float32)
    normed2, norm2_pull = jax.vjp(norm_rows, middle, ln2_gain_f, ln2_bias_f)
    normed2_b = normed2.astype(jnp.bfloat16)
    up_full, down_full = (
        lax.all_gather(w_up, "dp", axis=0, tiled=True),
        lax.all_gather(w_down, "dp", axis=1, tiled=True),
    )
    hidden = jnp.dot(normed2_b, up_full, preferred_element_type=jnp.float32) + b_up.astype(
        jnp.float32
    )
    active, gelu_pull = jax.vjp(partial(jax.nn.gelu, approximate=False), hidden)
    active_b = active.astype(jnp.bfloat16)
    mlp_part = jnp.dot(active_b, down_full, preferred_element_type=jnp.float32)
    mlp_total = lax.psum(mlp_part.astype(jnp.bfloat16), "tensor").astype(jnp.float32)
    mixed = (middle + mlp_total + b_down.astype(jnp.float32)).astype(jnp.bfloat16)
    seed_grad = cotangent.astype(jnp.float32)
    up_back, down_back = (up_full, down_full)
    grad_b_down = jnp.sum(seed_grad, axis=0)
    grad_down_local = left_dot(active_b, cotangent)
    grad_active = right_dot(cotangent, down_back)
    (grad_hidden,) = gelu_pull(grad_active)
    grad_hidden_b = grad_hidden.astype(jnp.bfloat16)
    grad_b_up = jnp.sum(grad_hidden_b.astype(jnp.float32), axis=0)
    grad_up_local = left_dot(normed2_b, grad_hidden_b)
    grad_normed2_part = right_dot(grad_hidden_b, up_back)
    grad_normed2 = lax.psum(grad_normed2_part, "tensor")
    grad_mid_norm, grad_ln2_gain, grad_ln2_bias = norm2_pull(grad_normed2)
    grad_middle = seed_grad + grad_mid_norm
    grad_w_up, grad_w_down = (
        lax.psum_scatter(grad_up_local, "dp", scatter_dimension=0, tiled=True),
        lax.psum_scatter(grad_down_local, "dp", scatter_dimension=1, tiled=True),
    )
    grad_branch_b = grad_middle.astype(jnp.bfloat16)
    grad_b_proj = jnp.sum(grad_branch_b.astype(jnp.float32), axis=0)
    grad_w_proj = left_dot(attended_b, grad_branch_b)
    grad_attended = (
        right_dot(grad_branch_b, w_proj).astype(jnp.bfloat16).reshape(rows, local_heads, HEAD_DIM)
    )
    grad_query_parts = []
    grad_keys = jnp.zeros((rows, local_heads, HEAD_DIM), jnp.float32)
    grad_values = jnp.zeros((rows, local_heads, HEAD_DIM), jnp.float32)
    for index in range(blocks):
        begin = index * block
        query_part = query[begin : begin + block]
        grad_out_part = grad_attended[begin : begin + block]
        allowed = allowed_rows(ids, live, begin, block)
        scores = (
            jnp.einsum("qhc,khc->hqk", query_part, keys, preferred_element_type=jnp.float32) * scale
        )
        scores = jnp.where(allowed[None], scores, -1e30)
        probs = jnp.exp(scores - totals[index])
        probs_b = probs.astype(jnp.bfloat16)
        grad_values = grad_values + jnp.einsum(
            "hqk,qhc->khc", probs_b, grad_out_part, preferred_element_type=jnp.float32
        )
        grad_probs = jnp.einsum(
            "qhc,khc->hqk", grad_out_part, values, preferred_element_type=jnp.float32
        )
        inner = jnp.sum(probs * grad_probs, axis=-1, keepdims=True)
        grad_scores_b = (probs * (grad_probs - inner)).astype(jnp.bfloat16)
        grad_query_parts.append(
            jnp.einsum("hqk,khc->qhc", grad_scores_b, keys, preferred_element_type=jnp.float32)
            * scale
        )
        grad_keys = (
            grad_keys
            + jnp.einsum(
                "hqk,qhc->khc", grad_scores_b, query_part, preferred_element_type=jnp.float32
            )
            * scale
        )
    grad_query = jnp.concatenate(grad_query_parts, axis=0)
    grad_qkv_b = (
        jnp.stack([grad_query, grad_keys, grad_values], axis=1)
        .reshape(rows, 3, local_width)
        .astype(jnp.bfloat16)
    )
    grad_qkv_f = grad_qkv_b.astype(jnp.float32)
    grad_b_qv = jnp.stack([jnp.sum(grad_qkv_f[:, 0], axis=0), jnp.sum(grad_qkv_f[:, 2], axis=0)])
    grad_w_qkv = jnp.einsum("td,tsc->dsc", normed_b, grad_qkv_b, preferred_element_type=jnp.float32)
    grad_normed_part = jnp.einsum(
        "tsc,dsc->td", grad_qkv_b, w_qkv, preferred_element_type=jnp.float32
    )
    grad_normed = lax.psum(grad_normed_part.astype(jnp.bfloat16), "tensor").astype(jnp.float32)
    grad_start_norm, grad_ln1_gain, grad_ln1_bias = norm1_pull(grad_normed)
    grad_start = grad_middle + grad_start_norm
    grad_input = jnp.where(masked, 0.0, grad_start)
    grad_token = jnp.sum(jnp.where(masked, grad_start, 0.0), axis=0)
    summed = lax.psum(
        (
            grad_token,
            grad_ln1_gain,
            grad_ln1_bias,
            grad_w_qkv,
            grad_b_qv,
            grad_w_proj,
            grad_b_proj,
            grad_ln2_gain,
            grad_ln2_bias,
            grad_b_up,
            grad_b_down,
        ),
        "dp",
    )
    return (
        mixed,
        grad_input,
        summed[0],
        summed[1],
        summed[2],
        summed[3],
        summed[4],
        summed[5],
        summed[6],
        summed[7],
        summed[8],
        grad_w_up,
        summed[9],
        grad_w_down,
        summed[10],
    )


def solution(mesh):
    placed = (
        P("dp", None),
        P("dp", None),
        P("dp", None),
        P("dp", None),
        P(),
        P(),
        P(),
        P(None, None, "tensor"),
        P(None, "tensor"),
        P("tensor", None),
        P(),
        P(),
        P(),
        P("dp", "tensor"),
        P("tensor"),
        P("tensor", "dp"),
        P(),
        P("dp", None),
    )
    fits = mesh.shape["dp"] == 16 and mesh.shape["tensor"] == 2
    return jax.shard_map(
        on_device if fits else spread,
        mesh=mesh,
        in_specs=placed,
        out_specs=(
            P("dp", None),
            P("dp", None),
            P(),
            P(),
            P(),
            P(None, None, "tensor"),
            P(None, "tensor"),
            P("tensor", None),
            P(),
            P(),
            P(),
            P("dp", "tensor"),
            P("tensor"),
            P("tensor", "dp"),
            P(),
        ),
        check_vma=False,
    )
```

```python
from functools import partial

import jax
import jax.numpy as jnp
from jax import lax
from jax.experimental import pallas as pl
from jax.experimental.pallas import tpu as pltpu
from jax.sharding import PartitionSpec as P

BF = jnp.bfloat16
F32 = jnp.float32
MESH = pl.DeviceIdType.MESH
EPS = 1e-06
T = 1024
H = 512
D = 768
HL = 384
BLK = 256
WIN = 768
CUT = 640
SENT, LANDED, LOCAL = 148, 143, 16


def nn(a, b):
    return lax.dot_general(a, b, (((1,), (0,)), ((), ())), preferred_element_type=F32)


def nt(a, b):
    return lax.dot_general(a, b, (((1,), (1,)), ((), ())), preferred_element_type=F32)


def tn(a, b):
    return lax.dot_general(a, b, (((0,), (0,)), ((), ())), preferred_element_type=F32)


def rowsum(v):
    return jnp.sum(v, axis=0, keepdims=True)


def lane_half(shape):
    return lax.broadcasted_iota(jnp.int32, shape, 1) < 64


def stats(v):
    mean = jnp.sum(v, axis=-1, keepdims=True) * (1.0 / D)
    cent = v - mean
    var = jnp.sum(cent * cent, axis=-1, keepdims=True) * (1.0 / D)
    return cent, lax.rsqrt(var + EPS)


def norm_back(xhat, r, d, gain):
    e = d * gain
    m1 = jnp.sum(e, axis=-1, keepdims=True) * (1.0 / D)
    m2 = jnp.sum(e * xhat, axis=-1, keepdims=True) * (1.0 / D)
    return r * (e - m1 - xhat * m2)


def mega(
    patches, ids, live, hidden_pos, token_b, ln1g_b, ln1b_b, bproj_b, ln2g_b, ln2b_b, bdown_b, wqkv_h, bqv_b, wproj,
    up, dn, bup, cot,
    mixed, gin, fA, gup, gdn, vout,
    n1, nT, qkv, attO, attF, wpf, Wu, Wd, mid, n2, dml, dmlT, outA, dn2A, rO, rN, act, dh, gU, gD,
    rG, rX, sy, ry, sc, rc, dO, rgp, rA, lseT, bupA, vecA, vR, pat, wqkv, codec, coder, vec, mixS, ginS, fS,
    gS, ssem, rsem, lsem,
):
    d = lax.axis_index("dp")
    t = lax.axis_index("tensor")
    z = lax.div(d, 4)
    x = lax.rem(lax.div(d, 2), 2)
    c = lax.rem(d, 2)
    zk = (z, z + 1 - 2 * lax.rem(z, 2), lax.rem(z + 2, 4), 3 - z)
    xr = (x, 1 - x)
    tr = (t, 1 - t)

    def dev(zz, xx, cc, tt):
        return ((zz * 2 + xx) * 2 + cc, tt)

    core = dev(z, x, 1 - c, t)
    xp = dev(z, 1 - x, c, t)
    yp = dev(z, x, c, 1 - t)
    z1 = dev(zk[1], x, c, t)
    z2 = dev(zk[2], x, c, t)
    z3 = dev(zk[3], x, c, t)
    mid_z = (z == 1) | (z == 2)
    end_z = (z == 0) | (z == 3)

    pending = []
    flushed = set()
    slots = [0]

    def slot():
        slots[0] += 1
        return slots[0] - 1

    def xchg(src, dst, to, when=None, land=None):
        i = len(pending)
        cp = pltpu.make_async_remote_copy(
            src_ref=src, dst_ref=dst, send_sem=ssem.at[i], recv_sem=rsem.at[slot() if land is None else land],
            device_id=to, device_id_type=MESH,
        )
        pending.append((cp, when))
        if when is None:
            cp.start()
        else:
            pl.when(when)(cp.start)
        return cp

    def landed(dst, land, frm):
        pltpu.make_async_remote_copy(
            src_ref=dst, dst_ref=dst, send_sem=ssem.at[0], recv_sem=rsem.at[land], device_id=frm, device_id_type=MESH
        ).wait_recv()

    def flush(cps):
        cps = set(id(cp) for cp in cps)
        for cp, when in pending:
            if id(cp) in cps and id(cp) not in flushed:
                flushed.add(id(cp))
                if when is None:
                    cp.wait_send()
                else:
                    pl.when(when)(cp.wait_send)

    def al(v, m):
        return pl.multiple_of(v, m)

    bar = pltpu.get_barrier_semaphore()
    peers = (core, xp, yp, z1, z2, z3)
    for p in peers:
        pl.semaphore_signal(bar, inc=1, device_id=p, device_id_type=MESH)
    loads = []

    def load(src, dst):
        cp = pltpu.make_async_copy(src, dst, lsem.at[len(loads)])
        cp.start()
        loads.append(cp)
        return cp

    lpat = load(patches, pat)
    lwq = load(wqkv_h, wqkv)
    code = ids[...] + 16 * live[...] + 32 * hidden_pos[...]
    coder[...] = code
    codec[...] = jnp.broadcast_to(code.astype(F32), (128, T)).T.astype(jnp.int32)
    for i, row in enumerate((token_b, ln1g_b, ln1b_b, bproj_b, ln2g_b, ln2b_b, bdown_b)):
        vec[i : i + 1, :] = row[...].astype(F32).reshape(1, D)
    bqv = bqv_b[...].astype(F32)
    bupA[0] = jnp.zeros((8, D), F32)
    for i in range(2):
        bupA[0, i : i + 1, :] = bup[i * D : i * D + D].astype(F32).reshape(1, D)
    pl.semaphore_wait(bar, len(peers))

    own = al(t * H, H)
    oth = al((1 - t) * H, H)
    cslot = al(c * H, H)
    sslot = al((1 - c) * H, H)
    W = (Wu, Wd)
    shards = (up, dn)

    def wblk(a, k, xx, yy):
        return W[a].at[tr[yy], pl.ds(al((zk[k] * 2 + xr[xx]) * 96, 32), 96), :]

    ccp = []
    mine = al((z * 2 + x) * 96 + c * 48, 16)
    for a in (0, 1):
        ccp.append(
            xchg(shards[a].at[:, pl.ds(al((1 - c) * D, 128), D)], W[a].at[t, pl.ds(mine, 48), :], core)
        )
    whalf = pl.ds(al(c * 192, 64), 192)
    cwp = xchg(wproj.at[whalf, :], wpf.at[t, whalf, :], yp)
    cbup = xchg(bupA.at[0, pl.ds(c, 1), :], bupA.at[1, pl.ds(c, 1), :], yp)
    cdml = xchg(cot.at[pl.ds(own, H), :], dml.at[pl.ds(cslot, H), :], core)
    ldml = load(cot.at[pl.ds(own, H), :], dml.at[pl.ds(cslot, H), :])
    lwp = load(wproj, wpf.at[t])
    for a in (0, 1):
        W[a][t, pl.ds(mine, 48), :] = shards[a][:, pl.ds(al(c * D, 128), D)]

    zc, xc, yc = {}, {}, {}

    chains = {
        "u": lambda k: wblk(0, k, 0, 0),
        "d": lambda k: wblk(1, k, 0, 0),
        "e": lambda k: wblk(1, k, 0, 1),
        "b": lambda k: Wu.at[tr[1], pl.ds(al(zk[k] * 192, 64), 192), CUT:D],
    }

    def zsend(q, k):
        zc[(q, k)] = xchg(chains[q](0), chains[q](0), z1 if k == 1 else z2)

    def zstart(q):
        zsend(q, 1)
        zsend(q, 2)

    def zstep(q):
        zc[(q, 2)].wait_recv()
        zc[(q, 3)] = xchg(chains[q](2), chains[q](2), z1)

    def zend(q):
        zc[(q, 3)].wait_recv()

    def xsend(a, k, yy):
        xc[(a, k, yy)] = xchg(wblk(a, k, 0, yy), wblk(a, k, 0, yy), xp)

    def ysend(a, k, xx):
        ref = wblk(a, k, xx, 0)
        if a == 0:
            ref = W[0].at[t, pl.ds(al((zk[k] * 2 + xr[xx]) * 96, 32), 96), 0:CUT]
        yc[(a, k, xx)] = xchg(ref, ref, yp)

    def bown(tt):
        return W[0].at[tt, pl.ds(al((z * 2 + x) * 96, 32), 96), CUT:D]

    token = vec[0:1, :]
    ln1g = vec[1:2, :]
    ln1b = vec[2:3, :]

    def start_rows(r0):
        m = lax.shift_right_logical(codec[pl.ds(r0, BLK), 0:1], 5) == 1
        return m, jnp.where(m, token, pat[pl.ds(r0, BLK), :].astype(F32))

    def ln1_block(b, carry):
        r0 = al(b * BLK, BLK)
        _, v = start_rows(r0)
        cent, r = stats(v)
        nb = (cent * r * ln1g + ln1b).astype(BF)
        n1[pl.ds(r0, BLK), :] = nb
        for s in range(3):
            y = nn(nb, wqkv[s])
            if s == 0:
                y = y + bqv[0:1, :]
            if s == 2:
                y = y + bqv[1:2, :]
            qkv[s, pl.ds(r0, BLK), :] = y.astype(BF)
        return carry

    lpat.wait()
    lwq.wait()
    lax.fori_loop(0, 1, ln1_block, 0)
    for a in (0, 1):
        ccp[a].wait_recv()
    zstart("u")
    zsend("d", 1)
    xsend(0, 0, 0)
    xsend(1, 0, 0)
    lax.fori_loop(1, 4, ln1_block, 0)

    def masked_pair(block, scale=None):
        low = lane_half(block.shape)
        zero = jnp.zeros_like(block)
        if scale is not None:
            block = block * jnp.asarray(scale, BF)
        return jnp.where(low, block, zero), jnp.where(low, zero, block)

    def att_block(half, edge):
        qb = half * 3 if edge else 1 + half
        win = H if edge else WIN
        r0 = al(qb * BLK, BLK)
        ws = al(half * H if edge else half * BLK, BLK)
        cr = codec[pl.ds(r0, BLK), 0:1]
        cw = coder[:, pl.ds(ws, win)]
        rid = r0 + lax.broadcasted_iota(jnp.int32, (BLK, win), 0)
        cid = ws + lax.broadcasted_iota(jnp.int32, (BLK, win), 1)
        ok = ((cr & 15) == (cw & 15)) & (((cw & 16) == 16) | (rid == cid))
        dn2A[0:BLK, 0:win] = jnp.where(ok, 0.0, -1e30)
        lane = lax.broadcasted_iota(jnp.int32, (BLK, 128), 1)

        def pair(p, lacc):
            cols = pl.ds(al(p * 128, 128), 128)
            qs = masked_pair(qkv[0, pl.ds(r0, BLK), cols], 0.125)
            kp = qkv[1, pl.ds(ws, win), cols]
            vp = qkv[2, pl.ds(ws, win), cols]
            outs = []
            for h in range(2):
                s = nt(qs[h], kp) + dn2A[0:BLK, 0:win]
                top = jnp.max(s, axis=-1, keepdims=True)
                e = jnp.exp(s - top)
                l = jnp.sum(e, axis=-1, keepdims=True)
                o = nn(e.astype(BF), vp) * (1.0 / l)
                outs.append(o)
                lacc = jnp.where(lane == (2 * p + h), top + jnp.log(l), lacc)
            attO[pl.ds(r0, BLK), cols] = jnp.where(lane_half((BLK, 128)), outs[0], outs[1]).astype(BF)
            return lacc

        lacc = lax.fori_loop(0, 3, pair, jnp.zeros((BLK, 128), F32))
        lseT[:, pl.ds(r0, BLK)] = lacc.T[0:8, :]
        return r0

    catt = []

    def att_send(r0):
        catt.append(xchg(attO.at[pl.ds(r0, BLK), :], attF.at[t, pl.ds(al(r0 - oth, BLK), BLK), :], yp))

    att_send(att_block(1 - t, True))
    att_send(att_block(1 - t, False))
    ysend(1, 0, 0)
    yb = xchg(bown(t), bown(t), yp)
    zc[("u", 1)].wait_recv()
    xsend(0, 1, 0)
    zstep("u")
    zsend("d", 2)
    xsend(0, 2, 0)
    cwp.wait_recv()
    cwc = xchg(wpf.at[1 - t, whalf, :], wpf.at[1 - t, whalf, :], core)
    for k in range(3):
        ysend(0, k, 0)
    att_block(t, True)
    att_block(t, False)
    attF[t] = attO[pl.ds(own, H), :]
    zend("u")
    xsend(0, 3, 0)
    zc[("d", 1)].wait_recv()
    xsend(1, 1, 0)
    ysend(0, 3, 0)

    bproj = vec[3:4, :]
    ln2g = vec[4:5, :]
    ln2b = vec[5:6, :]
    bdown = vec[6:7, :]
    ldml.wait()
    lwp.wait()
    for cp in catt:
        cp.wait_recv()
    cwc.wait_recv()

    def mid_block(b, carry):
        o0 = al(b * BLK, BLK)
        _, v = start_rows(al(own + o0, BLK))
        m = v + (nn(attF[0, pl.ds(o0, BLK), :], wpf[0]) + nn(attF[1, pl.ds(o0, BLK), :], wpf[1])) + bproj
        mid[pl.ds(o0, BLK), :] = m
        cent, r = stats(m)
        n2[pl.ds(al(cslot + o0, BLK), BLK), :] = (cent * r * ln2g + ln2b).astype(BF)
        return carry

    lax.fori_loop(0, 2, mid_block, 0)
    cn2 = xchg(n2.at[pl.ds(cslot, H), :], n2.at[pl.ds(cslot, H), :], core)
    zstep("d")
    xsend(1, 2, 0)
    yc[(1, 0, 0)].wait_recv()
    zstart("e")
    yb.wait_recv()
    xb = xchg(bown(1 - t), bown(1 - t), xp)
    cdml.wait_recv()
    cn2.wait_recv()
    nT[...] = n2[...].T
    dmlT[...] = dml[...].T
    cbup.wait_recv()
    for k in range(4):
        xc[(0, k, 0)].wait_recv()
        ysend(0, k, 1)
    zend("d")
    xsend(1, 3, 0)
    xsend(1, 0, 1)

    G = (gU, gD)
    rs = {}

    def addto(dst, src):
        dst[...] = (dst[...].astype(F32) + src[...].astype(F32)).astype(BF)

    def rs_x(a, j):
        rs[(a, j)] = [xchg(G[a].at[j, 1, h * 2 : h * 2 + 2], rG.at[a, j, h * 2 : h * 2 + 2], xp) for h in (0, 1)]

    rland = {(r, q): slot() for r in ((0, 0, 0), (0, 0, 1), (0, 1, 0), (1, 0, 0), (1, 1, 0)) for q in range(4, 9)}

    def rslot(r, q):
        a, j, xx = r
        if xx == 0:
            return rG.at[a, j, q]
        return rX.at[0] if q == 8 else rG.at[a, j, q - 4]

    def gblk(r, k):
        a, j, xx = r
        return G[a].at[j, xx, zk[k]]

    def rpass(r, k, to, q, when):
        xchg(gblk(r, k), rslot(r, q), to, when, rland[(r, q)])

    def radd(r, k, q):
        landed(rslot(r, q), rland[(r, q)], z1)
        addto(gblk(r, k), rslot(r, q))

    def rs_z0(r):
        for k, q in ((3, 4), (2, 5), (1, 6)):
            rpass(r, k, z1, q, end_z)

    def rs_z1(a, j):
        for cp in rs[(a, j)]:
            cp.wait_recv()
        for zz in range(4):
            addto(G[a].at[j, 0, zz], rG.at[a, j, zz])
        rs_z0((a, j, 0))

    def rs_z2(r):
        pl.when(mid_z)(partial(radd, r, 2, 4))
        rpass(r, 2, z3, 7, mid_z)
        pl.when(mid_z)(partial(radd, r, 3, 5))
        rpass(r, 3, z3, 8, mid_z)

    def rs_z3(r):
        pl.when(mid_z)(partial(radd, r, 1, 7))
        rpass(r, 1, z1, 8, mid_z)

    def rs_zsum(r):
        pl.when(mid_z)(partial(radd, r, 0, 6))
        radd(r, 0, 8)

    def rs_xlast():
        rs_zsum((0, 0, 1))
        rs["xlast"] = xchg(gblk((0, 0, 1), 0), rX.at[1], xp)

    def rs_sum(a, j):
        rs_zsum((a, j, 0))
        total = gblk((a, j, 0), 0)[...].astype(F32)
        if (a, j) == (0, 0):
            rs["xlast"].wait_recv()
            total = total + rX[1].astype(F32)
        return total

    def rs_y(a):
        sy[a] = rs_sum(a, 1).astype(BF)
        rs[(a, "y")] = xchg(sy.at[a], ry.at[a], yp)

    def rs_c(a):
        total = rs_sum(a, 0)
        rs[(a, "y")].wait_recv()
        sc[a] = total + ry[a].astype(F32)
        rs[(a, "c")] = xchg(sc.at[a, pl.ds(al((1 - c) * 48, 16), 48), :], rc.at[a], core)

    def rs_end(a):
        gS[a, :, pl.ds(al(c * D, 128), D)] = sc[a, pl.ds(al(c * 48, 16), 48), :]
        rs[(a, "c")].wait_recv()
        gS[a, :, pl.ds(al((1 - c) * D, 128), D)] = rc[a]
        load(gS.at[a], (gup, gdn)[a])

    bsums = []

    def ff_act(j):
        yy = tr[j]
        bu = bupA[j, pl.ds(c, 1), :]

        def block(b, carry):
            rows = pl.ds(al(b * BLK, BLK), BLK)
            hid = nn(n2[rows, :], Wu[yy]) + bu
            phi = 0.5 * (1.0 + lax.erf(hid * 0.7071067811865476))
            a = (hid * phi).astype(BF)
            act[rows, :] = a
            dh[rows, :] = (phi + hid * (jnp.exp(hid * hid * -0.5) * 0.3989422804014327)).astype(BF)
            return carry

        lax.fori_loop(0, 4, block, 0)

    def ff_out(j):
        yy = tr[j]

        def block(b, carry):
            rows = pl.ds(al(b * BLK, BLK), BLK)
            o = nt(act[rows, :], Wd[yy])
            if j == 0:
                outA[rows, :] = o
            else:
                outA[rows, :] += o
            return carry

        lax.fori_loop(0, 4, block, 0)

    def ff_bwd(j):
        yy = tr[j]

        def block(b, carry):
            rows = pl.ds(al(b * BLK, BLK), BLK)
            dhid = (nn(dml[rows, :], Wd[yy]) * dh[rows, :].astype(F32)).astype(BF)
            dh[rows, :] = dhid
            g = nt(dhid, Wu[yy])
            if j == 0:
                dn2A[rows, :] = g
            else:
                dn2A[rows, :] += g
            return carry + rowsum(dhid.astype(F32))

        bsums.append(lax.fori_loop(0, 4, block, jnp.zeros((1, D), F32)))

    def ff_grads(j, left, right, out):
        def gw_block(b, carry):
            r = nn(left[pl.ds(al(b * 192, 64), 192), :], right[...]).astype(BF)
            for xa in range(2):
                out[j, lax.rem(xa + x, 2), b] = r[xa * 96 : xa * 96 + 96]
            return carry

        lax.fori_loop(0, 4, gw_block, 0)

    def ff_gu(j):
        ff_grads(j, nT, dh, gU)

    def ff_gd(j):
        ff_grads(j, dmlT, act, gD)

    zrow = jnp.zeros((1, D), F32)
    ff_act(0)
    xb.wait_recv()
    zstart("b")
    ff_gd(0)
    zc[("e", 1)].wait_recv()
    xsend(1, 1, 1)
    for k in range(4):
        xc[(1, k, 0)].wait_recv()
    ff_out(0)
    zstep("e")
    xsend(1, 2, 1)
    ff_bwd(0)
    zstep("b")
    zend("e")
    xsend(1, 3, 1)
    rs_x(1, 0)
    ff_gu(0)
    rs_z0((0, 0, 1))
    rs_z0((0, 0, 0))
    zc[("b", 1)].wait_recv()
    zend("b")
    for k in range(4):
        yc[(0, k, 0)].wait_recv()
        yc[(0, k, 1)].wait_recv()
    ff_act(1)
    ff_gd(1)
    rs_x(1, 1)
    for k in range(4):
        xc[(1, k, 1)].wait_recv()
    ff_bwd(1)

    flush([cn2])
    n2[0:H, :] = dn2A[pl.ds(sslot, H), :].astype(BF)
    cN = xchg(n2.at[0:H, :], rN, core)
    ff_out(1)
    n2[H:T, :] = outA[pl.ds(sslot, H), :].astype(BF)
    cO = xchg(n2.at[H:T, :], rO, core)
    rs_z2((0, 0, 1))
    ff_gu(1)
    rs_x(0, 1)
    flush(catt)
    cN.wait_recv()
    flush([cN])

    sums = [zrow, zrow, zrow, zrow]
    cda = []
    for o in (t, 1 - t):
        o0 = al(o * BLK, BLK)
        rows = pl.ds(o0, BLK)
        crow = pl.ds(al(cslot + o0, BLK), BLK)
        dnb = dn2A[crow, :] + rN[rows, :].astype(F32)
        cent, r = stats(mid[rows, :])
        xhat = cent * r
        ct = dml[crow, :].astype(F32)
        dm = ct + norm_back(xhat, r, dnb, ln2g)
        db = dm.astype(BF)
        n2[rows, :] = db
        attO[rows, :] = nt(db, wpf[1 - t]).astype(BF)
        orow = pl.ds(al(own + o0, BLK), BLK)
        cda.append(xchg(attO.at[rows, :], dO.at[orow, :], yp))
        dO[orow, :] = nt(db, wpf[t]).astype(BF)
        dn2A[crow, :] = dm
        for i, term in enumerate((dnb * xhat, dnb, db.astype(F32), ct)):
            sums[i] = sums[i] + rowsum(term)
    s2g, s2b, sp, sd = sums

    cO.wait_recv()
    cmix = []

    def mixed_block(o):
        o0 = al(o * BLK, BLK)
        rows = pl.ds(o0, BLK)
        crow = pl.ds(al(cslot + o0, BLK), BLK)
        out = mid[rows, :] + (outA[crow, :] + rO[rows, :].astype(F32)) + bdown
        mixS[rows, :] = out.astype(BF)
        mid[rows, :] = dn2A[crow, :]

    def mixed_send(i):
        orow = pl.ds(own + i * 128, 128)
        rows = slice(i * 128, i * 128 + 128)
        cmix.append(xchg(mixS.at[rows, :], mixed.at[orow, :], yp))
        load(mixS.at[rows, :], mixed.at[orow, :])

    mixed_block(0)
    mixed_block(1)
    mixed_send(0)
    mixed_send(1)
    mixed_send(2)
    rs_z3((0, 0, 1))
    rs_z2((0, 0, 0))
    outA[...] = jnp.zeros((T, D), F32)
    nT[...] = n1[...].T
    rs_z1(1, 0)

    def att_back(half, edge):
        qb = half * 3 if edge else 1 + half
        wl = H if edge else WIN
        r0 = al(qb * BLK, BLK)
        ws = al(half * H if edge else half * BLK, BLK)
        cw = codec[pl.ds(ws, wl), 0:1]
        cr = coder[:, pl.ds(r0, BLK)]
        rid = r0 + lax.broadcasted_iota(jnp.int32, (wl, BLK), 1)
        cid = ws + lax.broadcasted_iota(jnp.int32, (wl, BLK), 0)
        ok = ((cr & 15) == (cw & 15)) & (((cw & 16) == 16) | (rid == cid))
        dn2A[0:wl, 0:BLK] = jnp.where(ok, 0.0, -1e30)
        rows = pl.ds(r0, BLK)
        win = pl.ds(ws, wl)

        def pair(p, carry):
            cols = pl.ds(al(p * 128, 128), 128)
            vcols = pl.ds(al(HL + p * 128, 128), 128)
            qp = qkv[0, rows, cols]
            op = dO[rows, cols]
            qs = masked_pair(qp, 0.125)
            os = masked_pair(op)
            kp = qkv[1, win, cols]
            vp = qkv[2, win, cols]
            dqs, dks, dvs = [], [], []
            for h in range(2):
                lse = lseT[pl.ds(2 * p + h, 1), rows]
                pr = jnp.exp(nt(kp, qs[h]) + dn2A[0:wl, 0:BLK] - lse)
                dp = nt(vp, os[h])
                inner = rowsum(pr * dp)
                ds = (pr * (dp - inner)).astype(BF)
                dvs.append(nn(pr.astype(BF), op))
                dks.append(nn(ds, qp))
                dqs.append(tn(ds, kp))
            low = lane_half((BLK, 128))
            lowk = lane_half((wl, 128))
            act[rows, cols] = (jnp.where(low, dqs[0], dqs[1]) * 0.125).astype(BF)
            outA[win, cols] += jnp.where(lowk, dks[0], dks[1])
            outA[win, vcols] += jnp.where(lowk, dvs[0], dvs[1])
            return carry

        lax.fori_loop(0, 3, pair, 0)

    def finish_rows(r0):
        rows = pl.ds(r0, BLK)
        act[rows, HL:D] = (outA[rows, 0:HL] * 0.125).astype(BF)
        dh[rows, 0:HL] = outA[rows, HL:D].astype(BF)

    def dn1_rows(r0):
        rows = pl.ds(r0, BLK)
        return nt(act[rows, 0:HL], wqkv[0]) + nt(act[rows, HL:D], wqkv[1]) + nt(dh[rows, 0:HL], wqkv[2])

    att_back(t, False)

    flush(ccp)
    flush([yb, xb])
    for q in (zc, xc, yc):
        flush(q.values())
    ar = {}

    def gA(s, r0, n):
        if s == 4:
            return Wd.at[0, pl.ds(r0, n), 0:HL]
        return Wu.at[s // 2, pl.ds(r0, n), (s % 2) * HL : (s % 2) * HL + HL]

    cbase = al(c * HL, 128)
    xbase = al(c * HL + x * 192, 64)
    XFIRST = (True, True, True, True, True)

    def blk_z(s, k):
        if XFIRST[s]:
            return al(xbase + zk[k] * 48, 16), 48
        return al(cbase + zk[k] * 96, 32), 96

    def spot_of(s):
        if XFIRST[s]:
            return al(xbase + z * 48, 16)
        return al(cbase + z * 96 + x * 48, 16)

    def ar_core(s):
        ar[(s, 0)] = xchg(gA(s, al((1 - c) * HL, 128), HL), rA.at[s, 0:HL, :], core)

    def ar_x(s):
        if XFIRST[s]:
            ar[(s, "x")] = xchg(gA(s, al(c * HL + (1 - x) * 192, 64), 192), rA.at[s, 384:576, :], xp)
        else:
            ar[(s, "x")] = xchg(gA(s, al(cbase + z * 96 + (1 - x) * 48, 16), 48), rA.at[s, 672:720, :], xp)

    def ar_xadd(s):
        ar[(s, "x")].wait_recv()
        if XFIRST[s]:
            addto(gA(s, xbase, 192), rA.at[s, 384:576, :])
        else:
            addto(gA(s, spot_of(s), 48), rA.at[s, 672:720, :])

    def ar_z1(s):
        o = 576 if XFIRST[s] else 384
        for i, k in ((0, 1), (1, 3)):
            r0, n = blk_z(s, k)
            ar[(s, "z1", i)] = xchg(gA(s, r0, n), rA.at[s, o + i * n : o + i * n + n, :], z1)

    def ar_z1add(s):
        o = 576 if XFIRST[s] else 384
        for i, k in ((0, 0), (1, 2)):
            r0, n = blk_z(s, k)
            ar[(s, "z1", i)].wait_recv()
            addto(gA(s, r0, n), rA.at[s, o + i * n : o + i * n + n, :])

    def ar_z2(s):
        o = 672 if XFIRST[s] else 576
        r0, n = blk_z(s, 2)
        ar[(s, "z2")] = xchg(gA(s, r0, n), rA.at[s, o : o + n, :], z2)

    def ar_z2add(s):
        o = 672 if XFIRST[s] else 576
        r0, n = blk_z(s, 0)
        ar[(s, "z2")].wait_recv()
        addto(gA(s, r0, n), rA.at[s, o : o + n, :])

    def ar_begin(s):
        ar[(s, 0)].wait_recv()
        addto(gA(s, cbase, HL), rA.at[s, 0:HL, :])
        (ar_x if XFIRST[s] else ar_z1)(s)

    def ar_step2(s):
        if XFIRST[s]:
            ar_xadd(s)
            ar_z1(s)
        else:
            ar_z1add(s)
            ar_z2(s)

    def ar_step3(s):
        if XFIRST[s]:
            ar_z1add(s)
            ar_z2(s)
        else:
            ar_z2add(s)
            ar_x(s)

    def ar_fin(s):
        (ar_z2add if XFIRST[s] else ar_xadd)(s)

    def fslot(s, r0, n):
        return fS.at[s, pl.ds(r0, n), :]

    def ag_z2(s):
        r0, n = blk_z(s, 0)
        f = fslot(s, r0, n)
        ar[(s, "g2")] = xchg(f, f, z2)
        ar[(s, "g1")] = xchg(f, f, z1)

    def ag_z1(s):
        ar[(s, "g2")].wait_recv()
        r0, n = blk_z(s, 2)
        f = fslot(s, r0, n)
        ar[(s, "g3")] = xchg(f, f, z1)

    def ag_zend(s):
        ar[(s, "g1")].wait_recv()
        ar[(s, "g3")].wait_recv()

    def ag_x(s):
        f = fslot(s, xbase, 192) if XFIRST[s] else fslot(s, spot_of(s), 48)
        ar[(s, "gx")] = xchg(f, f, xp)

    def ag_begin(s):
        r0 = spot_of(s)
        fslot(s, r0, 48)[...] = gA(s, r0, 48)[...]
        (ag_z2 if XFIRST[s] else ag_x)(s)

    def ag_step2(s):
        if XFIRST[s]:
            ag_z1(s)
        else:
            ar[(s, "gx")].wait_recv()
            ag_z2(s)

    def ag_step3(s):
        if XFIRST[s]:
            ag_zend(s)
            ag_x(s)
        else:
            ag_z1(s)

    def ag_core(s):
        if XFIRST[s]:
            ar[(s, "gx")].wait_recv()
        else:
            ag_zend(s)
        f = fslot(s, cbase, HL)
        ar[(s, "gc")] = xchg(f, fA.at[s, pl.ds(cbase, HL), :], core)
        load(f, fA.at[s, pl.ds(cbase, HL), :])

    for s, tt in ((3, t), (4, 1 - t)):
        gp = tn(attF[tt], n2[0:H, :])
        gA(s, 0, HL)[...] = gp[:, 0:HL].astype(BF)
        gA(s, HL, HL)[...] = gp[:, HL:D].astype(BF)
        ar_core(s)
    rs_z3((0, 0, 0))
    cda[0].wait_recv()
    att_back(1 - t, True)
    rs_z2((1, 0, 0))
    rs_z1(1, 1)
    cda[1].wait_recv()
    att_back(1 - t, False)

    flush([cO])
    cdn = []
    for o in (1 - t, t):
        r0 = al(oth + o * BLK, BLK)
        finish_rows(r0)
        rows = pl.ds(al(H + o * BLK, BLK), BLK)
        n2[rows, :] = dn1_rows(r0).astype(BF)
        cdn.append(xchg(n2.at[rows, :], rN.at[pl.ds(al(o * BLK, BLK), BLK), :], yp))
    for s in (3, 4):
        ar_begin(s)
    rs_z3((1, 0, 0))
    rs_z2((1, 1, 0))
    att_back(t, True)
    rs_z1(0, 1)
    for b in range(2):
        finish_rows(al(own + b * BLK, BLK))

    def gw(s, src):
        def body(m, carry):
            rows = pl.ds(al(m * BLK, BLK), BLK)
            gA(s, al(m * BLK, BLK), BLK)[...] = nn(nT[rows, :], src[...]).astype(BF)
            return carry

        lax.fori_loop(0, 3, body, 0)
        ar_core(s)

    gw(0, act.at[:, 0:HL])
    gw(1, act.at[:, HL:D])
    ar_begin(0)
    gw(2, dh.at[:, 0:HL])
    ar_begin(1)
    ar_begin(2)
    rs_z3((1, 1, 0))
    rs_xlast()

    vecA[0] = jnp.zeros((16, D), F32)
    for i, row in ((3, sp), (4, s2g), (5, s2b), (6, sd)):
        vecA[0, i : i + 1, :] = row
    vecA[0, pl.ds(8 + 2 * tr[0] + c, 1), :] = bsums[0]
    vecA[0, pl.ds(8 + 2 * tr[1] + c, 1), :] = bsums[1]
    vecA[0, pl.ds(12 + t, 1), 0:HL] = rowsum(act[:, 0:HL].astype(F32))
    vecA[0, pl.ds(12 + t, 1), HL:D] = rowsum(dh[:, 0:HL].astype(F32))
    stok, s1g, s1b = zrow, zrow, zrow
    cgin = []
    for i, o in enumerate((t, 1 - t)):
        o0 = al(o * BLK, BLK)
        r0 = al(own + o0, BLK)
        rows = pl.ds(r0, BLK)
        orow = pl.ds(o0, BLK)
        cdn[i].wait_recv()
        dnb = dn1_rows(r0) + rN[orow, :].astype(F32)
        m, v = start_rows(r0)
        cent, r = stats(v)
        xhat = cent * r
        dst = mid[orow, :] + norm_back(xhat, r, dnb, ln1g)
        ginS[orow, :] = jnp.where(m, 0.0, dst).astype(BF)
        stok = stok + rowsum(jnp.where(m, dst, 0.0))
        s1g = s1g + rowsum(dnb * xhat)
        s1b = s1b + rowsum(dnb)
        if i == 1:
            for n, row in ((0, stok), (1, s1g), (2, s1b)):
                vecA[0, n : n + 1, :] = row
            cv = xchg(vecA.at[0], vR.at[0], core)
        cgin.append(xchg(ginS.at[orow, :], gin.at[rows, :], yp))
        load(ginS.at[orow, :], gin.at[rows, :])
        if i == 0:
            ar_step2(0)
            rs_z2((0, 1, 0))
            ar_step2(3)
            ar_step2(4)
            ar_step2(1)
            rs_y(1)
            ar_step2(2)
            ar_step3(0)

    def sum_step(i, to):
        cv.wait_recv()
        vecA[i] = vecA[i - 1] + vR[i - 1]
        return xchg(vecA.at[i], vR.at[i], to)

    ar_step3(3)
    ar_step3(4)
    ar_step3(1)
    rs_z3((0, 1, 0))
    ar_fin(0)
    ag_begin(0)
    ar_step3(2)
    ar_fin(3)
    ar_fin(4)
    cgp = xchg(gA(4, spot_of(4), 48), rgp, yp)
    mixed_send(3)
    cv = sum_step(1, xp)
    ar_fin(1)
    ag_begin(1)
    ag_step2(0)
    ar_fin(2)
    ag_begin(2)
    ag_step2(1)
    ag_step3(0)
    cgp.wait_recv()
    addto(gA(3, spot_of(3), 48), rgp)
    ag_begin(3)
    cv = sum_step(2, z1)
    ag_step2(2)
    ag_step3(1)
    rs_y(0)
    ag_core(0)
    ag_step2(3)
    ag_step3(2)
    cv = sum_step(3, z2)
    ag_core(1)
    ag_step3(3)
    rs_c(0)
    rs_c(1)
    cv = sum_step(4, yp)
    ag_core(2)
    ag_core(3)
    rs_end(0)
    rs_end(1)
    cv.wait_recv()
    vout[...] = vecA[4] + vR[4]
    for s in range(4):
        ar[(s, "gc")].wait_recv()
    for cp in cmix + cgin:
        cp.wait_recv()
    flush([cp for cp, _ in pending])
    for cp in loads[4:]:
        cp.wait()
    assert (len(pending), slots[0], len(loads)) == (SENT, LANDED, LOCAL)


def scratch():
    def v(shape, dt):
        return pltpu.VMEM(shape, dt)

    return [
        v((T, D), BF), v((D, T), BF), v((3, T, HL), BF), v((T, HL), BF), v((2, H, HL), BF), v((2, HL, D), BF),
        v((2, D, D), BF), v((2, D, D), BF), v((H, D), F32), v((T, D), BF), v((T, D), BF), v((D, T), BF),
        v((T, D), F32), v((T, D), F32), v((H, D), BF), v((H, D), BF), v((T, D), BF), v((T, D), BF),
        v((2, 2, 4, 96, D), BF), v((2, 2, 4, 96, D), BF),
        v((2, 2, 9, 96, D), BF), v((2, 96, D), BF), v((2, 96, D), BF), v((2, 96, D), BF),
        v((2, 96, D), F32), v((2, 48, D), F32), v((T, HL), BF), v((48, HL), BF), v((5, 720, HL), BF),
        v((8, T), F32), v((2, 8, D), F32), v((5, 16, D), F32), v((5, 16, D), F32),
        v((T, D), BF), v((3, D, HL), BF), v((T, 128), jnp.int32), v((1, T), jnp.int32), v((8, D), F32),
        v((H, D), BF), v((H, D), BF), v((4, D, HL), BF), v((2, 48, 2 * D), F32),
        pltpu.SemaphoreType.DMA((SENT,)), pltpu.SemaphoreType.DMA((LANDED,)), pltpu.SemaphoreType.DMA((LOCAL,)),
    ]


def finish(mixed, gin, fa, gup, gdn, vs, o_mixed, o_gin, o_tok, o_g1, o_b1, o_qkv, o_bqv, o_proj, o_bp, o_g2, o_b2, o_up,
           o_bup, o_dn, o_bd, gb, gf, fb, ff, pf, mb, ub, sem):
    t = lax.axis_index("tensor")
    count = [0]

    def copy(src, dst):
        cp = pltpu.make_async_copy(src, dst, sem.at[count[0]])
        count[0] += 1
        cp.start()
        return cp

    fc = [copy(fa.at[s], fb.at[s]) for s in range(4)]
    gc = [copy(gin.at[b * BLK : b * BLK + BLK, :], gb.at[b * BLK : b * BLK + BLK, :]) for b in range(4)]
    through = [(copy(mixed, mb), mb, o_mixed), (copy(gup, ub.at[0]), ub.at[0], o_up), (copy(gdn, ub.at[1]), ub.at[1], o_dn)]
    out = []
    for i, o in enumerate((o_tok, o_g1, o_b1, o_bp, o_g2, o_b2, o_bd)):
        o[...] = vs[i : i + 1, :].reshape(D)
    for i in range(2):
        o_bup[i * D : i * D + D] = vs[pl.ds(8 + 2 * t + i, 1), :].reshape(D)
        o_bqv[i : i + 1, :] = vs[pl.ds(12 + t, 1), i * HL : i * HL + HL]
    for b in range(4):
        gc[b].wait()
        rows = slice(b * BLK, b * BLK + BLK)
        gf[rows, :] = gb[rows, :].astype(F32)
        out.append(copy(gf.at[rows, :], o_gin.at[rows, :]))
    for cp, here, there in through:
        cp.wait()
        out.append(copy(here, there))
    for s in range(4):
        fc[s].wait()
        if s < 3:
            ff[s] = fb[s].astype(F32)
            out.append(copy(ff.at[s], o_qkv.at[s]))
        else:
            pf[:, 0:HL] = fb[3, 0:HL, :].astype(F32)
            pf[:, HL:D] = fb[3, HL:D, :].astype(F32)
            out.append(copy(pf, o_proj))
    for cp in out:
        cp.wait()


def on_device(
    patches, image_ids, valid, mask_pos, mask_token, ln1_gain, ln1_bias, w_qkv, b_qv, w_proj, b_proj,
    ln2_gain, ln2_bias, w_up, b_up, w_down, b_down, cotangent,
):
    vm = pl.BlockSpec(memory_space=pltpu.VMEM)
    hbm = pl.BlockSpec(memory_space=pl.ANY)
    sds = jax.ShapeDtypeStruct
    parts = pl.pallas_call(
        mega,
        out_shape=(
            sds((T, D), BF), sds((T, D), BF), sds((4, D, HL), BF), sds((48, 2 * D), F32), sds((48, 2 * D), F32),
            sds((16, D), F32),
        ),
        in_specs=[hbm if i in (0, 11, 13, 17) else vm for i in range(18)],
        out_specs=(hbm,) * 5 + (vm,),
        scratch_shapes=scratch(),
        compiler_params=pltpu.CompilerParams(collective_id=0, has_side_effects=True, vmem_limit_bytes=66584576),
        name="block",
    )(
        patches, image_ids, valid, mask_pos, mask_token, ln1_gain, ln1_bias, b_proj, ln2_gain, ln2_bias, b_down,
        jnp.transpose(w_qkv, (1, 0, 2)), b_qv, w_proj, w_up, w_down.T, b_up, cotangent,
    )
    row = sds((D,), F32)
    big = {0, 1, 5, 7, 11, 13}
    outs = pl.pallas_call(
        finish,
        out_shape=(
            sds((T, D), BF), sds((T, D), F32), row, row, row, sds((3, D, HL), F32), sds((2, HL), F32), sds((HL, D), F32),
            row, row, row, sds((48, 2 * D), F32), sds((2 * D,), F32), sds((48, 2 * D), F32), row,
        ),
        in_specs=[hbm] * 5 + [vm],
        out_specs=tuple(hbm if i in big else vm for i in range(15)),
        scratch_shapes=[
            pltpu.VMEM((T, D), BF), pltpu.VMEM((T, D), F32), pltpu.VMEM((4, D, HL), BF), pltpu.VMEM((3, D, HL), F32),
            pltpu.VMEM((HL, D), F32), pltpu.VMEM((T, D), BF), pltpu.VMEM((2, 48, 2 * D), F32),
            pltpu.SemaphoreType.DMA((22,)),
        ],
        compiler_params=pltpu.CompilerParams(vmem_limit_bytes=66584576),
        name="finish",
    )(*parts)
    outs = list(outs)
    outs[5] = jnp.transpose(outs[5], (1, 0, 2))
    outs[13] = outs[13].T
    return tuple(outs)


HEAD_DIM = 64


def norm_rows(values, gain, shift):
    mean = jnp.mean(values, axis=-1, keepdims=True)
    cent = values - mean
    var = jnp.mean(cent * cent, axis=-1, keepdims=True)
    return cent * lax.rsqrt(var + EPS) * gain + shift


def left_dot(first, second):
    return lax.dot_general(
        first, second, (((0,), (0,)), ((), ())), preferred_element_type=jnp.float32
    )


def right_dot(first, second):
    return lax.dot_general(
        first, second, (((1,), (1,)), ((), ())), preferred_element_type=jnp.float32
    )


def allowed_rows(ids, live, begin, count):
    rows = ids.shape[0]
    own_ids = lax.dynamic_slice_in_dim(ids, begin, count, 0)
    places = begin + jnp.arange(count)
    same_place = places[:, None] == jnp.arange(rows)[None, :]
    return (own_ids[:, None] == ids[None, :]) & ((live[None, :] == 1) | same_place)


def spread(
    patches,
    image_ids,
    valid,
    mask_pos,
    mask_token,
    ln1_gain,
    ln1_bias,
    w_qkv,
    b_qv,
    w_proj,
    b_proj,
    ln2_gain,
    ln2_bias,
    w_up,
    b_up,
    w_down,
    b_down,
    cotangent,
):
    rows = patches.shape[0]
    local_width = w_qkv.shape[2]
    local_heads = local_width // HEAD_DIM
    scale = 1.0 / HEAD_DIM**0.5
    ids = image_ids[0]
    live = valid[0]
    masked = mask_pos[0][:, None] == 1
    block = min(512, rows)
    blocks = rows // block
    start = jnp.where(masked, mask_token.astype(jnp.float32)[None, :], patches.astype(jnp.float32))
    normed, norm1_pull = jax.vjp(
        norm_rows, start, ln1_gain.astype(jnp.float32), ln1_bias.astype(jnp.float32)
    )
    normed_b = normed.astype(jnp.bfloat16)
    qv_bias = b_qv.astype(jnp.float32)
    bias = jnp.stack([qv_bias[0], jnp.zeros_like(qv_bias[0]), qv_bias[1]])
    qkv = jnp.einsum("td,dsc->tsc", normed_b, w_qkv, preferred_element_type=jnp.float32)
    qkv_b = (qkv + bias[None]).astype(jnp.bfloat16)
    query = qkv_b[:, 0].reshape(rows, local_heads, HEAD_DIM)
    keys = qkv_b[:, 1].reshape(rows, local_heads, HEAD_DIM)
    values = qkv_b[:, 2].reshape(rows, local_heads, HEAD_DIM)
    outputs = []
    totals = []
    for index in range(blocks):
        begin = index * block
        query_part = query[begin : begin + block]
        allowed = allowed_rows(ids, live, begin, block)
        scores = (
            jnp.einsum("qhc,khc->hqk", query_part, keys, preferred_element_type=jnp.float32) * scale
        )
        scores = jnp.where(allowed[None], scores, -1e30)
        top = jnp.max(scores, axis=-1, keepdims=True)
        expd = jnp.exp(scores - top)
        summed = jnp.sum(expd, axis=-1, keepdims=True)
        probs_b = (expd / summed).astype(jnp.bfloat16)
        totals.append(top + jnp.log(summed))
        outputs.append(
            jnp.einsum("hqk,khc->qhc", probs_b, values, preferred_element_type=jnp.float32)
        )
    attended_b = jnp.concatenate(outputs, axis=0).reshape(rows, local_width).astype(jnp.bfloat16)
    attn_part = jnp.dot(attended_b, w_proj, preferred_element_type=jnp.float32)
    ln2_gain_f = ln2_gain.astype(jnp.float32)
    ln2_bias_f = ln2_bias.astype(jnp.float32)
    attn_total = lax.psum(attn_part, "tensor")
    middle = start + attn_total + b_proj.astype(jnp.float32)
    normed2, norm2_pull = jax.vjp(norm_rows, middle, ln2_gain_f, ln2_bias_f)
    normed2_b = normed2.astype(jnp.bfloat16)
    up_full, down_full = (
        lax.all_gather(w_up, "dp", axis=0, tiled=True),
        lax.all_gather(w_down, "dp", axis=1, tiled=True),
    )
    hidden = jnp.dot(normed2_b, up_full, preferred_element_type=jnp.float32) + b_up.astype(
        jnp.float32
    )
    active, gelu_pull = jax.vjp(partial(jax.nn.gelu, approximate=False), hidden)
    active_b = active.astype(jnp.bfloat16)
    mlp_part = jnp.dot(active_b, down_full, preferred_element_type=jnp.float32)
    mlp_total = lax.psum(mlp_part.astype(jnp.bfloat16), "tensor").astype(jnp.float32)
    mixed = (middle + mlp_total + b_down.astype(jnp.float32)).astype(jnp.bfloat16)
    seed_grad = cotangent.astype(jnp.float32)
    up_back, down_back = (up_full, down_full)
    grad_b_down = jnp.sum(seed_grad, axis=0)
    grad_down_local = left_dot(active_b, cotangent)
    grad_active = right_dot(cotangent, down_back)
    (grad_hidden,) = gelu_pull(grad_active)
    grad_hidden_b = grad_hidden.astype(jnp.bfloat16)
    grad_b_up = jnp.sum(grad_hidden_b.astype(jnp.float32), axis=0)
    grad_up_local = left_dot(normed2_b, grad_hidden_b)
    grad_normed2_part = right_dot(grad_hidden_b, up_back)
    grad_normed2 = lax.psum(grad_normed2_part, "tensor")
    grad_mid_norm, grad_ln2_gain, grad_ln2_bias = norm2_pull(grad_normed2)
    grad_middle = seed_grad + grad_mid_norm
    grad_w_up, grad_w_down = (
        lax.psum_scatter(grad_up_local, "dp", scatter_dimension=0, tiled=True),
        lax.psum_scatter(grad_down_local, "dp", scatter_dimension=1, tiled=True),
    )
    grad_branch_b = grad_middle.astype(jnp.bfloat16)
    grad_b_proj = jnp.sum(grad_branch_b.astype(jnp.float32), axis=0)
    grad_w_proj = left_dot(attended_b, grad_branch_b)
    grad_attended = (
        right_dot(grad_branch_b, w_proj).astype(jnp.bfloat16).reshape(rows, local_heads, HEAD_DIM)
    )
    grad_query_parts = []
    grad_keys = jnp.zeros((rows, local_heads, HEAD_DIM), jnp.float32)
    grad_values = jnp.zeros((rows, local_heads, HEAD_DIM), jnp.float32)
    for index in range(blocks):
        begin = index * block
        query_part = query[begin : begin + block]
        grad_out_part = grad_attended[begin : begin + block]
        allowed = allowed_rows(ids, live, begin, block)
        scores = (
            jnp.einsum("qhc,khc->hqk", query_part, keys, preferred_element_type=jnp.float32) * scale
        )
        scores = jnp.where(allowed[None], scores, -1e30)
        probs = jnp.exp(scores - totals[index])
        probs_b = probs.astype(jnp.bfloat16)
        grad_values = grad_values + jnp.einsum(
            "hqk,qhc->khc", probs_b, grad_out_part, preferred_element_type=jnp.float32
        )
        grad_probs = jnp.einsum(
            "qhc,khc->hqk", grad_out_part, values, preferred_element_type=jnp.float32
        )
        inner = jnp.sum(probs * grad_probs, axis=-1, keepdims=True)
        grad_scores_b = (probs * (grad_probs - inner)).astype(jnp.bfloat16)
        grad_query_parts.append(
            jnp.einsum("hqk,khc->qhc", grad_scores_b, keys, preferred_element_type=jnp.float32)
            * scale
        )
        grad_keys = (
            grad_keys
            + jnp.einsum(
                "hqk,qhc->khc", grad_scores_b, query_part, preferred_element_type=jnp.float32
            )
            * scale
        )
    grad_query = jnp.concatenate(grad_query_parts, axis=0)
    grad_qkv_b = (
        jnp.stack([grad_query, grad_keys, grad_values], axis=1)
        .reshape(rows, 3, local_width)
        .astype(jnp.bfloat16)
    )
    grad_qkv_f = grad_qkv_b.astype(jnp.float32)
    grad_b_qv = jnp.stack([jnp.sum(grad_qkv_f[:, 0], axis=0), jnp.sum(grad_qkv_f[:, 2], axis=0)])
    grad_w_qkv = jnp.einsum("td,tsc->dsc", normed_b, grad_qkv_b, preferred_element_type=jnp.float32)
    grad_normed_part = jnp.einsum(
        "tsc,dsc->td", grad_qkv_b, w_qkv, preferred_element_type=jnp.float32
    )
    grad_normed = lax.psum(grad_normed_part.astype(jnp.bfloat16), "tensor").astype(jnp.float32)
    grad_start_norm, grad_ln1_gain, grad_ln1_bias = norm1_pull(grad_normed)
    grad_start = grad_middle + grad_start_norm
    grad_input = jnp.where(masked, 0.0, grad_start)
    grad_token = jnp.sum(jnp.where(masked, grad_start, 0.0), axis=0)
    summed = lax.psum(
        (
            grad_token,
            grad_ln1_gain,
            grad_ln1_bias,
            grad_w_qkv,
            grad_b_qv,
            grad_w_proj,
            grad_b_proj,
            grad_ln2_gain,
            grad_ln2_bias,
            grad_b_up,
            grad_b_down,
        ),
        "dp",
    )
    return (
        mixed,
        grad_input,
        summed[0],
        summed[1],
        summed[2],
        summed[3],
        summed[4],
        summed[5],
        summed[6],
        summed[7],
        summed[8],
        grad_w_up,
        summed[9],
        grad_w_down,
        summed[10],
    )


def solution(mesh):
    placed = (
        P("dp", None),
        P("dp", None),
        P("dp", None),
        P("dp", None),
        P(),
        P(),
        P(),
        P(None, None, "tensor"),
        P(None, "tensor"),
        P("tensor", None),
        P(),
        P(),
        P(),
        P("dp", "tensor"),
        P("tensor"),
        P("tensor", "dp"),
        P(),
        P("dp", None),
    )
    fits = mesh.shape["dp"] == 16 and mesh.shape["tensor"] == 2
    return jax.shard_map(
        on_device if fits else spread,
        mesh=mesh,
        in_specs=placed,
        out_specs=(
            P("dp", None),
            P("dp", None),
            P(),
            P(),
            P(),
            P(None, None, "tensor"),
            P(None, "tensor"),
            P("tensor", None),
            P(),
            P(),
            P(),
            P("dp", "tensor"),
            P("tensor"),
            P("tensor", "dp"),
            P(),
        ),
        check_vma=False,
    )
```

```python
from functools import partial

import jax
import jax.numpy as jnp
from jax import lax
from jax.experimental import pallas as pl
from jax.experimental.pallas import tpu as pltpu
from jax.sharding import PartitionSpec as P

BF = jnp.bfloat16
F32 = jnp.float32
MESH = pl.DeviceIdType.MESH
EPS = 1e-06
T = 1024
H = 512
D = 768
HL = 384
BLK = 256
WIN = 768
CUT = 640
SENT, LANDED, LOCAL = 148, 143, 17


def nn(a, b):
    return lax.dot_general(a, b, (((1,), (0,)), ((), ())), preferred_element_type=F32)


def nt(a, b):
    return lax.dot_general(a, b, (((1,), (1,)), ((), ())), preferred_element_type=F32)


def tn(a, b):
    return lax.dot_general(a, b, (((0,), (0,)), ((), ())), preferred_element_type=F32)


def rowsum(v):
    return jnp.sum(v, axis=0, keepdims=True)


def lane_half(shape):
    return lax.broadcasted_iota(jnp.int32, shape, 1) < 64


def stats(v):
    mean = jnp.sum(v, axis=-1, keepdims=True) * (1.0 / D)
    cent = v - mean
    var = jnp.sum(cent * cent, axis=-1, keepdims=True) * (1.0 / D)
    return cent, lax.rsqrt(var + EPS)


def norm_back(xhat, r, d, gain):
    e = d * gain
    m1 = jnp.sum(e, axis=-1, keepdims=True) * (1.0 / D)
    m2 = jnp.sum(e * xhat, axis=-1, keepdims=True) * (1.0 / D)
    return r * (e - m1 - xhat * m2)


def mega(
    patches, ids, live, hidden_pos, token_b, ln1g_b, ln1b_b, bproj_b, ln2g_b, ln2b_b, bdown_b, wqkv_h, bqv_b, wproj,
    up, dn, bup, cot,
    mixed, gin, fA, gup, gdn, vout,
    n1, nT, qkv, attO, attF, wpf, Wu, Wd, mid, n2, dml, dmlT, outA, dn2A, rO, rN, act, dh, gU, gD,
    rG, rX, sy, ry, sc, rc, dO, rgp, rA, lseT, bupA, vecA, vR, pat, wqkv, codec, coder, vec, mixS, ginS, fS,
    gS, ssem, rsem, lsem,
):
    d = lax.axis_index("dp")
    t = lax.axis_index("tensor")
    z = lax.div(d, 4)
    x = lax.rem(lax.div(d, 2), 2)
    c = lax.rem(d, 2)
    zk = (z, z + 1 - 2 * lax.rem(z, 2), lax.rem(z + 2, 4), 3 - z)
    xr = (x, 1 - x)
    tr = (t, 1 - t)

    def dev(zz, xx, cc, tt):
        return ((zz * 2 + xx) * 2 + cc, tt)

    core = dev(z, x, 1 - c, t)
    xp = dev(z, 1 - x, c, t)
    yp = dev(z, x, c, 1 - t)
    z1 = dev(zk[1], x, c, t)
    z2 = dev(zk[2], x, c, t)
    z3 = dev(zk[3], x, c, t)
    mid_z = (z == 1) | (z == 2)
    end_z = (z == 0) | (z == 3)

    pending = []
    flushed = set()
    slots = [0]

    def slot():
        slots[0] += 1
        return slots[0] - 1

    def xchg(src, dst, to, when=None, land=None):
        i = len(pending)
        cp = pltpu.make_async_remote_copy(
            src_ref=src, dst_ref=dst, send_sem=ssem.at[i], recv_sem=rsem.at[slot() if land is None else land],
            device_id=to, device_id_type=MESH,
        )
        pending.append((cp, when))
        if when is None:
            cp.start()
        else:
            pl.when(when)(cp.start)
        return cp

    def landed(dst, land, frm):
        pltpu.make_async_remote_copy(
            src_ref=dst, dst_ref=dst, send_sem=ssem.at[0], recv_sem=rsem.at[land], device_id=frm, device_id_type=MESH
        ).wait_recv()

    def flush(cps):
        cps = set(id(cp) for cp in cps)
        for cp, when in pending:
            if id(cp) in cps and id(cp) not in flushed:
                flushed.add(id(cp))
                if when is None:
                    cp.wait_send()
                else:
                    pl.when(when)(cp.wait_send)

    def al(v, m):
        return pl.multiple_of(v, m)

    bar = pltpu.get_barrier_semaphore()
    peers = (core, xp, yp, z1, z2, z3)
    for p in peers:
        pl.semaphore_signal(bar, inc=1, device_id=p, device_id_type=MESH)
    loads = []

    def load(src, dst):
        cp = pltpu.make_async_copy(src, dst, lsem.at[len(loads)])
        cp.start()
        loads.append(cp)
        return cp

    lpat = load(patches, pat)
    lwq = load(wqkv_h, wqkv)
    code = ids[...] + 16 * live[...] + 32 * hidden_pos[...]
    coder[...] = code
    codec[...] = jnp.broadcast_to(code.astype(F32), (128, T)).T.astype(jnp.int32)
    for i, row in enumerate((token_b, ln1g_b, ln1b_b, bproj_b, ln2g_b, ln2b_b, bdown_b)):
        vec[i : i + 1, :] = row[...].astype(F32).reshape(1, D)
    bqv = bqv_b[...].astype(F32)
    bupA[0] = jnp.zeros((8, D), F32)
    for i in range(2):
        bupA[0, i : i + 1, :] = bup[i * D : i * D + D].astype(F32).reshape(1, D)
    pl.semaphore_wait(bar, len(peers))

    own = al(t * H, H)
    oth = al((1 - t) * H, H)
    cslot = al(c * H, H)
    sslot = al((1 - c) * H, H)
    W = (Wu, Wd)
    shards = (up, dn)

    def wblk(a, k, xx, yy):
        return W[a].at[tr[yy], pl.ds(al((zk[k] * 2 + xr[xx]) * 96, 32), 96), :]

    ccp = []
    mine = al((z * 2 + x) * 96 + c * 48, 16)
    for a in (0, 1):
        ccp.append(
            xchg(shards[a].at[:, pl.ds(al((1 - c) * D, 128), D)], W[a].at[t, pl.ds(mine, 48), :], core)
        )
    whalf = pl.ds(al(c * 192, 64), 192)
    cwp = xchg(wproj.at[whalf, :], wpf.at[t, whalf, :], yp)
    cbup = xchg(bupA.at[0, pl.ds(c, 1), :], bupA.at[1, pl.ds(c, 1), :], yp)
    cdml = xchg(cot.at[pl.ds(own, H), :], dml.at[pl.ds(cslot, H), :], core)
    ldml = load(cot.at[pl.ds(own, H), :], dml.at[pl.ds(cslot, H), :])
    lwp = load(wproj, wpf.at[t])
    for a in (0, 1):
        W[a][t, pl.ds(mine, 48), :] = shards[a][:, pl.ds(al(c * D, 128), D)]

    zc, xc, yc = {}, {}, {}

    chains = {
        "u": lambda k: wblk(0, k, 0, 0),
        "d": lambda k: wblk(1, k, 0, 0),
        "e": lambda k: wblk(1, k, 0, 1),
        "b": lambda k: Wu.at[tr[1], pl.ds(al(zk[k] * 192, 64), 192), CUT:D],
    }

    def zsend(q, k):
        zc[(q, k)] = xchg(chains[q](0), chains[q](0), z1 if k == 1 else z2)

    def zstart(q):
        zsend(q, 1)
        zsend(q, 2)

    def zstep(q):
        zc[(q, 2)].wait_recv()
        zc[(q, 3)] = xchg(chains[q](2), chains[q](2), z1)

    def zend(q):
        zc[(q, 3)].wait_recv()

    def xsend(a, k, yy):
        xc[(a, k, yy)] = xchg(wblk(a, k, 0, yy), wblk(a, k, 0, yy), xp)

    def ysend(a, k, xx):
        ref = wblk(a, k, xx, 0)
        if a == 0:
            ref = W[0].at[t, pl.ds(al((zk[k] * 2 + xr[xx]) * 96, 32), 96), 0:CUT]
        yc[(a, k, xx)] = xchg(ref, ref, yp)

    def bown(tt):
        return W[0].at[tt, pl.ds(al((z * 2 + x) * 96, 32), 96), CUT:D]

    token = vec[0:1, :]
    ln1g = vec[1:2, :]
    ln1b = vec[2:3, :]

    def start_rows(r0):
        m = lax.shift_right_logical(codec[pl.ds(r0, BLK), 0:1], 5) == 1
        return m, jnp.where(m, token, pat[pl.ds(r0, BLK), :].astype(F32))

    def ln1_block(b, carry):
        r0 = al(b * BLK, BLK)
        _, v = start_rows(r0)
        cent, r = stats(v)
        nb = (cent * r * ln1g + ln1b).astype(BF)
        n1[pl.ds(r0, BLK), :] = nb
        for s in range(3):
            y = nn(nb, wqkv[s])
            if s == 0:
                y = y + bqv[0:1, :]
            if s == 2:
                y = y + bqv[1:2, :]
            qkv[s, pl.ds(r0, BLK), :] = y.astype(BF)
        return carry

    lpat.wait()
    lwq.wait()
    lax.fori_loop(0, 1, ln1_block, 0)
    for a in (0, 1):
        ccp[a].wait_recv()
    zstart("u")
    zsend("d", 1)
    xsend(0, 0, 0)
    xsend(1, 0, 0)
    lax.fori_loop(1, 4, ln1_block, 0)

    def masked_pair(block, scale=None):
        low = lane_half(block.shape)
        zero = jnp.zeros_like(block)
        if scale is not None:
            block = block * jnp.asarray(scale, BF)
        return jnp.where(low, block, zero), jnp.where(low, zero, block)

    def att_block(half, edge):
        qb = half * 3 if edge else 1 + half
        win = H if edge else WIN
        r0 = al(qb * BLK, BLK)
        ws = al(half * H if edge else half * BLK, BLK)
        cr = codec[pl.ds(r0, BLK), 0:1]
        cw = coder[:, pl.ds(ws, win)]
        rid = r0 + lax.broadcasted_iota(jnp.int32, (BLK, win), 0)
        cid = ws + lax.broadcasted_iota(jnp.int32, (BLK, win), 1)
        ok = ((cr & 15) == (cw & 15)) & (((cw & 16) == 16) | (rid == cid))
        dn2A[0:BLK, 0:win] = jnp.where(ok, 0.0, -1e30)
        lane = lax.broadcasted_iota(jnp.int32, (BLK, 128), 1)

        def pair(p, lacc):
            cols = pl.ds(al(p * 128, 128), 128)
            qs = masked_pair(qkv[0, pl.ds(r0, BLK), cols], 0.125)
            kp = qkv[1, pl.ds(ws, win), cols]
            vp = qkv[2, pl.ds(ws, win), cols]
            outs = []
            for h in range(2):
                s = nt(qs[h], kp) + dn2A[0:BLK, 0:win]
                top = jnp.max(s, axis=-1, keepdims=True)
                e = jnp.exp(s - top)
                l = jnp.sum(e, axis=-1, keepdims=True)
                o = nn(e.astype(BF), vp) * (1.0 / l)
                outs.append(o)
                lacc = jnp.where(lane == (2 * p + h), top + jnp.log(l), lacc)
            attO[pl.ds(r0, BLK), cols] = jnp.where(lane_half((BLK, 128)), outs[0], outs[1]).astype(BF)
            return lacc

        lacc = lax.fori_loop(0, 3, pair, jnp.zeros((BLK, 128), F32))
        lseT[:, pl.ds(r0, BLK)] = lacc.T[0:8, :]
        return r0

    catt = []

    def att_send(r0):
        catt.append(xchg(attO.at[pl.ds(r0, BLK), :], attF.at[t, pl.ds(al(r0 - oth, BLK), BLK), :], yp))

    att_send(att_block(1 - t, True))
    att_send(att_block(1 - t, False))
    ysend(1, 0, 0)
    yb = xchg(bown(t), bown(t), yp)
    zc[("u", 1)].wait_recv()
    xsend(0, 1, 0)
    zstep("u")
    zsend("d", 2)
    xsend(0, 2, 0)
    cwp.wait_recv()
    cwc = xchg(wpf.at[1 - t, whalf, :], wpf.at[1 - t, whalf, :], core)
    for k in range(3):
        ysend(0, k, 0)
    att_block(t, True)
    att_block(t, False)
    attF[t] = attO[pl.ds(own, H), :]
    zend("u")
    xsend(0, 3, 0)
    zc[("d", 1)].wait_recv()
    xsend(1, 1, 0)
    ysend(0, 3, 0)

    bproj = vec[3:4, :]
    ln2g = vec[4:5, :]
    ln2b = vec[5:6, :]
    bdown = vec[6:7, :]
    ldml.wait()
    lwp.wait()
    for cp in catt:
        cp.wait_recv()
    cwc.wait_recv()

    def mid_block(b, carry):
        o0 = al(b * BLK, BLK)
        _, v = start_rows(al(own + o0, BLK))
        m = v + (nn(attF[0, pl.ds(o0, BLK), :], wpf[0]) + nn(attF[1, pl.ds(o0, BLK), :], wpf[1])) + bproj
        mid[pl.ds(o0, BLK), :] = m
        cent, r = stats(m)
        n2[pl.ds(al(cslot + o0, BLK), BLK), :] = (cent * r * ln2g + ln2b).astype(BF)
        return carry

    lax.fori_loop(0, 2, mid_block, 0)
    cn2 = xchg(n2.at[pl.ds(cslot, H), :], n2.at[pl.ds(cslot, H), :], core)
    zstep("d")
    xsend(1, 2, 0)
    yc[(1, 0, 0)].wait_recv()
    zstart("e")
    yb.wait_recv()
    xb = xchg(bown(1 - t), bown(1 - t), xp)
    cdml.wait_recv()
    cn2.wait_recv()
    nT[...] = n2[...].T
    dmlT[...] = dml[...].T
    cbup.wait_recv()
    for k in range(4):
        xc[(0, k, 0)].wait_recv()
        ysend(0, k, 1)
    zend("d")
    xsend(1, 3, 0)
    xsend(1, 0, 1)

    G = (gU, gD)
    rs = {}

    def addto(dst, src):
        dst[...] = (dst[...].astype(F32) + src[...].astype(F32)).astype(BF)

    def rs_x(a, j):
        rs[(a, j)] = [xchg(G[a].at[j, 1, h * 2 : h * 2 + 2], rG.at[a, j, h * 2 : h * 2 + 2], xp) for h in (0, 1)]

    rland = {(r, q): slot() for r in ((0, 0, 0), (0, 0, 1), (0, 1, 0), (1, 0, 0), (1, 1, 0)) for q in range(4, 9)}

    def rslot(r, q):
        a, j, xx = r
        if xx == 0:
            return rG.at[a, j, q]
        return rX.at[0] if q == 8 else rG.at[a, j, q - 4]

    def gblk(r, k):
        a, j, xx = r
        return G[a].at[j, xx, zk[k]]

    def rpass(r, k, to, q, when):
        xchg(gblk(r, k), rslot(r, q), to, when, rland[(r, q)])

    def radd(r, k, q):
        landed(rslot(r, q), rland[(r, q)], z1)
        addto(gblk(r, k), rslot(r, q))

    def rs_z0(r):
        for k, q in ((3, 4), (2, 5), (1, 6)):
            rpass(r, k, z1, q, end_z)

    def rs_z1(a, j):
        for cp in rs[(a, j)]:
            cp.wait_recv()
        for zz in range(4):
            addto(G[a].at[j, 0, zz], rG.at[a, j, zz])
        rs_z0((a, j, 0))

    def rs_z2(r):
        pl.when(mid_z)(partial(radd, r, 2, 4))
        rpass(r, 2, z3, 7, mid_z)
        pl.when(mid_z)(partial(radd, r, 3, 5))
        rpass(r, 3, z3, 8, mid_z)

    def rs_z3(r):
        pl.when(mid_z)(partial(radd, r, 1, 7))
        rpass(r, 1, z1, 8, mid_z)

    def rs_zsum(r):
        pl.when(mid_z)(partial(radd, r, 0, 6))
        radd(r, 0, 8)

    def rs_xlast():
        rs_zsum((0, 0, 1))
        rs["xlast"] = xchg(gblk((0, 0, 1), 0), rX.at[1], xp)

    def rs_sum(a, j):
        rs_zsum((a, j, 0))
        total = gblk((a, j, 0), 0)[...].astype(F32)
        if (a, j) == (0, 0):
            rs["xlast"].wait_recv()
            total = total + rX[1].astype(F32)
        return total

    def rs_y(a):
        sy[a] = rs_sum(a, 1).astype(BF)
        rs[(a, "y")] = xchg(sy.at[a], ry.at[a], yp)

    def rs_c(a):
        total = rs_sum(a, 0)
        rs[(a, "y")].wait_recv()
        sc[a] = total + ry[a].astype(F32)
        rs[(a, "c")] = xchg(sc.at[a, pl.ds(al((1 - c) * 48, 16), 48), :], rc.at[a], core)

    def rs_end(a):
        gS[a, :, pl.ds(al(c * D, 128), D)] = sc[a, pl.ds(al(c * 48, 16), 48), :]
        rs[(a, "c")].wait_recv()
        gS[a, :, pl.ds(al((1 - c) * D, 128), D)] = rc[a]
        load(gS.at[a], (gup, gdn)[a])

    bsums = []

    def ff_act(j):
        yy = tr[j]
        bu = bupA[j, pl.ds(c, 1), :]

        def block(b, carry):
            rows = pl.ds(al(b * BLK, BLK), BLK)
            hid = nn(n2[rows, :], Wu[yy]) + bu
            phi = 0.5 * (1.0 + lax.erf(hid * 0.7071067811865476))
            a = (hid * phi).astype(BF)
            act[rows, :] = a
            dh[rows, :] = (phi + hid * (jnp.exp(hid * hid * -0.5) * 0.3989422804014327)).astype(BF)
            return carry

        lax.fori_loop(0, 4, block, 0)

    def ff_out(j):
        yy = tr[j]

        def block(b, carry):
            rows = pl.ds(al(b * BLK, BLK), BLK)
            o = nt(act[rows, :], Wd[yy])
            if j == 0:
                outA[rows, :] = o
            else:
                outA[rows, :] += o
            return carry

        lax.fori_loop(0, 4, block, 0)

    def ff_bwd(j):
        yy = tr[j]

        def block(b, carry):
            rows = pl.ds(al(b * BLK, BLK), BLK)
            dhid = (nn(dml[rows, :], Wd[yy]) * dh[rows, :].astype(F32)).astype(BF)
            dh[rows, :] = dhid
            g = nt(dhid, Wu[yy])
            if j == 0:
                dn2A[rows, :] = g
            else:
                dn2A[rows, :] += g
            return carry + rowsum(dhid.astype(F32))

        bsums.append(lax.fori_loop(0, 4, block, jnp.zeros((1, D), F32)))

    def ff_grads(j, left, right, out):
        def gw_block(b, carry):
            r = nn(left[pl.ds(al(b * 192, 64), 192), :], right[...]).astype(BF)
            for xa in range(2):
                out[j, lax.rem(xa + x, 2), b] = r[xa * 96 : xa * 96 + 96]
            return carry

        lax.fori_loop(0, 4, gw_block, 0)

    def ff_gu(j):
        ff_grads(j, nT, dh, gU)

    def ff_gd(j):
        ff_grads(j, dmlT, act, gD)

    zrow = jnp.zeros((1, D), F32)
    ff_act(0)
    xb.wait_recv()
    zstart("b")
    ff_gd(0)
    zc[("e", 1)].wait_recv()
    xsend(1, 1, 1)
    for k in range(4):
        xc[(1, k, 0)].wait_recv()
    ff_out(0)
    zstep("e")
    xsend(1, 2, 1)
    ff_bwd(0)
    zstep("b")
    zend("e")
    xsend(1, 3, 1)
    rs_x(1, 0)
    ff_gu(0)
    rs_z0((0, 0, 1))
    rs_z0((0, 0, 0))
    zc[("b", 1)].wait_recv()
    zend("b")
    for k in range(4):
        yc[(0, k, 0)].wait_recv()
        yc[(0, k, 1)].wait_recv()
    ff_act(1)
    ff_gd(1)
    rs_x(1, 1)
    for k in range(4):
        xc[(1, k, 1)].wait_recv()
    ff_bwd(1)

    flush([cn2])
    n2[0:H, :] = dn2A[pl.ds(sslot, H), :].astype(BF)
    cN = xchg(n2.at[0:H, :], rN, core)
    ff_out(1)
    n2[H:T, :] = outA[pl.ds(sslot, H), :].astype(BF)
    cO = xchg(n2.at[H:T, :], rO, core)
    rs_z2((0, 0, 1))
    ff_gu(1)
    rs_x(0, 1)
    flush(catt)
    cN.wait_recv()
    flush([cN])

    sums = [zrow, zrow, zrow, zrow]
    cda = []
    for o in (t, 1 - t):
        o0 = al(o * BLK, BLK)
        rows = pl.ds(o0, BLK)
        crow = pl.ds(al(cslot + o0, BLK), BLK)
        dnb = dn2A[crow, :] + rN[rows, :].astype(F32)
        cent, r = stats(mid[rows, :])
        xhat = cent * r
        ct = dml[crow, :].astype(F32)
        dm = ct + norm_back(xhat, r, dnb, ln2g)
        db = dm.astype(BF)
        n2[rows, :] = db
        attO[rows, :] = nt(db, wpf[1 - t]).astype(BF)
        orow = pl.ds(al(own + o0, BLK), BLK)
        cda.append(xchg(attO.at[rows, :], dO.at[orow, :], yp))
        dO[orow, :] = nt(db, wpf[t]).astype(BF)
        dn2A[crow, :] = dm
        for i, term in enumerate((dnb * xhat, dnb, db.astype(F32), ct)):
            sums[i] = sums[i] + rowsum(term)
    s2g, s2b, sp, sd = sums

    cO.wait_recv()
    cmix = []

    def mixed_block(o):
        o0 = al(o * BLK, BLK)
        rows = pl.ds(o0, BLK)
        crow = pl.ds(al(cslot + o0, BLK), BLK)
        out = mid[rows, :] + (outA[crow, :] + rO[rows, :].astype(F32)) + bdown
        mixS[rows, :] = out.astype(BF)
        mid[rows, :] = dn2A[crow, :]

    def mixed_send(i):
        orow = pl.ds(own + i * 128, 128)
        rows = slice(i * 128, i * 128 + 128)
        cmix.append(xchg(mixS.at[rows, :], mixed.at[orow, :], yp))
        load(mixS.at[rows, :], mixed.at[orow, :])

    mixed_block(0)
    mixed_block(1)
    mixed_send(0)
    mixed_send(1)
    mixed_send(2)
    rs_z3((0, 0, 1))
    rs_z2((0, 0, 0))
    outA[...] = jnp.zeros((T, D), F32)
    nT[...] = n1[...].T
    rs_z1(1, 0)

    def att_back(half, edge):
        qb = half * 3 if edge else 1 + half
        wl = H if edge else WIN
        r0 = al(qb * BLK, BLK)
        ws = al(half * H if edge else half * BLK, BLK)
        cw = codec[pl.ds(ws, wl), 0:1]
        cr = coder[:, pl.ds(r0, BLK)]
        rid = r0 + lax.broadcasted_iota(jnp.int32, (wl, BLK), 1)
        cid = ws + lax.broadcasted_iota(jnp.int32, (wl, BLK), 0)
        ok = ((cr & 15) == (cw & 15)) & (((cw & 16) == 16) | (rid == cid))
        dn2A[0:wl, 0:BLK] = jnp.where(ok, 0.0, -1e30)
        rows = pl.ds(r0, BLK)
        win = pl.ds(ws, wl)

        def pair(p, carry):
            cols = pl.ds(al(p * 128, 128), 128)
            vcols = pl.ds(al(HL + p * 128, 128), 128)
            qp = qkv[0, rows, cols]
            op = dO[rows, cols]
            qs = masked_pair(qp, 0.125)
            os = masked_pair(op)
            kp = qkv[1, win, cols]
            vp = qkv[2, win, cols]
            dqs, dks, dvs = [], [], []
            for h in range(2):
                lse = lseT[pl.ds(2 * p + h, 1), rows]
                pr = jnp.exp(nt(kp, qs[h]) + dn2A[0:wl, 0:BLK] - lse)
                dp = nt(vp, os[h])
                inner = rowsum(pr * dp)
                ds = (pr * (dp - inner)).astype(BF)
                dvs.append(nn(pr.astype(BF), op))
                dks.append(nn(ds, qp))
                dqs.append(tn(ds, kp))
            low = lane_half((BLK, 128))
            lowk = lane_half((wl, 128))
            act[rows, cols] = (jnp.where(low, dqs[0], dqs[1]) * 0.125).astype(BF)
            outA[win, cols] += jnp.where(lowk, dks[0], dks[1])
            outA[win, vcols] += jnp.where(lowk, dvs[0], dvs[1])
            return carry

        lax.fori_loop(0, 3, pair, 0)

    def finish_rows(r0):
        rows = pl.ds(r0, BLK)
        act[rows, HL:D] = (outA[rows, 0:HL] * 0.125).astype(BF)
        dh[rows, 0:HL] = outA[rows, HL:D].astype(BF)

    def dn1_rows(r0):
        rows = pl.ds(r0, BLK)
        return nt(act[rows, 0:HL], wqkv[0]) + nt(act[rows, HL:D], wqkv[1]) + nt(dh[rows, 0:HL], wqkv[2])

    att_back(t, False)

    flush(ccp)
    flush([yb, xb])
    for q in (zc, xc, yc):
        flush(q.values())
    ar = {}

    def gA(s, r0, n):
        if s == 4:
            return Wd.at[0, pl.ds(r0, n), 0:HL]
        return Wu.at[s // 2, pl.ds(r0, n), (s % 2) * HL : (s % 2) * HL + HL]

    cbase = al(c * HL, 128)
    xbase = al(c * HL + x * 192, 64)
    XFIRST = (True, True, True, True, True)

    def blk_z(s, k):
        if XFIRST[s]:
            return al(xbase + zk[k] * 48, 16), 48
        return al(cbase + zk[k] * 96, 32), 96

    def spot_of(s):
        if XFIRST[s]:
            return al(xbase + z * 48, 16)
        return al(cbase + z * 96 + x * 48, 16)

    def ar_core(s):
        ar[(s, 0)] = xchg(gA(s, al((1 - c) * HL, 128), HL), rA.at[s, 0:HL, :], core)

    def ar_x(s):
        if XFIRST[s]:
            ar[(s, "x")] = xchg(gA(s, al(c * HL + (1 - x) * 192, 64), 192), rA.at[s, 384:576, :], xp)
        else:
            ar[(s, "x")] = xchg(gA(s, al(cbase + z * 96 + (1 - x) * 48, 16), 48), rA.at[s, 672:720, :], xp)

    def ar_xadd(s):
        ar[(s, "x")].wait_recv()
        if XFIRST[s]:
            addto(gA(s, xbase, 192), rA.at[s, 384:576, :])
        else:
            addto(gA(s, spot_of(s), 48), rA.at[s, 672:720, :])

    def ar_z1(s):
        o = 576 if XFIRST[s] else 384
        for i, k in ((0, 1), (1, 3)):
            r0, n = blk_z(s, k)
            ar[(s, "z1", i)] = xchg(gA(s, r0, n), rA.at[s, o + i * n : o + i * n + n, :], z1)

    def ar_z1add(s):
        o = 576 if XFIRST[s] else 384
        for i, k in ((0, 0), (1, 2)):
            r0, n = blk_z(s, k)
            ar[(s, "z1", i)].wait_recv()
            addto(gA(s, r0, n), rA.at[s, o + i * n : o + i * n + n, :])

    def ar_z2(s):
        o = 672 if XFIRST[s] else 576
        r0, n = blk_z(s, 2)
        ar[(s, "z2")] = xchg(gA(s, r0, n), rA.at[s, o : o + n, :], z2)

    def ar_z2add(s):
        o = 672 if XFIRST[s] else 576
        r0, n = blk_z(s, 0)
        ar[(s, "z2")].wait_recv()
        addto(gA(s, r0, n), rA.at[s, o : o + n, :])

    def ar_begin(s):
        ar[(s, 0)].wait_recv()
        addto(gA(s, cbase, HL), rA.at[s, 0:HL, :])
        (ar_x if XFIRST[s] else ar_z1)(s)

    def ar_step2(s):
        if XFIRST[s]:
            ar_xadd(s)
            ar_z1(s)
        else:
            ar_z1add(s)
            ar_z2(s)

    def ar_step3(s):
        if XFIRST[s]:
            ar_z1add(s)
            ar_z2(s)
        else:
            ar_z2add(s)
            ar_x(s)

    def ar_fin(s):
        (ar_z2add if XFIRST[s] else ar_xadd)(s)

    def fslot(s, r0, n):
        return fS.at[s, pl.ds(r0, n), :]

    def ag_z2(s):
        r0, n = blk_z(s, 0)
        f = fslot(s, r0, n)
        ar[(s, "g2")] = xchg(f, f, z2)
        ar[(s, "g1")] = xchg(f, f, z1)

    def ag_z1(s):
        ar[(s, "g2")].wait_recv()
        r0, n = blk_z(s, 2)
        f = fslot(s, r0, n)
        ar[(s, "g3")] = xchg(f, f, z1)

    def ag_zend(s):
        ar[(s, "g1")].wait_recv()
        ar[(s, "g3")].wait_recv()

    def ag_x(s):
        f = fslot(s, xbase, 192) if XFIRST[s] else fslot(s, spot_of(s), 48)
        ar[(s, "gx")] = xchg(f, f, xp)

    def ag_begin(s):
        r0 = spot_of(s)
        fslot(s, r0, 48)[...] = gA(s, r0, 48)[...]
        (ag_z2 if XFIRST[s] else ag_x)(s)

    def ag_step2(s):
        if XFIRST[s]:
            ag_z1(s)
        else:
            ar[(s, "gx")].wait_recv()
            ag_z2(s)

    def ag_step3(s):
        if XFIRST[s]:
            ag_zend(s)
            ag_x(s)
        else:
            ag_z1(s)

    def ag_core(s):
        if XFIRST[s]:
            ar[(s, "gx")].wait_recv()
        else:
            ag_zend(s)
        f = fslot(s, cbase, HL)
        ar[(s, "gc")] = xchg(f, fA.at[s, pl.ds(cbase, HL), :], core)
        load(f, fA.at[s, pl.ds(cbase, HL), :])

    for s, tt in ((3, t), (4, 1 - t)):
        gp = tn(attF[tt], n2[0:H, :])
        gA(s, 0, HL)[...] = gp[:, 0:HL].astype(BF)
        gA(s, HL, HL)[...] = gp[:, HL:D].astype(BF)
        ar_core(s)
    rs_z3((0, 0, 0))
    cda[0].wait_recv()
    att_back(1 - t, True)
    rs_z2((1, 0, 0))
    rs_z1(1, 1)
    cda[1].wait_recv()
    att_back(1 - t, False)

    flush([cO])
    cdn = []
    for o in (1 - t, t):
        r0 = al(oth + o * BLK, BLK)
        finish_rows(r0)
        rows = pl.ds(al(H + o * BLK, BLK), BLK)
        n2[rows, :] = dn1_rows(r0).astype(BF)
        cdn.append(xchg(n2.at[rows, :], rN.at[pl.ds(al(o * BLK, BLK), BLK), :], yp))
    for s in (3, 4):
        ar_begin(s)
    rs_z3((1, 0, 0))
    rs_z2((1, 1, 0))
    att_back(t, True)
    rs_z1(0, 1)
    for b in range(2):
        finish_rows(al(own + b * BLK, BLK))

    def gw(s, src):
        def body(m, carry):
            rows = pl.ds(al(m * BLK, BLK), BLK)
            gA(s, al(m * BLK, BLK), BLK)[...] = nn(nT[rows, :], src[...]).astype(BF)
            return carry

        lax.fori_loop(0, 3, body, 0)
        ar_core(s)

    gw(0, act.at[:, 0:HL])
    gw(1, act.at[:, HL:D])
    ar_begin(0)
    gw(2, dh.at[:, 0:HL])
    ar_begin(1)
    ar_begin(2)
    rs_z3((1, 1, 0))
    rs_xlast()

    vecA[0] = jnp.zeros((16, D), F32)
    for i, row in ((3, sp), (4, s2g), (5, s2b), (6, sd)):
        vecA[0, i : i + 1, :] = row
    vecA[0, pl.ds(8 + 2 * tr[0] + c, 1), :] = bsums[0]
    vecA[0, pl.ds(8 + 2 * tr[1] + c, 1), :] = bsums[1]
    vecA[0, pl.ds(12 + t, 1), 0:HL] = rowsum(act[:, 0:HL].astype(F32))
    vecA[0, pl.ds(12 + t, 1), HL:D] = rowsum(dh[:, 0:HL].astype(F32))
    stok, s1g, s1b = zrow, zrow, zrow
    cgin = []
    for i, o in enumerate((t, 1 - t)):
        o0 = al(o * BLK, BLK)
        r0 = al(own + o0, BLK)
        rows = pl.ds(r0, BLK)
        orow = pl.ds(o0, BLK)
        cdn[i].wait_recv()
        dnb = dn1_rows(r0) + rN[orow, :].astype(F32)
        m, v = start_rows(r0)
        cent, r = stats(v)
        xhat = cent * r
        dst = mid[orow, :] + norm_back(xhat, r, dnb, ln1g)
        ginS[orow, :] = jnp.where(m, 0.0, dst).astype(BF)
        stok = stok + rowsum(jnp.where(m, dst, 0.0))
        s1g = s1g + rowsum(dnb * xhat)
        s1b = s1b + rowsum(dnb)
        if i == 1:
            for n, row in ((0, stok), (1, s1g), (2, s1b)):
                vecA[0, n : n + 1, :] = row
            cv = cv0 = xchg(vecA.at[0], vR.at[0], core)
        cgin.append(xchg(ginS.at[orow, :], gin.at[rows, :], yp))
        load(ginS.at[orow, :], gin.at[rows, :])
        if i == 0:
            ar_step2(0)
            rs_z2((0, 1, 0))
            ar_step2(3)
            ar_step2(4)
            ar_step2(1)
            rs_y(1)
            ar_step2(2)
            ar_step3(0)

    def sum_step(i, to):
        cv.wait_recv()
        vecA[i] = vecA[i - 1] + vR[i - 1]
        return xchg(vecA.at[i], vR.at[i], to)

    ar_step3(3)
    ar_step3(4)
    ar_step3(1)
    rs_z3((0, 1, 0))
    ar_fin(0)
    ag_begin(0)
    ar_step3(2)
    ar_fin(3)
    ar_fin(4)
    cgp = xchg(gA(4, spot_of(4), 48), rgp, yp)
    mixed_send(3)
    cv = sum_step(1, xp)
    ar_fin(1)
    ag_begin(1)
    ag_step2(0)
    ar_fin(2)
    ag_begin(2)
    ag_step2(1)
    ag_step3(0)
    cgp.wait_recv()
    addto(gA(3, spot_of(3), 48), rgp)
    ag_begin(3)
    cv = sum_step(2, z1)
    ag_step2(2)
    ag_step3(1)
    rs_y(0)
    ag_core(0)
    ag_step2(3)
    ag_step3(2)
    cv = sum_step(3, z2)
    ag_core(1)
    ag_step3(3)
    rs_c(0)
    rs_c(1)
    flush([cv0])
    cv = sum_step(4, yp)
    ag_core(2)
    ag_core(3)
    rs_end(0)
    rs_end(1)
    cv.wait_recv()
    vecA[0] = vecA[4] + vR[4]
    load(vecA.at[0], vout)
    for s in range(4):
        ar[(s, "gc")].wait_recv()
    for cp in cmix + cgin:
        cp.wait_recv()
    flush([cp for cp, _ in pending])
    for cp in loads[4:]:
        cp.wait()
    assert (len(pending), slots[0], len(loads)) == (SENT, LANDED, LOCAL)


def scratch():
    def v(shape, dt):
        return pltpu.VMEM(shape, dt)

    return [
        v((T, D), BF), v((D, T), BF), v((3, T, HL), BF), v((T, HL), BF), v((2, H, HL), BF), v((2, HL, D), BF),
        v((2, D, D), BF), v((2, D, D), BF), v((H, D), F32), v((T, D), BF), v((T, D), BF), v((D, T), BF),
        v((T, D), F32), v((T, D), F32), v((H, D), BF), v((H, D), BF), v((T, D), BF), v((T, D), BF),
        v((2, 2, 4, 96, D), BF), v((2, 2, 4, 96, D), BF),
        v((2, 2, 9, 96, D), BF), v((2, 96, D), BF), v((2, 96, D), BF), v((2, 96, D), BF),
        v((2, 96, D), F32), v((2, 48, D), F32), v((T, HL), BF), v((48, HL), BF), v((5, 720, HL), BF),
        v((8, T), F32), v((2, 8, D), F32), v((5, 16, D), F32), v((5, 16, D), F32),
        v((T, D), BF), v((3, D, HL), BF), v((T, 128), jnp.int32), v((1, T), jnp.int32), v((8, D), F32),
        v((H, D), BF), v((H, D), BF), v((4, D, HL), BF), v((2, 48, 2 * D), F32),
        pltpu.SemaphoreType.DMA((SENT,)), pltpu.SemaphoreType.DMA((LANDED,)), pltpu.SemaphoreType.DMA((LOCAL,)),
    ]


def finish(mixed, gin, fa, gup, gdn, vs, o_mixed, o_gin, o_tok, o_g1, o_b1, o_qkv, o_bqv, o_proj, o_bp, o_g2, o_b2, o_up,
           o_bup, o_dn, o_bd, gb, gf, fb, ff, pf, mb, ub, vb, rows_1d, r_bup, r_bqv, sem):
    t = lax.axis_index("tensor")
    count = [0]

    def copy(src, dst):
        cp = pltpu.make_async_copy(src, dst, sem.at[count[0]])
        count[0] += 1
        cp.start()
        return cp

    vc = copy(vs, vb)
    fc = [copy(fa.at[s], fb.at[s]) for s in range(4)]
    gc = [copy(gin.at[b * BLK : b * BLK + BLK, :], gb.at[b * BLK : b * BLK + BLK, :]) for b in range(4)]
    through = [(copy(mixed, mb), mb, o_mixed), (copy(gup, ub.at[0]), ub.at[0], o_up), (copy(gdn, ub.at[1]), ub.at[1], o_dn)]
    out = []
    vc.wait()
    for i, o in enumerate((o_tok, o_g1, o_b1, o_bp, o_g2, o_b2, o_bd)):
        rows_1d[i][...] = vb[i : i + 1, :].reshape(D)
        out.append(copy(rows_1d[i], o))
    for i in range(2):
        r_bup[i * D : i * D + D] = vb[pl.ds(8 + 2 * t + i, 1), :].reshape(D)
        r_bqv[i : i + 1, :] = vb[pl.ds(12 + t, 1), i * HL : i * HL + HL]
    out += [copy(r_bup, o_bup), copy(r_bqv, o_bqv)]
    for b in range(4):
        gc[b].wait()
        rows = slice(b * BLK, b * BLK + BLK)
        gf[rows, :] = gb[rows, :].astype(F32)
        out.append(copy(gf.at[rows, :], o_gin.at[rows, :]))
    for cp, here, there in through:
        cp.wait()
        out.append(copy(here, there))
    for s in range(4):
        fc[s].wait()
        if s < 3:
            ff[s] = fb[s].astype(F32)
            out.append(copy(ff.at[s], o_qkv.at[s]))
        else:
            pf[:, 0:HL] = fb[3, 0:HL, :].astype(F32)
            pf[:, HL:D] = fb[3, HL:D, :].astype(F32)
            out.append(copy(pf, o_proj))
    for cp in out:
        cp.wait()


def on_device(
    patches, image_ids, valid, mask_pos, mask_token, ln1_gain, ln1_bias, w_qkv, b_qv, w_proj, b_proj,
    ln2_gain, ln2_bias, w_up, b_up, w_down, b_down, cotangent,
):
    vm = pl.BlockSpec(memory_space=pltpu.VMEM)
    hbm = pl.BlockSpec(memory_space=pl.ANY)
    sds = jax.ShapeDtypeStruct
    parts = pl.pallas_call(
        mega,
        out_shape=(
            sds((T, D), BF), sds((T, D), BF), sds((4, D, HL), BF), sds((48, 2 * D), F32), sds((48, 2 * D), F32),
            sds((16, D), F32),
        ),
        in_specs=[hbm if i in (0, 11, 13, 17) else vm for i in range(18)],
        out_specs=(hbm,) * 6,
        scratch_shapes=scratch(),
        compiler_params=pltpu.CompilerParams(collective_id=0, has_side_effects=True, vmem_limit_bytes=66584576),
        name="block",
    )(
        patches, image_ids, valid, mask_pos, mask_token, ln1_gain, ln1_bias, b_proj, ln2_gain, ln2_bias, b_down,
        jnp.transpose(w_qkv, (1, 0, 2)), b_qv, w_proj, w_up, w_down.T, b_up, cotangent,
    )
    row = sds((D,), F32)
    outs = pl.pallas_call(
        finish,
        out_shape=(
            sds((T, D), BF), sds((T, D), F32), row, row, row, sds((3, D, HL), F32), sds((2, HL), F32), sds((HL, D), F32),
            row, row, row, sds((48, 2 * D), F32), sds((2 * D,), F32), sds((48, 2 * D), F32), row,
        ),
        in_specs=[hbm] * 6,
        out_specs=(hbm,) * 15,
        scratch_shapes=[
            pltpu.VMEM((T, D), BF), pltpu.VMEM((T, D), F32), pltpu.VMEM((4, D, HL), BF), pltpu.VMEM((3, D, HL), F32),
            pltpu.VMEM((HL, D), F32), pltpu.VMEM((T, D), BF), pltpu.VMEM((2, 48, 2 * D), F32),
            pltpu.VMEM((16, D), F32), [pltpu.VMEM((D,), F32)] * 7, pltpu.VMEM((2 * D,), F32), pltpu.VMEM((2, HL), F32),
            pltpu.SemaphoreType.DMA((32,)),
        ],
        compiler_params=pltpu.CompilerParams(vmem_limit_bytes=66584576),
        name="finish",
    )(*parts)
    outs = list(outs)
    outs[5] = jnp.transpose(outs[5], (1, 0, 2))
    outs[13] = outs[13].T
    return tuple(outs)


HEAD_DIM = 64


def norm_rows(values, gain, shift):
    mean = jnp.mean(values, axis=-1, keepdims=True)
    cent = values - mean
    var = jnp.mean(cent * cent, axis=-1, keepdims=True)
    return cent * lax.rsqrt(var + EPS) * gain + shift


def left_dot(first, second):
    return lax.dot_general(
        first, second, (((0,), (0,)), ((), ())), preferred_element_type=jnp.float32
    )


def right_dot(first, second):
    return lax.dot_general(
        first, second, (((1,), (1,)), ((), ())), preferred_element_type=jnp.float32
    )


def allowed_rows(ids, live, begin, count):
    rows = ids.shape[0]
    own_ids = lax.dynamic_slice_in_dim(ids, begin, count, 0)
    places = begin + jnp.arange(count)
    same_place = places[:, None] == jnp.arange(rows)[None, :]
    return (own_ids[:, None] == ids[None, :]) & ((live[None, :] == 1) | same_place)


def spread(
    patches,
    image_ids,
    valid,
    mask_pos,
    mask_token,
    ln1_gain,
    ln1_bias,
    w_qkv,
    b_qv,
    w_proj,
    b_proj,
    ln2_gain,
    ln2_bias,
    w_up,
    b_up,
    w_down,
    b_down,
    cotangent,
):
    rows = patches.shape[0]
    local_width = w_qkv.shape[2]
    local_heads = local_width // HEAD_DIM
    scale = 1.0 / HEAD_DIM**0.5
    ids = image_ids[0]
    live = valid[0]
    masked = mask_pos[0][:, None] == 1
    block = min(512, rows)
    blocks = rows // block
    start = jnp.where(masked, mask_token.astype(jnp.float32)[None, :], patches.astype(jnp.float32))
    normed, norm1_pull = jax.vjp(
        norm_rows, start, ln1_gain.astype(jnp.float32), ln1_bias.astype(jnp.float32)
    )
    normed_b = normed.astype(jnp.bfloat16)
    qv_bias = b_qv.astype(jnp.float32)
    bias = jnp.stack([qv_bias[0], jnp.zeros_like(qv_bias[0]), qv_bias[1]])
    qkv = jnp.einsum("td,dsc->tsc", normed_b, w_qkv, preferred_element_type=jnp.float32)
    qkv_b = (qkv + bias[None]).astype(jnp.bfloat16)
    query = qkv_b[:, 0].reshape(rows, local_heads, HEAD_DIM)
    keys = qkv_b[:, 1].reshape(rows, local_heads, HEAD_DIM)
    values = qkv_b[:, 2].reshape(rows, local_heads, HEAD_DIM)
    outputs = []
    totals = []
    for index in range(blocks):
        begin = index * block
        query_part = query[begin : begin + block]
        allowed = allowed_rows(ids, live, begin, block)
        scores = (
            jnp.einsum("qhc,khc->hqk", query_part, keys, preferred_element_type=jnp.float32) * scale
        )
        scores = jnp.where(allowed[None], scores, -1e30)
        top = jnp.max(scores, axis=-1, keepdims=True)
        expd = jnp.exp(scores - top)
        summed = jnp.sum(expd, axis=-1, keepdims=True)
        probs_b = (expd / summed).astype(jnp.bfloat16)
        totals.append(top + jnp.log(summed))
        outputs.append(
            jnp.einsum("hqk,khc->qhc", probs_b, values, preferred_element_type=jnp.float32)
        )
    attended_b = jnp.concatenate(outputs, axis=0).reshape(rows, local_width).astype(jnp.bfloat16)
    attn_part = jnp.dot(attended_b, w_proj, preferred_element_type=jnp.float32)
    ln2_gain_f = ln2_gain.astype(jnp.float32)
    ln2_bias_f = ln2_bias.astype(jnp.float32)
    attn_total = lax.psum(attn_part, "tensor")
    middle = start + attn_total + b_proj.astype(jnp.float32)
    normed2, norm2_pull = jax.vjp(norm_rows, middle, ln2_gain_f, ln2_bias_f)
    normed2_b = normed2.astype(jnp.bfloat16)
    up_full, down_full = (
        lax.all_gather(w_up, "dp", axis=0, tiled=True),
        lax.all_gather(w_down, "dp", axis=1, tiled=True),
    )
    hidden = jnp.dot(normed2_b, up_full, preferred_element_type=jnp.float32) + b_up.astype(
        jnp.float32
    )
    active, gelu_pull = jax.vjp(partial(jax.nn.gelu, approximate=False), hidden)
    active_b = active.astype(jnp.bfloat16)
    mlp_part = jnp.dot(active_b, down_full, preferred_element_type=jnp.float32)
    mlp_total = lax.psum(mlp_part.astype(jnp.bfloat16), "tensor").astype(jnp.float32)
    mixed = (middle + mlp_total + b_down.astype(jnp.float32)).astype(jnp.bfloat16)
    seed_grad = cotangent.astype(jnp.float32)
    up_back, down_back = (up_full, down_full)
    grad_b_down = jnp.sum(seed_grad, axis=0)
    grad_down_local = left_dot(active_b, cotangent)
    grad_active = right_dot(cotangent, down_back)
    (grad_hidden,) = gelu_pull(grad_active)
    grad_hidden_b = grad_hidden.astype(jnp.bfloat16)
    grad_b_up = jnp.sum(grad_hidden_b.astype(jnp.float32), axis=0)
    grad_up_local = left_dot(normed2_b, grad_hidden_b)
    grad_normed2_part = right_dot(grad_hidden_b, up_back)
    grad_normed2 = lax.psum(grad_normed2_part, "tensor")
    grad_mid_norm, grad_ln2_gain, grad_ln2_bias = norm2_pull(grad_normed2)
    grad_middle = seed_grad + grad_mid_norm
    grad_w_up, grad_w_down = (
        lax.psum_scatter(grad_up_local, "dp", scatter_dimension=0, tiled=True),
        lax.psum_scatter(grad_down_local, "dp", scatter_dimension=1, tiled=True),
    )
    grad_branch_b = grad_middle.astype(jnp.bfloat16)
    grad_b_proj = jnp.sum(grad_branch_b.astype(jnp.float32), axis=0)
    grad_w_proj = left_dot(attended_b, grad_branch_b)
    grad_attended = (
        right_dot(grad_branch_b, w_proj).astype(jnp.bfloat16).reshape(rows, local_heads, HEAD_DIM)
    )
    grad_query_parts = []
    grad_keys = jnp.zeros((rows, local_heads, HEAD_DIM), jnp.float32)
    grad_values = jnp.zeros((rows, local_heads, HEAD_DIM), jnp.float32)
    for index in range(blocks):
        begin = index * block
        query_part = query[begin : begin + block]
        grad_out_part = grad_attended[begin : begin + block]
        allowed = allowed_rows(ids, live, begin, block)
        scores = (
            jnp.einsum("qhc,khc->hqk", query_part, keys, preferred_element_type=jnp.float32) * scale
        )
        scores = jnp.where(allowed[None], scores, -1e30)
        probs = jnp.exp(scores - totals[index])
        probs_b = probs.astype(jnp.bfloat16)
        grad_values = grad_values + jnp.einsum(
            "hqk,qhc->khc", probs_b, grad_out_part, preferred_element_type=jnp.float32
        )
        grad_probs = jnp.einsum(
            "qhc,khc->hqk", grad_out_part, values, preferred_element_type=jnp.float32
        )
        inner = jnp.sum(probs * grad_probs, axis=-1, keepdims=True)
        grad_scores_b = (probs * (grad_probs - inner)).astype(jnp.bfloat16)
        grad_query_parts.append(
            jnp.einsum("hqk,khc->qhc", grad_scores_b, keys, preferred_element_type=jnp.float32)
            * scale
        )
        grad_keys = (
            grad_keys
            + jnp.einsum(
                "hqk,qhc->khc", grad_scores_b, query_part, preferred_element_type=jnp.float32
            )
            * scale
        )
    grad_query = jnp.concatenate(grad_query_parts, axis=0)
    grad_qkv_b = (
        jnp.stack([grad_query, grad_keys, grad_values], axis=1)
        .reshape(rows, 3, local_width)
        .astype(jnp.bfloat16)
    )
    grad_qkv_f = grad_qkv_b.astype(jnp.float32)
    grad_b_qv = jnp.stack([jnp.sum(grad_qkv_f[:, 0], axis=0), jnp.sum(grad_qkv_f[:, 2], axis=0)])
    grad_w_qkv = jnp.einsum("td,tsc->dsc", normed_b, grad_qkv_b, preferred_element_type=jnp.float32)
    grad_normed_part = jnp.einsum(
        "tsc,dsc->td", grad_qkv_b, w_qkv, preferred_element_type=jnp.float32
    )
    grad_normed = lax.psum(grad_normed_part.astype(jnp.bfloat16), "tensor").astype(jnp.float32)
    grad_start_norm, grad_ln1_gain, grad_ln1_bias = norm1_pull(grad_normed)
    grad_start = grad_middle + grad_start_norm
    grad_input = jnp.where(masked, 0.0, grad_start)
    grad_token = jnp.sum(jnp.where(masked, grad_start, 0.0), axis=0)
    summed = lax.psum(
        (
            grad_token,
            grad_ln1_gain,
            grad_ln1_bias,
            grad_w_qkv,
            grad_b_qv,
            grad_w_proj,
            grad_b_proj,
            grad_ln2_gain,
            grad_ln2_bias,
            grad_b_up,
            grad_b_down,
        ),
        "dp",
    )
    return (
        mixed,
        grad_input,
        summed[0],
        summed[1],
        summed[2],
        summed[3],
        summed[4],
        summed[5],
        summed[6],
        summed[7],
        summed[8],
        grad_w_up,
        summed[9],
        grad_w_down,
        summed[10],
    )


def solution(mesh):
    placed = (
        P("dp", None),
        P("dp", None),
        P("dp", None),
        P("dp", None),
        P(),
        P(),
        P(),
        P(None, None, "tensor"),
        P(None, "tensor"),
        P("tensor", None),
        P(),
        P(),
        P(),
        P("dp", "tensor"),
        P("tensor"),
        P("tensor", "dp"),
        P(),
        P("dp", None),
    )
    fits = mesh.shape["dp"] == 16 and mesh.shape["tensor"] == 2
    return jax.shard_map(
        on_device if fits else spread,
        mesh=mesh,
        in_specs=placed,
        out_specs=(
            P("dp", None),
            P("dp", None),
            P(),
            P(),
            P(),
            P(None, None, "tensor"),
            P(None, "tensor"),
            P("tensor", None),
            P(),
            P(),
            P(),
            P("dp", "tensor"),
            P("tensor"),
            P("tensor", "dp"),
            P(),
        ),
        check_vma=False,
    )
```

```python
from functools import partial

import jax
import jax.numpy as jnp
from jax import lax
from jax.experimental import pallas as pl
from jax.experimental.pallas import tpu as pltpu
from jax.sharding import PartitionSpec as P

BF = jnp.bfloat16
F32 = jnp.float32
MESH = pl.DeviceIdType.MESH
EPS = 1e-06
T = 1024
H = 512
D = 768
HL = 384
BLK = 256
WIN = 768
CUT = 640
SENT, LANDED, LOCAL = 145, 140, 31


def nn(a, b):
    return lax.dot_general(a, b, (((1,), (0,)), ((), ())), preferred_element_type=F32)


def nt(a, b):
    return lax.dot_general(a, b, (((1,), (1,)), ((), ())), preferred_element_type=F32)


def tn(a, b):
    return lax.dot_general(a, b, (((0,), (0,)), ((), ())), preferred_element_type=F32)


def rowsum(v):
    return jnp.sum(v, axis=0, keepdims=True)


def lane_half(shape):
    return lax.broadcasted_iota(jnp.int32, shape, 1) < 64


def stats(v):
    mean = jnp.sum(v, axis=-1, keepdims=True) * (1.0 / D)
    cent = v - mean
    var = jnp.sum(cent * cent, axis=-1, keepdims=True) * (1.0 / D)
    return cent, lax.rsqrt(var + EPS)


def norm_back(xhat, r, d, gain):
    e = d * gain
    m1 = jnp.sum(e, axis=-1, keepdims=True) * (1.0 / D)
    m2 = jnp.sum(e * xhat, axis=-1, keepdims=True) * (1.0 / D)
    return r * (e - m1 - xhat * m2)


def mega(
    patches, wqkv_h, wproj, cot, ids_h, live_h, hidden_h, token_h, ln1g_h, ln1b_h, bproj_h, ln2g_h, ln2b_h, bdown_h, bqv_h,
    up_h, dn_h, bup_h,
    mixed, gin, fA, gup, gdn, vout,
    n1, nT, qkv, attO, attF, wpf, Wu, Wd, mid, n2, dml, dmlT, outA, dn2A, rO, rN, act, dh, gU, gD,
    rG, rX, sy, ry, sc, rc, dO, rgp, rA, lseT, bupA, vecA, vR, pat, wqkv, codec, coder, vec, mixS, ginS, fS,
    gS, small, ssem, rsem, lsem,
):
    d = lax.axis_index("dp")
    t = lax.axis_index("tensor")
    z = lax.div(d, 4)
    x = lax.rem(lax.div(d, 2), 2)
    c = lax.rem(d, 2)
    zk = (z, z + 1 - 2 * lax.rem(z, 2), lax.rem(z + 2, 4), 3 - z)
    xr = (x, 1 - x)
    tr = (t, 1 - t)

    def dev(zz, xx, cc, tt):
        return ((zz * 2 + xx) * 2 + cc, tt)

    core = dev(z, x, 1 - c, t)
    xp = dev(z, 1 - x, c, t)
    yp = dev(z, x, c, 1 - t)
    z1 = dev(zk[1], x, c, t)
    z2 = dev(zk[2], x, c, t)
    z3 = dev(zk[3], x, c, t)
    mid_z = (z == 1) | (z == 2)
    end_z = (z == 0) | (z == 3)

    pending = []
    flushed = set()
    slots = [0]

    def slot():
        slots[0] += 1
        return slots[0] - 1

    def xchg(src, dst, to, when=None, land=None):
        i = len(pending)
        cp = pltpu.make_async_remote_copy(
            src_ref=src, dst_ref=dst, send_sem=ssem.at[i], recv_sem=rsem.at[slot() if land is None else land],
            device_id=to, device_id_type=MESH,
        )
        pending.append((cp, when))
        if when is None:
            cp.start()
        else:
            pl.when(when)(cp.start)
        return cp

    def landed(dst, land, frm):
        pltpu.make_async_remote_copy(
            src_ref=dst, dst_ref=dst, send_sem=ssem.at[0], recv_sem=rsem.at[land], device_id=frm, device_id_type=MESH
        ).wait_recv()

    def flush(cps):
        cps = set(id(cp) for cp in cps)
        for cp, when in pending:
            if id(cp) in cps and id(cp) not in flushed:
                flushed.add(id(cp))
                if when is None:
                    cp.wait_send()
                else:
                    pl.when(when)(cp.wait_send)

    def al(v, m):
        return pl.multiple_of(v, m)

    bar = pltpu.get_barrier_semaphore()
    peers = (core, xp, yp, z1, z2, z3)
    for p in peers:
        pl.semaphore_signal(bar, inc=1, device_id=p, device_id_type=MESH)
    loads = []

    def load(src, dst):
        cp = pltpu.make_async_copy(src, dst, lsem.at[len(loads)])
        cp.start()
        loads.append(cp)
        return cp

    ids, live, hidden_pos, token_b, ln1g_b, ln1b_b, bproj_b, ln2g_b, ln2b_b, bdown_b, bqv_b, up, dn, bup = small
    sources = (
        ids_h, live_h, hidden_h, token_h, ln1g_h, ln1b_h, bproj_h, ln2g_h, ln2b_h, bdown_h, bqv_h, up_h, dn_h, bup_h
    )
    first = [load(src, dst) for src, dst in zip(sources, small)]
    lpat = load(patches, pat)
    lwq = load(wqkv_h, wqkv)
    for cp in first:
        cp.wait()
    code = ids[...] + 16 * live[...] + 32 * hidden_pos[...]
    coder[...] = code
    codec[...] = jnp.broadcast_to(code.astype(F32), (128, T)).T.astype(jnp.int32)
    for i, row in enumerate((token_b, ln1g_b, ln1b_b, bproj_b, ln2g_b, ln2b_b, bdown_b)):
        vec[i : i + 1, :] = row[...].astype(F32).reshape(1, D)
    bqv = bqv_b[...].astype(F32)
    bupA[0] = jnp.zeros((8, D), F32)
    for i in range(2):
        bupA[0, i : i + 1, :] = bup[i * D : i * D + D].astype(F32).reshape(1, D)
    pl.semaphore_wait(bar, len(peers))

    own = al(t * H, H)
    oth = al((1 - t) * H, H)
    cslot = al(c * H, H)
    sslot = al((1 - c) * H, H)
    W = (Wu, Wd)
    shards = (up, dn)

    def wblk(a, k, xx, yy):
        return W[a].at[tr[yy], pl.ds(al((zk[k] * 2 + xr[xx]) * 96, 32), 96), :]

    ccp = []
    mine = al((z * 2 + x) * 96 + c * 48, 16)
    for a in (0, 1):
        ccp.append(
            xchg(shards[a].at[:, pl.ds(al((1 - c) * D, 128), D)], W[a].at[t, pl.ds(mine, 48), :], core)
        )
    whalf = pl.ds(al(c * 192, 64), 192)
    cwp = xchg(wproj.at[whalf, :], wpf.at[t, whalf, :], yp)
    cbup = xchg(bupA.at[0, pl.ds(c, 1), :], bupA.at[1, pl.ds(c, 1), :], yp)
    cdml = xchg(cot.at[pl.ds(own, H), :], dml.at[pl.ds(cslot, H), :], core)
    ldml = load(cot.at[pl.ds(own, H), :], dml.at[pl.ds(cslot, H), :])
    lwp = load(wproj, wpf.at[t])
    for a in (0, 1):
        W[a][t, pl.ds(mine, 48), :] = shards[a][:, pl.ds(al(c * D, 128), D)]

    zc, xc, yc = {}, {}, {}

    chains = {
        "u": lambda k: wblk(0, k, 0, 0),
        "d": lambda k: wblk(1, k, 0, 0),
        "e": lambda k: wblk(1, k, 0, 1),
        "b": lambda k: Wu.at[tr[1], pl.ds(al(zk[k] * 192, 64), 192), CUT:D],
    }

    def zsend(q, k):
        zc[(q, k)] = xchg(chains[q](0), chains[q](0), z1 if k == 1 else z2)

    def zstart(q):
        zsend(q, 1)
        zsend(q, 2)

    def zstep(q):
        zc[(q, 2)].wait_recv()
        zc[(q, 3)] = xchg(chains[q](2), chains[q](2), z1)

    def zend(q):
        zc[(q, 3)].wait_recv()

    def xsend(a, k, yy):
        xc[(a, k, yy)] = xchg(wblk(a, k, 0, yy), wblk(a, k, 0, yy), xp)

    def ysend(a, k, xx):
        ref = wblk(a, k, xx, 0)
        if a == 0:
            ref = W[0].at[t, pl.ds(al((zk[k] * 2 + xr[xx]) * 96, 32), 96), 0:CUT]
        yc[(a, k, xx)] = xchg(ref, ref, yp)

    def bown(tt):
        return W[0].at[tt, pl.ds(al((z * 2 + x) * 96, 32), 96), CUT:D]

    token = vec[0:1, :]
    ln1g = vec[1:2, :]
    ln1b = vec[2:3, :]

    def start_rows(r0):
        m = lax.shift_right_logical(codec[pl.ds(r0, BLK), 0:1], 5) == 1
        return m, jnp.where(m, token, pat[pl.ds(r0, BLK), :].astype(F32))

    def ln1_block(b, carry):
        r0 = al(b * BLK, BLK)
        _, v = start_rows(r0)
        cent, r = stats(v)
        nb = (cent * r * ln1g + ln1b).astype(BF)
        n1[pl.ds(r0, BLK), :] = nb
        for s in range(3):
            y = nn(nb, wqkv[s])
            if s == 0:
                y = y + bqv[0:1, :]
            if s == 2:
                y = y + bqv[1:2, :]
            qkv[s, pl.ds(r0, BLK), :] = y.astype(BF)
        return carry

    lpat.wait()
    lwq.wait()
    lax.fori_loop(0, 1, ln1_block, 0)
    for a in (0, 1):
        ccp[a].wait_recv()
    zstart("u")
    zsend("d", 1)
    xsend(0, 0, 0)
    xsend(1, 0, 0)
    lax.fori_loop(1, 4, ln1_block, 0)

    def masked_pair(block, scale=None):
        low = lane_half(block.shape)
        zero = jnp.zeros_like(block)
        if scale is not None:
            block = block * jnp.asarray(scale, BF)
        return jnp.where(low, block, zero), jnp.where(low, zero, block)

    def att_block(half, edge):
        qb = half * 3 if edge else 1 + half
        win = H if edge else WIN
        r0 = al(qb * BLK, BLK)
        ws = al(half * H if edge else half * BLK, BLK)
        cr = codec[pl.ds(r0, BLK), 0:1]
        cw = coder[:, pl.ds(ws, win)]
        rid = r0 + lax.broadcasted_iota(jnp.int32, (BLK, win), 0)
        cid = ws + lax.broadcasted_iota(jnp.int32, (BLK, win), 1)
        ok = ((cr & 15) == (cw & 15)) & (((cw & 16) == 16) | (rid == cid))
        dn2A[0:BLK, 0:win] = jnp.where(ok, 0.0, -1e30)
        lane = lax.broadcasted_iota(jnp.int32, (BLK, 128), 1)

        def pair(p, lacc):
            cols = pl.ds(al(p * 128, 128), 128)
            qs = masked_pair(qkv[0, pl.ds(r0, BLK), cols], 0.125)
            kp = qkv[1, pl.ds(ws, win), cols]
            vp = qkv[2, pl.ds(ws, win), cols]
            outs = []
            for h in range(2):
                s = nt(qs[h], kp) + dn2A[0:BLK, 0:win]
                top = jnp.max(s, axis=-1, keepdims=True)
                e = jnp.exp(s - top)
                l = jnp.sum(e, axis=-1, keepdims=True)
                o = nn(e.astype(BF), vp) * (1.0 / l)
                outs.append(o)
                lacc = jnp.where(lane == (2 * p + h), top + jnp.log(l), lacc)
            attO[pl.ds(r0, BLK), cols] = jnp.where(lane_half((BLK, 128)), outs[0], outs[1]).astype(BF)
            return lacc

        lacc = lax.fori_loop(0, 3, pair, jnp.zeros((BLK, 128), F32))
        lseT[:, pl.ds(r0, BLK)] = lacc.T[0:8, :]
        return r0

    catt = []

    def att_send(r0):
        catt.append(xchg(attO.at[pl.ds(r0, BLK), :], attF.at[t, pl.ds(al(r0 - oth, BLK), BLK), :], yp))

    att_send(att_block(1 - t, True))
    att_send(att_block(1 - t, False))
    ysend(1, 0, 0)
    yb = xchg(bown(t), bown(t), yp)
    zc[("u", 1)].wait_recv()
    xsend(0, 1, 0)
    zstep("u")
    zsend("d", 2)
    xsend(0, 2, 0)
    cwp.wait_recv()
    cwc = xchg(wpf.at[1 - t, whalf, :], wpf.at[1 - t, whalf, :], core)
    for k in range(3):
        ysend(0, k, 0)
    att_block(t, True)
    att_block(t, False)
    attF[t] = attO[pl.ds(own, H), :]
    zend("u")
    xsend(0, 3, 0)
    zc[("d", 1)].wait_recv()
    xsend(1, 1, 0)
    ysend(0, 3, 0)

    bproj = vec[3:4, :]
    ln2g = vec[4:5, :]
    ln2b = vec[5:6, :]
    bdown = vec[6:7, :]
    ldml.wait()
    lwp.wait()
    for cp in catt:
        cp.wait_recv()
    cwc.wait_recv()

    def mid_block(b, carry):
        o0 = al(b * BLK, BLK)
        _, v = start_rows(al(own + o0, BLK))
        m = v + (nn(attF[0, pl.ds(o0, BLK), :], wpf[0]) + nn(attF[1, pl.ds(o0, BLK), :], wpf[1])) + bproj
        mid[pl.ds(o0, BLK), :] = m
        cent, r = stats(m)
        n2[pl.ds(al(cslot + o0, BLK), BLK), :] = (cent * r * ln2g + ln2b).astype(BF)
        return carry

    lax.fori_loop(0, 2, mid_block, 0)
    cn2 = xchg(n2.at[pl.ds(cslot, H), :], n2.at[pl.ds(cslot, H), :], core)
    zstep("d")
    xsend(1, 2, 0)
    yc[(1, 0, 0)].wait_recv()
    zstart("e")
    yb.wait_recv()
    xb = xchg(bown(1 - t), bown(1 - t), xp)
    cdml.wait_recv()
    cn2.wait_recv()
    nT[...] = n2[...].T
    dmlT[...] = dml[...].T
    cbup.wait_recv()
    for k in range(4):
        xc[(0, k, 0)].wait_recv()
        ysend(0, k, 1)
    zend("d")
    xsend(1, 3, 0)
    xsend(1, 0, 1)

    G = (gU, gD)
    rs = {}

    def addto(dst, src):
        dst[...] = (dst[...].astype(F32) + src[...].astype(F32)).astype(BF)

    def rs_x(a, j):
        rs[(a, j)] = [xchg(G[a].at[j, 1], rG.at[a, j, 0:4], xp)]

    rland = {(r, q): slot() for r in ((0, 0, 0), (0, 0, 1), (0, 1, 0), (1, 0, 0), (1, 1, 0)) for q in range(4, 9)}

    def rslot(r, q):
        a, j, xx = r
        if xx == 0:
            return rG.at[a, j, q]
        return rX.at[0] if q == 8 else rG.at[a, j, q - 4]

    def gblk(r, k):
        a, j, xx = r
        return G[a].at[j, xx, zk[k]]

    def rpass(r, k, to, q, when):
        xchg(gblk(r, k), rslot(r, q), to, when, rland[(r, q)])

    def radd(r, k, q):
        landed(rslot(r, q), rland[(r, q)], z1)
        addto(gblk(r, k), rslot(r, q))

    def rs_z0(r):
        for k, q in ((3, 4), (2, 5), (1, 6)):
            rpass(r, k, z1, q, end_z)

    def rs_z1(a, j):
        for cp in rs[(a, j)]:
            cp.wait_recv()
        for zz in range(4):
            addto(G[a].at[j, 0, zz], rG.at[a, j, zz])
        rs_z0((a, j, 0))

    def rs_z2(r):
        pl.when(mid_z)(partial(radd, r, 2, 4))
        rpass(r, 2, z3, 7, mid_z)
        pl.when(mid_z)(partial(radd, r, 3, 5))
        rpass(r, 3, z3, 8, mid_z)

    def rs_z3(r):
        pl.when(mid_z)(partial(radd, r, 1, 7))
        rpass(r, 1, z1, 8, mid_z)

    def rs_zsum(r):
        pl.when(mid_z)(partial(radd, r, 0, 6))
        radd(r, 0, 8)

    def rs_xlast():
        rs_zsum((0, 0, 1))
        rs["xlast"] = xchg(gblk((0, 0, 1), 0), rX.at[1], xp)

    def rs_sum(a, j):
        rs_zsum((a, j, 0))
        total = gblk((a, j, 0), 0)[...].astype(F32)
        if (a, j) == (0, 0):
            rs["xlast"].wait_recv()
            total = total + rX[1].astype(F32)
        return total

    def rs_y(a):
        sy[a] = rs_sum(a, 1).astype(BF)
        rs[(a, "y")] = xchg(sy.at[a], ry.at[a], yp)

    def rs_c(a):
        total = rs_sum(a, 0)
        rs[(a, "y")].wait_recv()
        sc[a] = total + ry[a].astype(F32)
        rs[(a, "c")] = xchg(sc.at[a, pl.ds(al((1 - c) * 48, 16), 48), :], rc.at[a], core)

    def rs_end(a):
        gS[a, :, pl.ds(al(c * D, 128), D)] = sc[a, pl.ds(al(c * 48, 16), 48), :]
        rs[(a, "c")].wait_recv()
        gS[a, :, pl.ds(al((1 - c) * D, 128), D)] = rc[a]
        load(gS.at[a], (gup, gdn)[a])

    bsums = []

    def ff_act(j):
        yy = tr[j]
        bu = bupA[j, pl.ds(c, 1), :]

        def block(b, carry):
            rows = pl.ds(al(b * BLK, BLK), BLK)
            hid = nn(n2[rows, :], Wu[yy]) + bu
            phi = 0.5 * (1.0 + lax.erf(hid * 0.7071067811865476))
            a = (hid * phi).astype(BF)
            act[rows, :] = a
            dh[rows, :] = (phi + hid * (jnp.exp(hid * hid * -0.5) * 0.3989422804014327)).astype(BF)
            return carry

        lax.fori_loop(0, 4, block, 0)

    def ff_out(j):
        yy = tr[j]

        def block(b, carry):
            rows = pl.ds(al(b * BLK, BLK), BLK)
            o = nt(act[rows, :], Wd[yy])
            if j == 0:
                outA[rows, :] = o
            else:
                outA[rows, :] += o
            return carry

        lax.fori_loop(0, 4, block, 0)

    def ff_bwd(j):
        yy = tr[j]

        def block(b, carry):
            rows = pl.ds(al(b * BLK, BLK), BLK)
            dhid = (nn(dml[rows, :], Wd[yy]) * dh[rows, :].astype(F32)).astype(BF)
            dh[rows, :] = dhid
            g = nt(dhid, Wu[yy])
            if j == 0:
                dn2A[rows, :] = g
            else:
                dn2A[rows, :] += g
            return carry + rowsum(dhid.astype(F32))

        bsums.append(lax.fori_loop(0, 4, block, jnp.zeros((1, D), F32)))

    def ff_grads(j, left, right, out):
        def gw_block(b, carry):
            r = nn(left[pl.ds(al(b * 192, 64), 192), :], right[...]).astype(BF)
            for xa in range(2):
                out[j, lax.rem(xa + x, 2), b] = r[xa * 96 : xa * 96 + 96]
            return carry

        lax.fori_loop(0, 4, gw_block, 0)

    def ff_gu(j):
        ff_grads(j, nT, dh, gU)

    def ff_gd(j):
        ff_grads(j, dmlT, act, gD)

    zrow = jnp.zeros((1, D), F32)
    ff_act(0)
    xb.wait_recv()
    zstart("b")
    ff_gd(0)
    zc[("e", 1)].wait_recv()
    xsend(1, 1, 1)
    for k in range(4):
        xc[(1, k, 0)].wait_recv()
    ff_out(0)
    zstep("e")
    xsend(1, 2, 1)
    ff_bwd(0)
    zstep("b")
    zend("e")
    xsend(1, 3, 1)
    rs_x(1, 0)
    ff_gu(0)
    rs_z0((0, 0, 1))
    rs_z0((0, 0, 0))
    zc[("b", 1)].wait_recv()
    zend("b")
    for k in range(4):
        yc[(0, k, 0)].wait_recv()
        yc[(0, k, 1)].wait_recv()
    ff_act(1)
    ff_gd(1)
    rs_x(1, 1)
    for k in range(4):
        xc[(1, k, 1)].wait_recv()
    ff_bwd(1)

    flush([cn2])
    n2[0:H, :] = dn2A[pl.ds(sslot, H), :].astype(BF)
    cN = xchg(n2.at[0:H, :], rN, core)
    ff_out(1)
    n2[H:T, :] = outA[pl.ds(sslot, H), :].astype(BF)
    cO = xchg(n2.at[H:T, :], rO, core)
    rs_z2((0, 0, 1))
    ff_gu(1)
    rs_x(0, 1)
    flush(catt)
    cN.wait_recv()
    flush([cN])

    sums = [zrow, zrow, zrow, zrow]
    cda = []
    for o in (t, 1 - t):
        o0 = al(o * BLK, BLK)
        rows = pl.ds(o0, BLK)
        crow = pl.ds(al(cslot + o0, BLK), BLK)
        dnb = dn2A[crow, :] + rN[rows, :].astype(F32)
        cent, r = stats(mid[rows, :])
        xhat = cent * r
        ct = dml[crow, :].astype(F32)
        dm = ct + norm_back(xhat, r, dnb, ln2g)
        db = dm.astype(BF)
        n2[rows, :] = db
        attO[rows, :] = nt(db, wpf[1 - t]).astype(BF)
        orow = pl.ds(al(own + o0, BLK), BLK)
        cda.append(xchg(attO.at[rows, :], dO.at[orow, :], yp))
        dO[orow, :] = nt(db, wpf[t]).astype(BF)
        dn2A[crow, :] = dm
        for i, term in enumerate((dnb * xhat, dnb, db.astype(F32), ct)):
            sums[i] = sums[i] + rowsum(term)
    s2g, s2b, sp, sd = sums

    cO.wait_recv()
    cmix = []

    def mixed_block(o):
        o0 = al(o * BLK, BLK)
        rows = pl.ds(o0, BLK)
        crow = pl.ds(al(cslot + o0, BLK), BLK)
        out = mid[rows, :] + (outA[crow, :] + rO[rows, :].astype(F32)) + bdown
        mixS[rows, :] = out.astype(BF)
        mid[rows, :] = dn2A[crow, :]

    def mixed_send(i):
        orow = pl.ds(own + i * 128, 128)
        rows = slice(i * 128, i * 128 + 128)
        cmix.append(xchg(mixS.at[rows, :], mixed.at[orow, :], yp))
        load(mixS.at[rows, :], mixed.at[orow, :])

    mixed_block(0)
    mixed_block(1)
    mixed_send(0)
    mixed_send(1)
    mixed_send(2)
    rs_z3((0, 0, 1))
    rs_z2((0, 0, 0))
    outA[...] = jnp.zeros((T, D), F32)
    nT[...] = n1[...].T
    flush(ccp)
    flush([yb, xb])
    for q in (zc, xc, yc):
        flush(q.values())
    rs_z1(1, 0)

    def att_back(half, edge):
        qb = half * 3 if edge else 1 + half
        wl = H if edge else WIN
        r0 = al(qb * BLK, BLK)
        ws = al(half * H if edge else half * BLK, BLK)
        cw = codec[pl.ds(ws, wl), 0:1]
        cr = coder[:, pl.ds(r0, BLK)]
        rid = r0 + lax.broadcasted_iota(jnp.int32, (wl, BLK), 1)
        cid = ws + lax.broadcasted_iota(jnp.int32, (wl, BLK), 0)
        ok = ((cr & 15) == (cw & 15)) & (((cw & 16) == 16) | (rid == cid))
        dn2A[0:wl, 0:BLK] = jnp.where(ok, 0.0, -1e30)
        rows = pl.ds(r0, BLK)
        win = pl.ds(ws, wl)

        def pair(p, carry):
            cols = pl.ds(al(p * 128, 128), 128)
            vcols = pl.ds(al(HL + p * 128, 128), 128)
            qp = qkv[0, rows, cols]
            op = dO[rows, cols]
            qs = masked_pair(qp, 0.125)
            os = masked_pair(op)
            kp = qkv[1, win, cols]
            vp = qkv[2, win, cols]
            dqs, dks, dvs = [], [], []
            for h in range(2):
                lse = lseT[pl.ds(2 * p + h, 1), rows]
                pr = jnp.exp(nt(kp, qs[h]) + dn2A[0:wl, 0:BLK] - lse)
                dp = nt(vp, os[h])
                inner = rowsum(pr * dp)
                ds = (pr * (dp - inner)).astype(BF)
                dvs.append(nn(pr.astype(BF), op))
                dks.append(nn(ds, qp))
                dqs.append(tn(ds, kp))
            low = lane_half((BLK, 128))
            lowk = lane_half((wl, 128))
            act[rows, cols] = (jnp.where(low, dqs[0], dqs[1]) * 0.125).astype(BF)
            outA[win, cols] += jnp.where(lowk, dks[0], dks[1])
            outA[win, vcols] += jnp.where(lowk, dvs[0], dvs[1])
            return carry

        lax.fori_loop(0, 3, pair, 0)

    def finish_rows(r0):
        rows = pl.ds(r0, BLK)
        act[rows, HL:D] = (outA[rows, 0:HL] * 0.125).astype(BF)
        dh[rows, 0:HL] = outA[rows, HL:D].astype(BF)

    def dn1_rows(r0):
        rows = pl.ds(r0, BLK)
        return nt(act[rows, 0:HL], wqkv[0]) + nt(act[rows, HL:D], wqkv[1]) + nt(dh[rows, 0:HL], wqkv[2])

    att_back(t, False)

    ar = {}

    def gA(s, r0, n):
        if s == 4:
            return Wd.at[0, pl.ds(r0, n), 0:HL]
        return Wu.at[s // 2, pl.ds(r0, n), (s % 2) * HL : (s % 2) * HL + HL]

    cbase = al(c * HL, 128)
    xbase = al(c * HL + x * 192, 64)
    XFIRST = (True, True, True, True, True)

    def blk_z(s, k):
        if XFIRST[s]:
            return al(xbase + zk[k] * 48, 16), 48
        return al(cbase + zk[k] * 96, 32), 96

    def spot_of(s):
        if XFIRST[s]:
            return al(xbase + z * 48, 16)
        return al(cbase + z * 96 + x * 48, 16)

    def ar_core(s):
        ar[(s, 0)] = xchg(gA(s, al((1 - c) * HL, 128), HL), rA.at[s, 0:HL, :], core)

    def ar_x(s):
        if XFIRST[s]:
            ar[(s, "x")] = xchg(gA(s, al(c * HL + (1 - x) * 192, 64), 192), rA.at[s, 384:576, :], xp)
        else:
            ar[(s, "x")] = xchg(gA(s, al(cbase + z * 96 + (1 - x) * 48, 16), 48), rA.at[s, 672:720, :], xp)

    def ar_xadd(s):
        ar[(s, "x")].wait_recv()
        if XFIRST[s]:
            addto(gA(s, xbase, 192), rA.at[s, 384:576, :])
        else:
            addto(gA(s, spot_of(s), 48), rA.at[s, 672:720, :])

    def ar_z1(s):
        o = 576 if XFIRST[s] else 384
        for i, k in ((0, 1), (1, 3)):
            r0, n = blk_z(s, k)
            ar[(s, "z1", i)] = xchg(gA(s, r0, n), rA.at[s, o + i * n : o + i * n + n, :], z1)

    def ar_z1add(s):
        o = 576 if XFIRST[s] else 384
        for i, k in ((0, 0), (1, 2)):
            r0, n = blk_z(s, k)
            ar[(s, "z1", i)].wait_recv()
            addto(gA(s, r0, n), rA.at[s, o + i * n : o + i * n + n, :])

    def ar_z2(s):
        o = 672 if XFIRST[s] else 576
        r0, n = blk_z(s, 2)
        ar[(s, "z2")] = xchg(gA(s, r0, n), rA.at[s, o : o + n, :], z2)

    def ar_z2add(s):
        o = 672 if XFIRST[s] else 576
        r0, n = blk_z(s, 0)
        ar[(s, "z2")].wait_recv()
        addto(gA(s, r0, n), rA.at[s, o : o + n, :])

    def ar_begin(s):
        ar[(s, 0)].wait_recv()
        addto(gA(s, cbase, HL), rA.at[s, 0:HL, :])
        (ar_x if XFIRST[s] else ar_z1)(s)

    def ar_step2(s):
        if XFIRST[s]:
            ar_xadd(s)
            ar_z1(s)
        else:
            ar_z1add(s)
            ar_z2(s)

    def ar_step3(s):
        if XFIRST[s]:
            ar_z1add(s)
            ar_z2(s)
        else:
            ar_z2add(s)
            ar_x(s)

    def ar_fin(s):
        (ar_z2add if XFIRST[s] else ar_xadd)(s)

    def fslot(s, r0, n):
        return fS.at[s, pl.ds(r0, n), :]

    def ag_z2(s):
        r0, n = blk_z(s, 0)
        f = fslot(s, r0, n)
        ar[(s, "g2")] = xchg(f, f, z2)
        ar[(s, "g1")] = xchg(f, f, z1)

    def ag_z1(s):
        ar[(s, "g2")].wait_recv()
        r0, n = blk_z(s, 2)
        f = fslot(s, r0, n)
        ar[(s, "g3")] = xchg(f, f, z1)

    def ag_zend(s):
        ar[(s, "g1")].wait_recv()
        ar[(s, "g3")].wait_recv()

    def ag_x(s):
        f = fslot(s, xbase, 192) if XFIRST[s] else fslot(s, spot_of(s), 48)
        ar[(s, "gx")] = xchg(f, f, xp)

    def ag_begin(s):
        r0 = spot_of(s)
        fslot(s, r0, 48)[...] = gA(s, r0, 48)[...]
        (ag_z2 if XFIRST[s] else ag_x)(s)

    def ag_step2(s):
        if XFIRST[s]:
            ag_z1(s)
        else:
            ar[(s, "gx")].wait_recv()
            ag_z2(s)

    def ag_step3(s):
        if XFIRST[s]:
            ag_zend(s)
            ag_x(s)
        else:
            ag_z1(s)

    def ag_core(s):
        if XFIRST[s]:
            ar[(s, "gx")].wait_recv()
        else:
            ag_zend(s)
        f = fslot(s, cbase, HL)
        ar[(s, "gc")] = xchg(f, fA.at[s, pl.ds(cbase, HL), :], core)
        load(f, fA.at[s, pl.ds(cbase, HL), :])

    for s, tt in ((3, t), (4, 1 - t)):
        gp = tn(attF[tt], n2[0:H, :])
        gA(s, 0, HL)[...] = gp[:, 0:HL].astype(BF)
        gA(s, HL, HL)[...] = gp[:, HL:D].astype(BF)
        ar_core(s)
    rs_z3((0, 0, 0))
    cda[0].wait_recv()
    att_back(1 - t, True)
    rs_z2((1, 0, 0))
    rs_z1(1, 1)
    cda[1].wait_recv()
    att_back(1 - t, False)

    flush([cO])
    cdn = []
    for o in (1 - t, t):
        r0 = al(oth + o * BLK, BLK)
        finish_rows(r0)
        rows = pl.ds(al(H + o * BLK, BLK), BLK)
        n2[rows, :] = dn1_rows(r0).astype(BF)
        cdn.append(xchg(n2.at[rows, :], rN.at[pl.ds(al(o * BLK, BLK), BLK), :], yp))
    for s in (3, 4):
        ar_begin(s)
    rs_z3((1, 0, 0))
    rs_z2((1, 1, 0))
    att_back(t, True)
    rs_z1(0, 1)
    for b in range(2):
        finish_rows(al(own + b * BLK, BLK))

    def gw(s, src):
        def body(m, carry):
            rows = pl.ds(al(m * BLK, BLK), BLK)
            gA(s, al(m * BLK, BLK), BLK)[...] = nn(nT[rows, :], src[...]).astype(BF)
            return carry

        lax.fori_loop(0, 3, body, 0)
        ar_core(s)

    before = [cp for cp, _ in pending]
    gw(0, act.at[:, 0:HL])
    gw(1, act.at[:, HL:D])
    ar_begin(0)
    gw(2, dh.at[:, 0:HL])
    ar_begin(1)
    ar_begin(2)
    rs_z3((1, 1, 0))
    rs_xlast()

    vecA[0] = jnp.zeros((16, D), F32)
    for i, row in ((3, sp), (4, s2g), (5, s2b), (6, sd)):
        vecA[0, i : i + 1, :] = row
    vecA[0, pl.ds(8 + 2 * tr[0] + c, 1), :] = bsums[0]
    vecA[0, pl.ds(8 + 2 * tr[1] + c, 1), :] = bsums[1]
    vecA[0, pl.ds(12 + t, 1), 0:HL] = rowsum(act[:, 0:HL].astype(F32))
    vecA[0, pl.ds(12 + t, 1), HL:D] = rowsum(dh[:, 0:HL].astype(F32))
    stok, s1g, s1b = zrow, zrow, zrow
    cgin = []
    for i, o in enumerate((t, 1 - t)):
        o0 = al(o * BLK, BLK)
        r0 = al(own + o0, BLK)
        rows = pl.ds(r0, BLK)
        orow = pl.ds(o0, BLK)
        cdn[i].wait_recv()
        dnb = dn1_rows(r0) + rN[orow, :].astype(F32)
        m, v = start_rows(r0)
        cent, r = stats(v)
        xhat = cent * r
        dst = mid[orow, :] + norm_back(xhat, r, dnb, ln1g)
        ginS[orow, :] = jnp.where(m, 0.0, dst).astype(BF)
        stok = stok + rowsum(jnp.where(m, dst, 0.0))
        s1g = s1g + rowsum(dnb * xhat)
        s1b = s1b + rowsum(dnb)
        if i == 1:
            for n, row in ((0, stok), (1, s1g), (2, s1b)):
                vecA[0, n : n + 1, :] = row
            cv = cv0 = xchg(vecA.at[0], vR.at[0], core)
        cgin.append(xchg(ginS.at[orow, :], gin.at[rows, :], yp))
        load(ginS.at[orow, :], gin.at[rows, :])
        if i == 0:
            ar_step2(0)
            rs_z2((0, 1, 0))
            ar_step2(3)
            ar_step2(4)
            ar_step2(1)
            rs_y(1)
            ar_step2(2)
            ar_step3(0)

    def sum_step(i, to):
        cv.wait_recv()
        vecA[i] = vecA[i - 1] + vR[i - 1]
        return xchg(vecA.at[i], vR.at[i], to)

    ar_step3(3)
    ar_step3(4)
    ar_step3(1)
    rs_z3((0, 1, 0))
    ar_fin(0)
    ag_begin(0)
    ar_step3(2)
    ar_fin(3)
    ar_fin(4)
    cgp = xchg(gA(4, spot_of(4), 48), rgp, yp)
    mixed_send(3)
    cv = sum_step(1, xp)
    ar_fin(1)
    ag_begin(1)
    ag_step2(0)
    ar_fin(2)
    ag_begin(2)
    ag_step2(1)
    ag_step3(0)
    cgp.wait_recv()
    addto(gA(3, spot_of(3), 48), rgp)
    ag_begin(3)
    cv = sum_step(2, z1)
    ag_step2(2)
    ag_step3(1)
    rs_y(0)
    flush(before[:-12])
    ag_core(0)
    ag_step2(3)
    ag_step3(2)
    cv = sum_step(3, z2)
    ag_core(1)
    ag_step3(3)
    rs_c(0)
    rs_c(1)
    flush([cv0])
    cv = sum_step(4, yp)
    flush(before)
    flush([ar[k] if not isinstance(ar[k], list) else ar[k][0] for k in ar if k[1] in (0, "x", "z1", "z2")])
    ag_core(2)
    ag_core(3)
    rs_end(0)
    rs_end(1)
    cv.wait_recv()
    vecA[0] = vecA[4] + vR[4]
    load(vecA.at[0], vout)
    for s in range(4):
        ar[(s, "gc")].wait_recv()
    for cp in cmix + cgin:
        cp.wait_recv()
    flush([cp for cp, _ in pending])
    for cp in loads[18:]:
        cp.wait()
    assert (len(pending), slots[0], len(loads)) == (SENT, LANDED, LOCAL)


def scratch():
    def v(shape, dt):
        return pltpu.VMEM(shape, dt)

    return [
        v((T, D), BF), v((D, T), BF), v((3, T, HL), BF), v((T, HL), BF), v((2, H, HL), BF), v((2, HL, D), BF),
        v((2, D, D), BF), v((2, D, D), BF), v((H, D), F32), v((T, D), BF), v((T, D), BF), v((D, T), BF),
        v((T, D), F32), v((T, D), F32), v((H, D), BF), v((H, D), BF), v((T, D), BF), v((T, D), BF),
        v((2, 2, 4, 96, D), BF), v((2, 2, 4, 96, D), BF),
        v((2, 2, 9, 96, D), BF), v((2, 96, D), BF), v((2, 96, D), BF), v((2, 96, D), BF),
        v((2, 96, D), F32), v((2, 48, D), F32), v((T, HL), BF), v((48, HL), BF), v((5, 720, HL), BF),
        v((8, T), F32), v((2, 8, D), F32), v((5, 16, D), F32), v((5, 16, D), F32),
        v((T, D), BF), v((3, D, HL), BF), v((T, 128), jnp.int32), v((1, T), jnp.int32), v((8, D), F32),
        v((H, D), BF), v((H, D), BF), v((4, D, HL), BF), v((2, 48, 2 * D), F32),
        [v((1, T), jnp.int32)] * 3 + [v((D,), BF)] * 7 + [v((2, HL), BF)] + [v((48, 2 * D), BF)] * 2 + [v((2 * D,), BF)],
        pltpu.SemaphoreType.DMA((SENT,)), pltpu.SemaphoreType.DMA((LANDED,)), pltpu.SemaphoreType.DMA((LOCAL,)),
    ]


def finish(mixed, gin, fa, gup, gdn, vs, o_mixed, o_gin, o_tok, o_g1, o_b1, o_qkv, o_bqv, o_proj, o_bp, o_g2, o_b2, o_up,
           o_bup, o_dn, o_bd, gb, gf, fb, ff, pf, mb, ub, vb, rows_1d, r_bup, r_bqv, sem):
    t = lax.axis_index("tensor")
    count = [0]

    def copy(src, dst):
        cp = pltpu.make_async_copy(src, dst, sem.at[count[0]])
        count[0] += 1
        cp.start()
        return cp

    vc = copy(vs, vb)
    fc = [copy(fa.at[s], fb.at[s]) for s in range(4)]
    gc = [copy(gin.at[b * BLK : b * BLK + BLK, :], gb.at[b * BLK : b * BLK + BLK, :]) for b in range(4)]
    through = [(copy(mixed, mb), mb, o_mixed), (copy(gup, ub.at[0]), ub.at[0], o_up), (copy(gdn, ub.at[1]), ub.at[1], o_dn)]
    out = []
    vc.wait()
    for i, o in enumerate((o_tok, o_g1, o_b1, o_bp, o_g2, o_b2, o_bd)):
        rows_1d[i][...] = vb[i : i + 1, :].reshape(D)
        out.append(copy(rows_1d[i], o))
    for i in range(2):
        r_bup[i * D : i * D + D] = vb[pl.ds(8 + 2 * t + i, 1), :].reshape(D)
        r_bqv[i : i + 1, :] = vb[pl.ds(12 + t, 1), i * HL : i * HL + HL]
    out += [copy(r_bup, o_bup), copy(r_bqv, o_bqv)]
    for b in range(4):
        gc[b].wait()
        rows = slice(b * BLK, b * BLK + BLK)
        gf[rows, :] = gb[rows, :].astype(F32)
        out.append(copy(gf.at[rows, :], o_gin.at[rows, :]))
    for cp, here, there in through:
        cp.wait()
        out.append(copy(here, there))
    for s in range(4):
        fc[s].wait()
        if s < 3:
            ff[s] = fb[s].astype(F32)
            out.append(copy(ff.at[s], o_qkv.at[s]))
        else:
            pf[:, 0:HL] = fb[3, 0:HL, :].astype(F32)
            pf[:, HL:D] = fb[3, HL:D, :].astype(F32)
            out.append(copy(pf, o_proj))
    for cp in out:
        cp.wait()


def on_device(
    patches, image_ids, valid, mask_pos, mask_token, ln1_gain, ln1_bias, w_qkv, b_qv, w_proj, b_proj,
    ln2_gain, ln2_bias, w_up, b_up, w_down, b_down, cotangent,
):
    hbm = pl.BlockSpec(memory_space=pl.ANY)
    sds = jax.ShapeDtypeStruct
    parts = pl.pallas_call(
        mega,
        out_shape=(
            sds((T, D), BF), sds((T, D), BF), sds((4, D, HL), BF), sds((48, 2 * D), F32), sds((48, 2 * D), F32),
            sds((16, D), F32),
        ),
        in_specs=[hbm] * 18,
        out_specs=(hbm,) * 6,
        scratch_shapes=scratch(),
        compiler_params=pltpu.CompilerParams(collective_id=0, has_side_effects=True, vmem_limit_bytes=66584576),
        name="block",
    )(
        patches, jnp.transpose(w_qkv, (1, 0, 2)), w_proj, cotangent, image_ids, valid, mask_pos, mask_token, ln1_gain,
        ln1_bias, b_proj, ln2_gain, ln2_bias, b_down, b_qv, w_up, w_down.T, b_up,
    )
    row = sds((D,), F32)
    outs = pl.pallas_call(
        finish,
        out_shape=(
            sds((T, D), BF), sds((T, D), F32), row, row, row, sds((3, D, HL), F32), sds((2, HL), F32), sds((HL, D), F32),
            row, row, row, sds((48, 2 * D), F32), sds((2 * D,), F32), sds((48, 2 * D), F32), row,
        ),
        in_specs=[hbm] * 6,
        out_specs=(hbm,) * 15,
        scratch_shapes=[
            pltpu.VMEM((T, D), BF), pltpu.VMEM((T, D), F32), pltpu.VMEM((4, D, HL), BF), pltpu.VMEM((3, D, HL), F32),
            pltpu.VMEM((HL, D), F32), pltpu.VMEM((T, D), BF), pltpu.VMEM((2, 48, 2 * D), F32),
            pltpu.VMEM((16, D), F32), [pltpu.VMEM((D,), F32)] * 7, pltpu.VMEM((2 * D,), F32), pltpu.VMEM((2, HL), F32),
            pltpu.SemaphoreType.DMA((32,)),
        ],
        compiler_params=pltpu.CompilerParams(vmem_limit_bytes=66584576),
        name="finish",
    )(*parts)
    outs = list(outs)
    outs[5] = jnp.transpose(outs[5], (1, 0, 2))
    outs[13] = outs[13].T
    return tuple(outs)


HEAD_DIM = 64


def norm_rows(values, gain, shift):
    mean = jnp.mean(values, axis=-1, keepdims=True)
    cent = values - mean
    var = jnp.mean(cent * cent, axis=-1, keepdims=True)
    return cent * lax.rsqrt(var + EPS) * gain + shift


def left_dot(first, second):
    return lax.dot_general(
        first, second, (((0,), (0,)), ((), ())), preferred_element_type=jnp.float32
    )


def right_dot(first, second):
    return lax.dot_general(
        first, second, (((1,), (1,)), ((), ())), preferred_element_type=jnp.float32
    )


def allowed_rows(ids, live, begin, count):
    rows = ids.shape[0]
    own_ids = lax.dynamic_slice_in_dim(ids, begin, count, 0)
    places = begin + jnp.arange(count)
    same_place = places[:, None] == jnp.arange(rows)[None, :]
    return (own_ids[:, None] == ids[None, :]) & ((live[None, :] == 1) | same_place)


def spread(
    patches,
    image_ids,
    valid,
    mask_pos,
    mask_token,
    ln1_gain,
    ln1_bias,
    w_qkv,
    b_qv,
    w_proj,
    b_proj,
    ln2_gain,
    ln2_bias,
    w_up,
    b_up,
    w_down,
    b_down,
    cotangent,
):
    rows = patches.shape[0]
    local_width = w_qkv.shape[2]
    local_heads = local_width // HEAD_DIM
    scale = 1.0 / HEAD_DIM**0.5
    ids = image_ids[0]
    live = valid[0]
    masked = mask_pos[0][:, None] == 1
    block = min(512, rows)
    blocks = rows // block
    start = jnp.where(masked, mask_token.astype(jnp.float32)[None, :], patches.astype(jnp.float32))
    normed, norm1_pull = jax.vjp(
        norm_rows, start, ln1_gain.astype(jnp.float32), ln1_bias.astype(jnp.float32)
    )
    normed_b = normed.astype(jnp.bfloat16)
    qv_bias = b_qv.astype(jnp.float32)
    bias = jnp.stack([qv_bias[0], jnp.zeros_like(qv_bias[0]), qv_bias[1]])
    qkv = jnp.einsum("td,dsc->tsc", normed_b, w_qkv, preferred_element_type=jnp.float32)
    qkv_b = (qkv + bias[None]).astype(jnp.bfloat16)
    query = qkv_b[:, 0].reshape(rows, local_heads, HEAD_DIM)
    keys = qkv_b[:, 1].reshape(rows, local_heads, HEAD_DIM)
    values = qkv_b[:, 2].reshape(rows, local_heads, HEAD_DIM)
    outputs = []
    totals = []
    for index in range(blocks):
        begin = index * block
        query_part = query[begin : begin + block]
        allowed = allowed_rows(ids, live, begin, block)
        scores = (
            jnp.einsum("qhc,khc->hqk", query_part, keys, preferred_element_type=jnp.float32) * scale
        )
        scores = jnp.where(allowed[None], scores, -1e30)
        top = jnp.max(scores, axis=-1, keepdims=True)
        expd = jnp.exp(scores - top)
        summed = jnp.sum(expd, axis=-1, keepdims=True)
        probs_b = (expd / summed).astype(jnp.bfloat16)
        totals.append(top + jnp.log(summed))
        outputs.append(
            jnp.einsum("hqk,khc->qhc", probs_b, values, preferred_element_type=jnp.float32)
        )
    attended_b = jnp.concatenate(outputs, axis=0).reshape(rows, local_width).astype(jnp.bfloat16)
    attn_part = jnp.dot(attended_b, w_proj, preferred_element_type=jnp.float32)
    ln2_gain_f = ln2_gain.astype(jnp.float32)
    ln2_bias_f = ln2_bias.astype(jnp.float32)
    attn_total = lax.psum(attn_part, "tensor")
    middle = start + attn_total + b_proj.astype(jnp.float32)
    normed2, norm2_pull = jax.vjp(norm_rows, middle, ln2_gain_f, ln2_bias_f)
    normed2_b = normed2.astype(jnp.bfloat16)
    up_full, down_full = (
        lax.all_gather(w_up, "dp", axis=0, tiled=True),
        lax.all_gather(w_down, "dp", axis=1, tiled=True),
    )
    hidden = jnp.dot(normed2_b, up_full, preferred_element_type=jnp.float32) + b_up.astype(
        jnp.float32
    )
    active, gelu_pull = jax.vjp(partial(jax.nn.gelu, approximate=False), hidden)
    active_b = active.astype(jnp.bfloat16)
    mlp_part = jnp.dot(active_b, down_full, preferred_element_type=jnp.float32)
    mlp_total = lax.psum(mlp_part.astype(jnp.bfloat16), "tensor").astype(jnp.float32)
    mixed = (middle + mlp_total + b_down.astype(jnp.float32)).astype(jnp.bfloat16)
    seed_grad = cotangent.astype(jnp.float32)
    up_back, down_back = (up_full, down_full)
    grad_b_down = jnp.sum(seed_grad, axis=0)
    grad_down_local = left_dot(active_b, cotangent)
    grad_active = right_dot(cotangent, down_back)
    (grad_hidden,) = gelu_pull(grad_active)
    grad_hidden_b = grad_hidden.astype(jnp.bfloat16)
    grad_b_up = jnp.sum(grad_hidden_b.astype(jnp.float32), axis=0)
    grad_up_local = left_dot(normed2_b, grad_hidden_b)
    grad_normed2_part = right_dot(grad_hidden_b, up_back)
    grad_normed2 = lax.psum(grad_normed2_part, "tensor")
    grad_mid_norm, grad_ln2_gain, grad_ln2_bias = norm2_pull(grad_normed2)
    grad_middle = seed_grad + grad_mid_norm
    grad_w_up, grad_w_down = (
        lax.psum_scatter(grad_up_local, "dp", scatter_dimension=0, tiled=True),
        lax.psum_scatter(grad_down_local, "dp", scatter_dimension=1, tiled=True),
    )
    grad_branch_b = grad_middle.astype(jnp.bfloat16)
    grad_b_proj = jnp.sum(grad_branch_b.astype(jnp.float32), axis=0)
    grad_w_proj = left_dot(attended_b, grad_branch_b)
    grad_attended = (
        right_dot(grad_branch_b, w_proj).astype(jnp.bfloat16).reshape(rows, local_heads, HEAD_DIM)
    )
    grad_query_parts = []
    grad_keys = jnp.zeros((rows, local_heads, HEAD_DIM), jnp.float32)
    grad_values = jnp.zeros((rows, local_heads, HEAD_DIM), jnp.float32)
    for index in range(blocks):
        begin = index * block
        query_part = query[begin : begin + block]
        grad_out_part = grad_attended[begin : begin + block]
        allowed = allowed_rows(ids, live, begin, block)
        scores = (
            jnp.einsum("qhc,khc->hqk", query_part, keys, preferred_element_type=jnp.float32) * scale
        )
        scores = jnp.where(allowed[None], scores, -1e30)
        probs = jnp.exp(scores - totals[index])
        probs_b = probs.astype(jnp.bfloat16)
        grad_values = grad_values + jnp.einsum(
            "hqk,qhc->khc", probs_b, grad_out_part, preferred_element_type=jnp.float32
        )
        grad_probs = jnp.einsum(
            "qhc,khc->hqk", grad_out_part, values, preferred_element_type=jnp.float32
        )
        inner = jnp.sum(probs * grad_probs, axis=-1, keepdims=True)
        grad_scores_b = (probs * (grad_probs - inner)).astype(jnp.bfloat16)
        grad_query_parts.append(
            jnp.einsum("hqk,khc->qhc", grad_scores_b, keys, preferred_element_type=jnp.float32)
            * scale
        )
        grad_keys = (
            grad_keys
            + jnp.einsum(
                "hqk,qhc->khc", grad_scores_b, query_part, preferred_element_type=jnp.float32
            )
            * scale
        )
    grad_query = jnp.concatenate(grad_query_parts, axis=0)
    grad_qkv_b = (
        jnp.stack([grad_query, grad_keys, grad_values], axis=1)
        .reshape(rows, 3, local_width)
        .astype(jnp.bfloat16)
    )
    grad_qkv_f = grad_qkv_b.astype(jnp.float32)
    grad_b_qv = jnp.stack([jnp.sum(grad_qkv_f[:, 0], axis=0), jnp.sum(grad_qkv_f[:, 2], axis=0)])
    grad_w_qkv = jnp.einsum("td,tsc->dsc", normed_b, grad_qkv_b, preferred_element_type=jnp.float32)
    grad_normed_part = jnp.einsum(
        "tsc,dsc->td", grad_qkv_b, w_qkv, preferred_element_type=jnp.float32
    )
    grad_normed = lax.psum(grad_normed_part.astype(jnp.bfloat16), "tensor").astype(jnp.float32)
    grad_start_norm, grad_ln1_gain, grad_ln1_bias = norm1_pull(grad_normed)
    grad_start = grad_middle + grad_start_norm
    grad_input = jnp.where(masked, 0.0, grad_start)
    grad_token = jnp.sum(jnp.where(masked, grad_start, 0.0), axis=0)
    summed = lax.psum(
        (
            grad_token,
            grad_ln1_gain,
            grad_ln1_bias,
            grad_w_qkv,
            grad_b_qv,
            grad_w_proj,
            grad_b_proj,
            grad_ln2_gain,
            grad_ln2_bias,
            grad_b_up,
            grad_b_down,
        ),
        "dp",
    )
    return (
        mixed,
        grad_input,
        summed[0],
        summed[1],
        summed[2],
        summed[3],
        summed[4],
        summed[5],
        summed[6],
        summed[7],
        summed[8],
        grad_w_up,
        summed[9],
        grad_w_down,
        summed[10],
    )


def solution(mesh):
    placed = (
        P("dp", None),
        P("dp", None),
        P("dp", None),
        P("dp", None),
        P(),
        P(),
        P(),
        P(None, None, "tensor"),
        P(None, "tensor"),
        P("tensor", None),
        P(),
        P(),
        P(),
        P("dp", "tensor"),
        P("tensor"),
        P("tensor", "dp"),
        P(),
        P("dp", None),
    )
    fits = mesh.shape["dp"] == 16 and mesh.shape["tensor"] == 2
    return jax.shard_map(
        on_device if fits else spread,
        mesh=mesh,
        in_specs=placed,
        out_specs=(
            P("dp", None),
            P("dp", None),
            P(),
            P(),
            P(),
            P(None, None, "tensor"),
            P(None, "tensor"),
            P("tensor", None),
            P(),
            P(),
            P(),
            P("dp", "tensor"),
            P("tensor"),
            P("tensor", "dp"),
            P(),
        ),
        check_vma=False,
    )
```
